256 devices in a mesh: shot: 16 (over x, y_lo, core), space: 16 (over y_hi, z).
Axes of the slice: x: 4, y: 4 (y_hi: 2, y_lo: 2; y = y_hi * 2 + y_lo), z: 8, core: 2. Of those that a mesh axis runs over, the one named last changes fastest.
Arguments:
- courant: float32 [256, 64, 256], P('space'), may hold values from 0.05 to 0.18
- snapshot_store: bfloat16 [256, 2, 16, 64, 256], P('shot', None, 'space'), may hold values from -6 to 6
- slab_holder: int32 [16, 16], replicated, may hold values from 0 to 255, as said below
- snap_step: int32 [16], P('shot'), may hold values from 0 to 55
- window_end: int32 [16], P('shot'), may hold values from 2 to 63, as said below
- source_cell: int32 [16], P('shot'), may hold values from 0 to 4194303
- wavelet: float32 [64], replicated, may hold values from -6 to 6
- receiver_cells: int32 [16, 256], P('shot'), may hold values from 0 to 4194303
- residual_data: float32 [16, 3, 256], P('shot'), may hold values from -6 to 6
- adjoint_prev: float32 [16, 256, 64, 256], P('shot', 'space'), may hold values from -6 to 6
- adjoint_now: float32 [16, 256, 64, 256], P('shot', 'space'), may hold values from -6 to 6
Outputs:
- image: float32 [256, 16384], P('space', 'shot')
- adjoint_out: float32 [16, 256, 64, 256], P('shot', 'space')
The draws below stay inside these ranges and needn't reach their ends.
Inputs may be any that keep to these rules, and one draw needn't show every extreme that they name: `slab_holder`: every slot holds exactly one slab; a storing index s' holds exactly 2 slabs of a shot group or none, and slot // 16 is the storing index. window_end - snap_step lies between 2 and 8, and equals 8 for some shot group.
All inputs are finite; a program needn't handle non-finite values.
Results may differ from the reference program's by a relative error of at most 0.0003.
Values may be sent and summed in bfloat16 or wider, within the bound.
A program may use at most 128 MiB of HBM per device.

```python
import math
import jax
import jax.numpy as jnp
from jax import lax

CY = 64
CZ = 256
SLABS = 16
CAP = 2
FWD = 8
ADJ = 3
NT = 64
RECV = 256
SHOTS = 16
NX = 256
N_SPACE = 16


def roster_parts(key):
    first, second, third = jax.random.split(key, 3)
    counts = jax.random.randint(first, (SHOTS,), ADJ - 1, FWD + 1)
    longest = jax.random.randint(second, (), 0, SHOTS)
    counts = counts.at[longest].set(FWD)
    starts = jax.random.randint(third, (SHOTS,), 0, NT - FWD)
    starts = starts.at[longest].set(NT - FWD - 1)
    return (starts.astype(jnp.int32), (starts + counts).astype(jnp.int32))


def draw_snap_step(key, part):
    return roster_parts(key)[0]


def draw_window_end(key, part):
    return roster_parts(key)[1]


def draw_slab_holder(key, part):
    key = jax.random.fold_in(key, 11)
    first, second = jax.random.split(key)
    groups = SLABS // CAP
    offsets = jax.random.permutation(first, SHOTS)[:groups]
    orders = jax.vmap(lambda single: jax.random.permutation(single, SLABS))(jax.random.split(second, SHOTS))
    owners = jnp.arange(SHOTS)[:, None]
    slab_ids = jnp.arange(SLABS)[None, :]
    storers = (owners + offsets[slab_ids // CAP]) % SHOTS
    positions = orders[storers, jnp.broadcast_to(slab_ids, storers.shape)]
    return (storers * SLABS + positions).astype(jnp.int32)


def plant(result, key, smallest, high):
    spot = [jax.random.randint(jax.random.fold_in(key, axis), (), 0, length) for axis, length in enumerate(result.shape)]
    main_axis = result.shape.index(max(result.shape))
    next_to = spot[:main_axis] + [(spot[main_axis] + 1) % result.shape[main_axis]] + spot[main_axis + 1:]
    return result.at[tuple(spot)].set(smallest).at[tuple(next_to)].set(high)


def block_scale(rng, dims, cuts, low, high):
    loudness = 1.0
    for position, parts in cuts:
        heights = jax.random.uniform(jax.random.fold_in(jax.random.fold_in(rng, 6), position), (parts,), jnp.float32, low / len(cuts), high / len(cuts))
        loudness = loudness * jnp.repeat(jnp.exp(heights), dims[position] // parts).reshape((-1,) + (1,) * (len(dims) - 1 - position))
    return loudness


def bell_draw(key, dims, width, limit, cuts=(), dtype=jnp.bfloat16):
    factor_of = block_scale(key, dims, cuts, -0.22, 0.18) if cuts else 1.0
    result = jax.random.normal(key, dims, jnp.float32) * width * factor_of
    return jnp.minimum(jnp.maximum(result, -limit), limit).astype(dtype)


def setup_inputs(seed: int = 0) -> dict:
    keys = jax.random.split(jax.random.key(seed), 12)
    courant = jnp.clip(jnp.exp(math.log(0.18) - 1.2809339 * jax.random.uniform(keys[0], (NX, CY, CZ), jnp.float32) ** block_scale(keys[0], (NX, CY, CZ), ((0, 16),), -0.2, 0.2)), 0.05, 0.18)
    snapshot_store = bell_draw(keys[1], (SHOTS * SLABS, 2, NX // SLABS, CY, CZ), 1.0, 6.0, ((0, 16), (2, 16)))
    slab_holder = draw_slab_holder(jax.random.fold_in(keys[11], 71), 0)
    snap_step = draw_snap_step(jax.random.fold_in(keys[11], 71), 0)
    window_end = draw_window_end(jax.random.fold_in(keys[11], 71), 0)
    source_cell = plant(jax.random.randint(keys[5], (SHOTS,), 0, NX * CY * CZ), jax.random.fold_in(keys[5], 1), 0, (NX * CY * CZ) - 1).astype(jnp.int32)
    wavelet = bell_draw(keys[6], (NT,), 1.0, 6.0, (), jnp.float32)
    receiver_cells = plant(jax.random.randint(keys[7], (SHOTS, RECV), 0, NX * CY * CZ), jax.random.fold_in(keys[7], 1), 0, (NX * CY * CZ) - 1).astype(jnp.int32)
    residual_data = bell_draw(keys[8], (SHOTS, ADJ, RECV), 1.0, 6.0, ((0, 16),), jnp.float32)
    adjoint_prev = bell_draw(keys[9], (SHOTS, NX, CY, CZ), 1.0, 6.0, ((0, 16), (1, 16)), jnp.float32)
    adjoint_now = bell_draw(keys[10], (SHOTS, NX, CY, CZ), 1.0, 6.0, ((0, 16), (1, 16)), jnp.float32)
    return dict(courant=courant, snapshot_store=snapshot_store, slab_holder=slab_holder, snap_step=snap_step, window_end=window_end, source_cell=source_cell, wavelet=wavelet, receiver_cells=receiver_cells, residual_data=residual_data, adjoint_prev=adjoint_prev, adjoint_now=adjoint_now)


COEFS = (-205.0 / 72.0, 8.0 / 5.0, -1.0 / 5.0, 8.0 / 315.0, -1.0 / 560.0)


def laplace(padded):
    size_x = padded.shape[0] - 8
    size_y = padded.shape[1] - 8
    size_z = padded.shape[2] - 8
    center = padded[4:4 + size_x, 4:4 + size_y, 4:4 + size_z]
    total = (3.0 * COEFS[0]) * center
    for offset in range(1, 5):
        weight = COEFS[offset]
        total = total + weight * (padded[4 + offset:4 + offset + size_x, 4:4 + size_y, 4:4 + size_z] + padded[4 - offset:4 - offset + size_x, 4:4 + size_y, 4:4 + size_z])
        total = total + weight * (padded[4:4 + size_x, 4 + offset:4 + offset + size_y, 4:4 + size_z] + padded[4:4 + size_x, 4 - offset:4 - offset + size_y, 4:4 + size_z])
        total = total + weight * (padded[4:4 + size_x, 4:4 + size_y, 4 + offset:4 + offset + size_z] + padded[4:4 + size_x, 4:4 + size_y, 4 - offset:4 - offset + size_z])
    return total


def reference(courant, snapshot_store, slab_holder, snap_step, window_end, source_cell, wavelet, receiver_cells, residual_data, adjoint_prev, adjoint_now):
    size_x, size_y, size_z = courant.shape
    thick = size_x // (N_SPACE * SLABS)

    def one_shot(total, shot):
        slots = jnp.take(snapshot_store, slab_holder[shot], axis=0)
        slots = slots.reshape(SLABS, 2, N_SPACE, thick, size_y, size_z).transpose(1, 2, 0, 3, 4, 5)
        levels = slots.reshape(2, size_x, size_y, size_z).astype(jnp.float32)
        count = window_end[shot] - snap_step[shot]
        start = snap_step[shot]
        source = source_cell[shot]

        def advance(turn, carry):
            previous, current, buffer = carry
            amplitude = lax.dynamic_index_in_dim(wavelet, start + turn, 0, keepdims=False)
            following = 2.0 * current - previous + courant * laplace(jnp.pad(current, 4))
            following = following.reshape(-1).at[source].add(amplitude).reshape(size_x, size_y, size_z)
            buffer = lax.dynamic_update_index_in_dim(buffer, following, (turn + 1) % ADJ, 0)
            return current, following, buffer

        buffer = jnp.zeros((ADJ, size_x, size_y, size_z), jnp.float32).at[0].set(levels[1])
        _, _, buffer = lax.fori_loop(0, count, advance, (levels[0], levels[1], buffer))
        previous = adjoint_prev[shot]
        current = adjoint_now[shot]
        for turn in range(ADJ):
            forward_field = lax.dynamic_index_in_dim(buffer, (count - turn) % ADJ, 0, keepdims=False)
            total = total + forward_field * current
            following = 2.0 * current - previous + laplace(jnp.pad(courant * current, 4))
            following = following.reshape(-1).at[receiver_cells[shot]].add(residual_data[shot, turn]).reshape(size_x, size_y, size_z)
            previous, current = current, following
        return total, current

    start_total = jnp.zeros((size_x, size_y, size_z), jnp.float32)
    total, finals = lax.scan(one_shot, start_total, jnp.arange(SHOTS))
    image = (total * (1.0 / ADJ)).reshape(size_x, size_y * size_z)
    return image, finals
```

```python
import functools

import jax
import jax.numpy as jnp
from jax import lax
from jax.experimental import pallas as pl
from jax.experimental.pallas import tpu as pltpu
from jax.sharding import PartitionSpec as P

FWD = 8
ADJ = 3
HALO = 4
CAP = 2
SCALE = 5040.0
TAPS = (8064.0, -1008.0, 128.0, -9.0)
CENTRE_Z = -43008.0
CENTRE_Y = -42.0
MESH = pl.DeviceIdType.MESH
F32 = jnp.float32
BF16 = jnp.bfloat16


def band(size, block, centre):
    row = lax.broadcasted_iota(jnp.int32, (size, size), 0)
    col = lax.broadcasted_iota(jnp.int32, (size, size), 1)
    gap = jnp.abs(row - col)
    result = jnp.where(gap == 0, centre, 0.0)
    for offset, tap in enumerate(TAPS, 1):
        result = jnp.where(gap == offset, tap, result)
    if block < size:
        result = jnp.where(row // block == col // block, result, 0.0)
    return result.astype(BF16)


def split(value):
    high = value.astype(BF16)
    return high, (value - high.astype(F32)).astype(BF16)


def kernel(
    shots,
    spaces,
    cap,
    holder,
    snap_step,
    window_end,
    source_cell,
    wavelet,
    cells,
    residual,
    courant_in,
    store_in,
    prev_in,
    now_in,
    image_out,
    adjoint_out,
    courant,
    store,
    adj,
    field,
    wave,
    packed,
    landed,
    band_z,
    band_y,
    spot,
    col_hot,
    image,
    from_core,
    to_chip,
    from_chip,
    last,
    last_in,
    local_sem,
    fetch_send,
    fetch_recv,
    adj_send,
    adj_recv,
    wave_send,
    wave_recv,
    core_sem,
    chip_send,
    chip_recv,
    last_sem,
    out_sem,
):
    me = lax.axis_index("shot")
    place = lax.axis_index("space")
    planes, size_y, size_z = courant.shape
    slabs = store.shape[0]
    has_low = place > 0
    has_high = place < spaces - 1
    core = lax.rem(me, 2)
    chip = lax.div(me, 2)
    chips = shots // 2
    partner = chip * 2 + 1 - core
    half = planes // 2
    chunk = HALO
    chunks = planes // chunk
    inside = HALO

    def peer(shot):
        return (shot, place)

    loads = [
        pltpu.make_async_copy(now_in, adj.at[1], local_sem.at[0]),
        pltpu.make_async_copy(courant_in, courant, local_sem.at[1]),
        pltpu.make_async_copy(store_in, store, local_sem.at[2]),
        pltpu.make_async_copy(prev_in, adj.at[0], local_sem.at[3]),
    ]
    for load in loads:
        load.start()

    barrier = pltpu.get_barrier_semaphore()

    def greet(turn, carry):
        other = lax.rem(me + turn, shots)
        pl.semaphore_signal(barrier, inc=1, device_id=peer(other), device_id_type=MESH)
        return carry

    lax.fori_loop(1, shots, greet, 0)

    @pl.when(has_low)
    def _():
        pl.semaphore_signal(barrier, inc=1, device_id=(me, place - 1), device_id_type=MESH)

    @pl.when(has_high)
    def _():
        pl.semaphore_signal(barrier, inc=1, device_id=(me, place + 1), device_id_type=MESH)

    band_z[...] = band(size_z, size_z, CENTRE_Z)
    band_y[...] = band(chunk * size_y, size_y, CENTRE_Y)

    @pl.when(jnp.logical_not(has_low))
    def _():
        for slot in range(2):
            field[slot, :HALO] = jnp.zeros((HALO, size_y, size_z), F32)
            wave[slot, :HALO] = jnp.zeros((HALO, size_y, size_z), F32)

    @pl.when(jnp.logical_not(has_high))
    def _():
        for slot in range(2):
            field[slot, planes + HALO :] = jnp.zeros((HALO, size_y, size_z), F32)
            wave[slot, planes + HALO :] = jnp.zeros((HALO, size_y, size_z), F32)

    plane_cells = size_y * size_z
    source = source_cell[0]
    source_plane = lax.div(source, plane_cells) - place * planes
    in_plane = lax.rem(source, plane_cells)
    flat = lax.broadcasted_iota(jnp.int32, (size_y, size_z), 0) * size_z + lax.broadcasted_iota(
        jnp.int32, (size_y, size_z), 1
    )
    spot[...] = jnp.where(flat == in_plane, 1.0, 0.0)

    recv_cells = cells[...]
    recv_row = recv_cells // size_z - place * (planes * size_y)
    recv_col = recv_cells % size_z
    count = recv_cells.shape[1]
    col_hot[...] = jnp.where(
        lax.broadcasted_iota(jnp.int32, (size_z, count), 0) == recv_col, 1.0, 0.0
    ).astype(BF16)

    def halo_copies(ref, slot, send, recv):
        low = pltpu.make_async_remote_copy(
            src_ref=ref.at[slot, pl.ds(inside, HALO)],
            dst_ref=ref.at[slot, pl.ds(inside + planes, HALO)],
            send_sem=send.at[slot, 0],
            recv_sem=recv.at[slot, 0],
            device_id=(me, place - 1),
            device_id_type=MESH,
        )
        high = pltpu.make_async_remote_copy(
            src_ref=ref.at[slot, pl.ds(planes, HALO)],
            dst_ref=ref.at[slot, pl.ds(0, HALO)],
            send_sem=send.at[slot, 1],
            recv_sem=recv.at[slot, 1],
            device_id=(me, place + 1),
            device_id_type=MESH,
        )
        return low, high

    def halo_start(ref, slot, send, recv):
        low, high = halo_copies(ref, slot, send, recv)

        @pl.when(has_low)
        def _():
            low.start()

        @pl.when(has_high)
        def _():
            high.start()

    def halo_wait(ref, slot, send, recv):
        low, high = halo_copies(ref, slot, send, recv)

        @pl.when(has_low)
        def _():
            low.wait_send()
            high.wait_recv()

        @pl.when(has_high)
        def _():
            high.wait_send()
            low.wait_recv()

    def stencil(ref, slot, index):
        first = inside + chunk * index
        middle = ref[slot, pl.ds(first, chunk)]
        high, low = split(middle.reshape(chunk * size_y, size_z))
        right = band_z[...]
        left = band_y[...]
        total = jnp.dot(high, right, preferred_element_type=F32)
        total += jnp.dot(low, right, preferred_element_type=F32)
        total += jnp.dot(left, high, preferred_element_type=F32)
        total += jnp.dot(left, low, preferred_element_type=F32)
        total = total.reshape(chunk, size_y, size_z)
        for offset, tap in enumerate(TAPS, 1):
            total += tap * (
                ref[slot, pl.ds(first + offset, chunk)] + ref[slot, pl.ds(first - offset, chunk)]
            )
        return total

    loads[0].wait()
    loads[1].wait()
    for index in (0, chunks - 1) + tuple(range(1, chunks - 1)):
        part = pl.ds(chunk * index, chunk)
        scaled = courant[part] * (1.0 / SCALE)
        courant[part] = scaled
        field[0, pl.ds(inside + chunk * index, chunk)] = scaled * adj[1, part]

    low_count = jnp.where(has_low, 1, 0)
    high_count = jnp.where(has_high, 1, 0)
    pl.semaphore_wait(barrier, shots - 1 + low_count + high_count)
    halo_start(field, 0, adj_send, adj_recv)

    def fetch_copy(level, other):
        return pltpu.make_async_remote_copy(
            src_ref=packed.at[level, pl.ds(other * cap, cap)],
            dst_ref=landed.at[level, pl.ds(me * cap, cap)],
            send_sem=fetch_send.at[level, other],
            recv_sem=fetch_recv.at[level, me],
            device_id=peer(other),
            device_id_type=MESH,
        )

    def fetch_arrival(level, other):
        return pltpu.make_async_remote_copy(
            src_ref=packed.at[level, pl.ds(other * cap, cap)],
            dst_ref=landed.at[level, pl.ds(other * cap, cap)],
            send_sem=fetch_send.at[level, other],
            recv_sem=fetch_recv.at[level, other],
            device_id=peer(other),
            device_id_type=MESH,
        )

    loads[2].wait()

    def held_for(other):
        found = jnp.int32(0)
        spots = [jnp.int32(0)] * cap
        for slab in range(slabs):
            slot = holder[other, slab]
            mine = lax.div(slot, slabs) == me
            where = lax.rem(slot, slabs)
            for rank in range(cap):
                spots[rank] = jnp.where(jnp.logical_and(mine, found == rank), where, spots[rank])
            found = found + jnp.where(mine, 1, 0)
        return spots

    def pack(turn, carry):
        other = lax.rem(me + turn, shots)
        spots = held_for(other)
        for rank in range(cap):
            for level in (1, 0):
                packed[level, other * cap + rank] = store[spots[rank], level]
        fetch_copy(1, other).start()
        return carry

    lax.fori_loop(1, shots, pack, 0)

    def send_older(turn, carry):
        fetch_copy(0, lax.rem(me + turn, shots)).start()
        return carry

    lax.fori_loop(1, shots, send_older, 0)
    own = held_for(me)
    for rank in range(cap):
        for level in (1, 0):
            landed[level, me * cap + rank] = store[own[rank], level]

    loads[3].wait()

    def adjoint_step(turn, carry):
        slot = lax.rem(turn, 2)
        halo_wait(field, slot, adj_send, adj_recv)
        data = residual[pl.ds(turn, 1)]
        data_high, data_low = split(data)
        data_high = data_high.astype(F32)
        data_low = data_low.astype(F32)
        hot = col_hot[...]

        def advance(index):
            part = pl.ds(chunk * index, chunk)
            row = lax.broadcasted_iota(jnp.int32, (chunk * size_y, count), 0) + (
                chunk * size_y * index
            )
            hit = row == recv_row
            total = lax.dot_general(
                jnp.where(hit, data_high, 0.0).astype(BF16),
                hot,
                (((1,), (1,)), ((), ())),
                preferred_element_type=F32,
            )
            total += lax.dot_general(
                jnp.where(hit, data_low, 0.0).astype(BF16),
                hot,
                (((1,), (1,)), ((), ())),
                preferred_element_type=F32,
            )
            total = total.reshape(chunk, size_y, size_z) + stencil(field, slot, index)
            current = adj[turn + 1, part]
            following = (current + current) - adj[turn, part] + total
            adj[turn + 2, part] = following
            field[1 - slot, pl.ds(inside + chunk * index, chunk)] = courant[part] * following

        advance(0)
        advance(chunks - 1)

        @pl.when(turn < ADJ - 1)
        def _():
            halo_start(field, 1 - slot, adj_send, adj_recv)

        for index in range(1, chunks - 1):
            advance(index)
        return carry

    lax.fori_loop(0, ADJ, adjoint_step, 0)
    result = pltpu.make_async_copy(adj.at[ADJ + 1], adjoint_out, out_sem.at[0])
    result.start()

    steps = window_end[0] - snap_step[0]
    idle = FWD - steps
    now_level = 1 - lax.rem(idle, 2)

    def arrive(turn, carry):
        other = lax.rem(me + turn, shots)
        for level in (1, 0):
            fetch_arrival(level, other).wait_recv()
        return carry

    lax.fori_loop(1, shots, arrive, 0)

    def unpack(slab, carry):
        storer = lax.div(holder[me, slab], slabs)
        rank = jnp.int32(0)
        for before in range(slabs):
            same = jnp.logical_and(lax.div(holder[me, before], slabs) == storer, before < slab)
            rank = rank + jnp.where(same, 1, 0)
        where = storer * cap + rank
        wave[0, inside + slab] = landed[now_level, where].astype(F32)
        wave[1, inside + slab] = landed[1 - now_level, where].astype(F32)
        return carry

    lax.fori_loop(0, slabs, unpack, 0)
    halo_start(wave, 0, wave_send, wave_recv)

    def forward_step(turn, carry):
        slot = lax.rem(turn, 2)
        moving = jnp.where(turn >= idle, 1.0, 0.0)
        amplitude = wavelet[snap_step[0] + jnp.maximum(turn - idle, 0)]
        halo_wait(wave, slot, wave_send, wave_recv)

        def advance(index):
            part = pl.ds(chunk * index, chunk)
            padded = pl.ds(inside + chunk * index, chunk)
            total = courant[part] * stencil(wave, slot, index)
            gap = wave[slot, padded] - wave[1 - slot, padded]
            total = total + (gap + gap)
            pattern = spot[...]
            for plane in range(chunk):
                push = jnp.where(source_plane == chunk * index + plane, amplitude, 0.0)
                wave[1 - slot, inside + chunk * index + plane] = wave[
                    1 - slot, inside + chunk * index + plane
                ] + moving * (total[plane] + push * pattern)

        advance(0)
        advance(chunks - 1)

        @pl.when(turn < FWD - 1)
        def _():
            halo_start(wave, 1 - slot, wave_send, wave_recv)

        for index in range(1, chunks - 1):
            advance(index)

        for late in range(2):

            @pl.when(turn == FWD - 3 + late)
            def _():
                for index in range(chunks):
                    part = pl.ds(chunk * index, chunk)
                    term = (
                        wave[1 - slot, pl.ds(inside + chunk * index, chunk)]
                        * adj[ADJ - late, part]
                    )
                    image[part] = term if late == 0 else image[part] + term

        return carry

    lax.fori_loop(0, FWD, forward_step, 0)
    for index in range(chunks):
        part = pl.ds(chunk * index, chunk)
        image[part] = image[part] + wave[FWD % 2, pl.ds(inside + chunk * index, chunk)] * adj[1, part]

    theirs = (1 - core) * half
    mine = core * half
    swap = pltpu.make_async_remote_copy(
        src_ref=image.at[pl.ds(theirs, half)],
        dst_ref=from_core,
        send_sem=core_sem.at[0],
        recv_sem=core_sem.at[1],
        device_id=peer(partner),
        device_id_type=MESH,
    )
    swap.start()
    swap.wait()
    rows = size_y // chips
    for target in range(chips):
        cut = slice(target * rows, (target + 1) * rows)
        to_chip[target] = image[pl.ds(mine, half), cut] + from_core[:, cut]

    def chip_copy(target, landing):
        return pltpu.make_async_remote_copy(
            src_ref=to_chip.at[target],
            dst_ref=from_chip.at[landing],
            send_sem=chip_send.at[target],
            recv_sem=chip_recv.at[landing],
            device_id=peer(target * 2 + core),
            device_id_type=MESH,
        )

    def chip_start(turn, carry):
        chip_copy(lax.rem(chip + turn, chips), chip).start()
        return carry

    lax.fori_loop(1, chips, chip_start, 0)
    last[...] = to_chip[chip]

    def chip_add(turn, carry):
        other = lax.rem(chip + turn, chips)
        chip_copy(other, other).wait_recv()
        last[...] = last[...] + from_chip[other]
        return carry

    lax.fori_loop(1, chips, chip_add, 0)
    trade = pltpu.make_async_remote_copy(
        src_ref=last,
        dst_ref=last_in,
        send_sem=last_sem.at[0],
        recv_sem=last_sem.at[1],
        device_id=peer(partner),
        device_id_type=MESH,
    )
    trade.start()
    trade.wait()
    row_half = rows // 2
    first_core = core == 0
    for block, offset in ((last, mine), (last_in, theirs)):
        value = block[...]
        chosen = jnp.where(first_core, 1.0, 0.0)
        image_out[pl.ds(offset, half)] = (
            chosen * value[:, :row_half] + (1.0 - chosen) * value[:, row_half:]
        )

    def drain(turn, carry):
        other = lax.rem(me + turn, shots)
        for level in (1, 0):
            fetch_copy(level, other).wait_send()
        return carry

    lax.fori_loop(1, shots, drain, 0)

    def chip_drain(turn, carry):
        target = lax.rem(chip + turn, chips)
        chip_copy(target, chip).wait_send()
        return carry

    lax.fori_loop(1, chips, chip_drain, 0)
    result.wait()


def local(
    shots,
    spaces,
    courant,
    snapshot_store,
    slab_holder,
    snap_step,
    window_end,
    source_cell,
    wavelet,
    receiver_cells,
    residual_data,
    adjoint_prev,
    adjoint_now,
):
    planes, size_y, size_z = courant.shape
    slabs = snapshot_store.shape[0]
    cap = CAP
    chips = shots // 2
    rows = size_y // chips
    smem = pl.BlockSpec(memory_space=pltpu.SMEM)
    vmem = pl.BlockSpec(memory_space=pltpu.VMEM)
    anywhere = pl.BlockSpec(memory_space=pl.ANY)
    half = planes // 2
    padded = (2, planes + 2 * HALO, size_y, size_z)
    dma = pltpu.SemaphoreType.DMA
    image, adjoint = pl.pallas_call(
        functools.partial(kernel, shots, spaces, cap),
        out_shape=(
            jax.ShapeDtypeStruct((planes, rows // 2, size_z), F32),
            jax.ShapeDtypeStruct((planes, size_y, size_z), F32),
        ),
        in_specs=[smem] * 5 + [vmem] * 2 + [anywhere] * 4,
        out_specs=(vmem, anywhere),
        scratch_shapes=[
            pltpu.VMEM((planes, size_y, size_z), F32),
            pltpu.VMEM((slabs, 2, size_y, size_z), BF16),
            pltpu.VMEM((ADJ + 2, planes, size_y, size_z), F32),
            pltpu.VMEM(padded, F32),
            pltpu.VMEM(padded, F32),
            pltpu.VMEM((2, shots * cap, size_y, size_z), BF16),
            pltpu.VMEM((2, shots * cap, size_y, size_z), BF16),
            pltpu.VMEM((size_z, size_z), BF16),
            pltpu.VMEM((HALO * size_y, HALO * size_y), BF16),
            pltpu.VMEM((size_y, size_z), F32),
            pltpu.VMEM((size_z, receiver_cells.shape[1]), BF16),
            pltpu.VMEM((planes, size_y, size_z), F32),
            pltpu.VMEM((half, size_y, size_z), F32),
            pltpu.VMEM((chips, half, rows, size_z), F32),
            pltpu.VMEM((chips, half, rows, size_z), F32),
            pltpu.VMEM((half, rows, size_z), F32),
            pltpu.VMEM((half, rows, size_z), F32),
            dma((4,)),
            dma((2, shots)),
            dma((2, shots)),
            dma((2, 2)),
            dma((2, 2)),
            dma((2, 2)),
            dma((2, 2)),
            dma((2,)),
            dma((chips,)),
            dma((chips,)),
            dma((2,)),
            dma((1,)),
        ],
        compiler_params=pltpu.CompilerParams(
            collective_id=0, has_side_effects=True, vmem_limit_bytes=48 * 2**20
        ),
    )(
        slab_holder,
        snap_step,
        window_end,
        source_cell,
        wavelet,
        receiver_cells,
        residual_data[0],
        courant,
        snapshot_store.reshape(slabs, 2, size_y, size_z),
        adjoint_prev[0],
        adjoint_now[0],
    )
    return (image * (1.0 / ADJ)).reshape(planes, rows // 2 * size_z), adjoint[None]


def solution(mesh):
    in_specs = (
        P("space", None, None),
        P("shot", None, "space", None, None),
        P(),
        P("shot"),
        P("shot"),
        P("shot"),
        P(),
        P("shot", None),
        P("shot", None, None),
        P("shot", "space", None, None),
        P("shot", "space", None, None),
    )
    out_specs = (P("space", "shot"), P("shot", "space", None, None))
    return jax.shard_map(
        functools.partial(local, mesh.shape["shot"], mesh.shape["space"]),
        mesh=mesh,
        in_specs=in_specs,
        out_specs=out_specs,
        check_vma=False,
    )
```

```python
import functools

import jax
import jax.numpy as jnp
from jax import lax
from jax.experimental import pallas as pl
from jax.experimental.pallas import tpu as pltpu
from jax.sharding import PartitionSpec as P

FWD = 8
ADJ = 3
HALO = 4
CAP = 2
SCALE = 5040.0
TAPS = (8064.0, -1008.0, 128.0, -9.0)
CENTRE_Z = -43008.0
CENTRE_Y = -42.0
CODE_BITS = 13.0
SCALE_ROWS = 16
MESH = pl.DeviceIdType.MESH
F32 = jnp.float32
BF16 = jnp.bfloat16


def band(size, block, centre):
    row = lax.broadcasted_iota(jnp.int32, (size, size), 0)
    col = lax.broadcasted_iota(jnp.int32, (size, size), 1)
    gap = jnp.abs(row - col)
    result = jnp.where(gap == 0, centre, 0.0)
    for offset, tap in enumerate(TAPS, 1):
        result = jnp.where(gap == offset, tap, result)
    if block < size:
        result = jnp.where(row // block == col // block, result, 0.0)
    return result.astype(BF16)


def split(value):
    high = value.astype(BF16)
    return high, (value - high.astype(F32)).astype(BF16)


def encode(value):
    rows = value.shape[0] * value.shape[1]
    flat = value.reshape(rows, value.shape[2])
    top = jnp.max(jnp.abs(flat), axis=0, keepdims=True)
    power = jnp.floor(jnp.log2(jnp.maximum(top, 1e-30)))
    code = jnp.round(flat * jnp.exp2(CODE_BITS - power)).astype(jnp.int32).astype(jnp.int16)
    scale = jnp.broadcast_to(power.astype(jnp.int32), (SCALE_ROWS, value.shape[2])).astype(jnp.int16)
    return code, scale


def decode(code, scale, shape):
    power = scale.astype(jnp.int32).astype(F32)[:1]
    return (code.astype(jnp.int32).astype(F32) * jnp.exp2(power - CODE_BITS)).reshape(shape)


def kernel(
    shots,
    spaces,
    cap,
    holder,
    snap_step,
    window_end,
    source_cell,
    wavelet,
    cells,
    residual,
    courant_in,
    store_in,
    prev_in,
    now_in,
    image_out,
    adjoint_out,
    courant,
    store,
    adj,
    field,
    wave,
    adj_code,
    adj_land,
    wave_code,
    wave_land,
    packed,
    landed,
    band_z,
    band_y,
    spot,
    col_hot,
    image,
    from_core,
    to_chip,
    from_chip,
    last,
    last_in,
    local_sem,
    fetch_send,
    fetch_recv,
    adj_send,
    adj_recv,
    wave_send,
    wave_recv,
    core_sem,
    chip_send,
    chip_recv,
    last_sem,
    out_sem,
):
    me = lax.axis_index("shot")
    place = lax.axis_index("space")
    planes, size_y, size_z = courant.shape
    slabs = store.shape[0]
    has_low = place > 0
    has_high = place < spaces - 1
    core = lax.rem(me, 2)
    chip = lax.div(me, 2)
    chips = shots // 2
    partner = chip * 2 + 1 - core
    half = planes // 2
    chunk = HALO
    chunks = planes // chunk
    inside = HALO

    def peer(shot):
        return (shot, place)

    loads = [
        pltpu.make_async_copy(now_in, adj.at[1], local_sem.at[0]),
        pltpu.make_async_copy(courant_in, courant, local_sem.at[1]),
        pltpu.make_async_copy(store_in, store, local_sem.at[2]),
        pltpu.make_async_copy(prev_in, adj.at[0], local_sem.at[3]),
    ]
    for load in loads:
        load.start()

    barrier = pltpu.get_barrier_semaphore()

    def greet(turn, carry):
        other = lax.rem(me + turn, shots)
        pl.semaphore_signal(barrier, inc=1, device_id=peer(other), device_id_type=MESH)
        return carry

    lax.fori_loop(1, shots, greet, 0)

    @pl.when(has_low)
    def _():
        pl.semaphore_signal(barrier, inc=1, device_id=(me, place - 1), device_id_type=MESH)

    @pl.when(has_high)
    def _():
        pl.semaphore_signal(barrier, inc=1, device_id=(me, place + 1), device_id_type=MESH)

    band_z[...] = band(size_z, size_z, CENTRE_Z)
    band_y[...] = band(chunk * size_y, size_y, CENTRE_Y)

    @pl.when(jnp.logical_not(has_low))
    def _():
        for slot in range(2):
            field[slot, :HALO] = jnp.zeros((HALO, size_y, size_z), F32)
            wave[slot, :HALO] = jnp.zeros((HALO, size_y, size_z), F32)

    @pl.when(jnp.logical_not(has_high))
    def _():
        for slot in range(2):
            field[slot, planes + HALO :] = jnp.zeros((HALO, size_y, size_z), F32)
            wave[slot, planes + HALO :] = jnp.zeros((HALO, size_y, size_z), F32)

    plane_cells = size_y * size_z
    source = source_cell[0]
    source_plane = lax.div(source, plane_cells) - place * planes
    in_plane = lax.rem(source, plane_cells)
    flat = lax.broadcasted_iota(jnp.int32, (size_y, size_z), 0) * size_z + lax.broadcasted_iota(
        jnp.int32, (size_y, size_z), 1
    )
    spot[...] = jnp.where(flat == in_plane, 1.0, 0.0)

    recv_cells = cells[...]
    recv_row = recv_cells // size_z - place * (planes * size_y)
    recv_col = recv_cells % size_z
    count = recv_cells.shape[1]
    col_hot[...] = jnp.where(
        lax.broadcasted_iota(jnp.int32, (size_z, count), 0) == recv_col, 1.0, 0.0
    ).astype(BF16)

    halo_rows = HALO * size_y
    edge_shape = (HALO, size_y, size_z)

    def halo_copy(code, land, slot, send, recv, side):
        return pltpu.make_async_remote_copy(
            src_ref=code.at[slot, side],
            dst_ref=land.at[slot, side],
            send_sem=send.at[slot, side],
            recv_sem=recv.at[slot, side],
            device_id=(me, place + 2 * side - 1),
            device_id_type=MESH,
        )

    has_side = (has_low, has_high)

    def halo_start(value, code, land, slot, send, recv, side):
        @pl.when(has_side[side])
        def _():
            numbers, scale = encode(value)
            code[slot, side, :halo_rows] = numbers
            code[slot, side, halo_rows:] = scale
            halo_copy(code, land, slot, send, recv, side).start()

    def halo_wait(ref, code, land, slot, send, recv, side):
        @pl.when(has_side[side])
        def _():
            halo_copy(code, land, slot, send, recv, side).wait_send()
            halo_copy(code, land, slot, send, recv, 1 - side).wait_recv()
            ref[slot, pl.ds((inside + planes) * side, HALO)] = decode(
                land[slot, 1 - side, :halo_rows], land[slot, 1 - side, halo_rows:], edge_shape
            )

    def stencil(ref, slot, index):
        first = inside + chunk * index
        middle = ref[slot, pl.ds(first, chunk)]
        high, low = split(middle.reshape(chunk * size_y, size_z))
        right = band_z[...]
        left = band_y[...]
        total = jnp.dot(high, right, preferred_element_type=F32)
        total += jnp.dot(low, right, preferred_element_type=F32)
        total += jnp.dot(left, high, preferred_element_type=F32)
        total += jnp.dot(left, low, preferred_element_type=F32)
        total = total.reshape(chunk, size_y, size_z)
        for offset, tap in enumerate(TAPS, 1):
            total += tap * (
                ref[slot, pl.ds(first + offset, chunk)] + ref[slot, pl.ds(first - offset, chunk)]
            )
        return total

    loads[0].wait()
    loads[1].wait()
    adj_halo = (adj_code, adj_land)
    adj_sems = (adj_send, adj_recv)
    wave_halo = (wave_code, wave_land)
    wave_sems = (wave_send, wave_recv)

    def first_field(index):
        part = pl.ds(chunk * index, chunk)
        scaled = courant[part] * (1.0 / SCALE)
        courant[part] = scaled
        value = scaled * adj[1, part]
        field[0, pl.ds(inside + chunk * index, chunk)] = value
        return value

    low_count = jnp.where(has_low, 1, 0)
    high_count = jnp.where(has_high, 1, 0)
    pl.semaphore_wait(barrier, shots - 1 + low_count + high_count)
    halo_start(first_field(0), *adj_halo, 0, *adj_sems, 0)
    halo_start(first_field(chunks - 1), *adj_halo, 0, *adj_sems, 1)

    def fetch_copy(level, other):
        return pltpu.make_async_remote_copy(
            src_ref=packed.at[level, pl.ds(other * cap, cap)],
            dst_ref=landed.at[level, pl.ds(me * cap, cap)],
            send_sem=fetch_send.at[level, other],
            recv_sem=fetch_recv.at[level, me],
            device_id=peer(other),
            device_id_type=MESH,
        )

    def fetch_arrival(level, other):
        return pltpu.make_async_remote_copy(
            src_ref=packed.at[level, pl.ds(other * cap, cap)],
            dst_ref=landed.at[level, pl.ds(other * cap, cap)],
            send_sem=fetch_send.at[level, other],
            recv_sem=fetch_recv.at[level, other],
            device_id=peer(other),
            device_id_type=MESH,
        )

    loads[2].wait()

    def held_for(other):
        found = jnp.int32(0)
        spots = [jnp.int32(0)] * cap
        for slab in range(slabs):
            slot = holder[other, slab]
            mine = lax.div(slot, slabs) == me
            where = lax.rem(slot, slabs)
            for rank in range(cap):
                spots[rank] = jnp.where(jnp.logical_and(mine, found == rank), where, spots[rank])
            found = found + jnp.where(mine, 1, 0)
        return spots

    def pack(turn, carry):
        other = lax.rem(me + turn, shots)
        spots = held_for(other)
        for rank in range(cap):
            for level in (1, 0):
                packed[level, other * cap + rank] = store[spots[rank], level]
        fetch_copy(1, other).start()
        return carry

    lax.fori_loop(1, shots, pack, 0)

    def send_older(turn, carry):
        fetch_copy(0, lax.rem(me + turn, shots)).start()
        return carry

    lax.fori_loop(1, shots, send_older, 0)
    own = held_for(me)
    for rank in range(cap):
        for level in (1, 0):
            landed[level, me * cap + rank] = store[own[rank], level]

    for index in range(1, chunks - 1):
        first_field(index)
    loads[3].wait()

    def adjoint_step(turn, carry):
        slot = lax.rem(turn, 2)
        data = residual[pl.ds(turn, 1)]
        data_high, data_low = split(data)
        data_high = data_high.astype(F32)
        data_low = data_low.astype(F32)
        hot = col_hot[...]

        def advance(index):
            part = pl.ds(chunk * index, chunk)
            row = lax.broadcasted_iota(jnp.int32, (chunk * size_y, count), 0) + (
                chunk * size_y * index
            )
            hit = row == recv_row
            total = lax.dot_general(
                jnp.where(hit, data_high, 0.0).astype(BF16),
                hot,
                (((1,), (1,)), ((), ())),
                preferred_element_type=F32,
            )
            total += lax.dot_general(
                jnp.where(hit, data_low, 0.0).astype(BF16),
                hot,
                (((1,), (1,)), ((), ())),
                preferred_element_type=F32,
            )
            total = total.reshape(chunk, size_y, size_z) + stencil(field, slot, index)
            current = adj[turn + 1, part]
            following = (current + current) - adj[turn, part] + total
            adj[turn + 2, part] = following
            value = courant[part] * following
            field[1 - slot, pl.ds(inside + chunk * index, chunk)] = value
            return value

        for side, index in ((0, 0), (1, chunks - 1)):
            halo_wait(field, *adj_halo, slot, *adj_sems, side)
            advance(index)

            @pl.when(turn < ADJ - 1)
            def _():
                value = field[1 - slot, pl.ds(inside + chunk * index, chunk)]
                halo_start(value, *adj_halo, 1 - slot, *adj_sems, side)

        for index in range(1, chunks - 1):
            advance(index)
        return carry

    lax.fori_loop(0, ADJ, adjoint_step, 0)
    result = pltpu.make_async_copy(adj.at[ADJ + 1], adjoint_out, out_sem.at[0])
    result.start()

    steps = window_end[0] - snap_step[0]
    idle = FWD - steps
    now_level = 1 - lax.rem(idle, 2)

    def arrive(turn, carry):
        other = lax.rem(me + turn, shots)
        for level in (1, 0):
            fetch_arrival(level, other).wait_recv()
        return carry

    lax.fori_loop(1, shots, arrive, 0)

    def unpack(slab, carry):
        storer = lax.div(holder[me, slab], slabs)
        rank = jnp.int32(0)
        for before in range(slabs):
            same = jnp.logical_and(lax.div(holder[me, before], slabs) == storer, before < slab)
            rank = rank + jnp.where(same, 1, 0)
        where = storer * cap + rank
        wave[0, inside + slab] = landed[now_level, where].astype(F32)
        wave[1, inside + slab] = landed[1 - now_level, where].astype(F32)
        return carry

    lax.fori_loop(0, slabs, unpack, 0)
    halo_start(wave[0, pl.ds(inside, HALO)], *wave_halo, 0, *wave_sems, 0)
    halo_start(wave[0, pl.ds(planes, HALO)], *wave_halo, 0, *wave_sems, 1)

    def forward_step(turn, carry):
        slot = lax.rem(turn, 2)
        moving = jnp.where(turn >= idle, 1.0, 0.0)
        amplitude = wavelet[snap_step[0] + jnp.maximum(turn - idle, 0)]

        def advance(index):
            part = pl.ds(chunk * index, chunk)
            padded = pl.ds(inside + chunk * index, chunk)
            total = courant[part] * stencil(wave, slot, index)
            gap = wave[slot, padded] - wave[1 - slot, padded]
            total = total + (gap + gap)
            pattern = spot[...]
            for plane in range(chunk):
                push = jnp.where(source_plane == chunk * index + plane, amplitude, 0.0)
                wave[1 - slot, inside + chunk * index + plane] = wave[
                    1 - slot, inside + chunk * index + plane
                ] + moving * (total[plane] + push * pattern)

        for side, index in ((0, 0), (1, chunks - 1)):
            halo_wait(wave, *wave_halo, slot, *wave_sems, side)
            advance(index)

            @pl.when(turn < FWD - 1)
            def _():
                value = wave[1 - slot, pl.ds(inside + chunk * index, chunk)]
                halo_start(value, *wave_halo, 1 - slot, *wave_sems, side)

        for index in range(1, chunks - 1):
            advance(index)

        for late in range(2):

            @pl.when(turn == FWD - 3 + late)
            def _():
                for index in range(chunks):
                    part = pl.ds(chunk * index, chunk)
                    term = (
                        wave[1 - slot, pl.ds(inside + chunk * index, chunk)]
                        * adj[ADJ - late, part]
                    )
                    image[part] = term if late == 0 else image[part] + term

        return carry

    lax.fori_loop(0, FWD, forward_step, 0)
    for index in range(chunks):
        part = pl.ds(chunk * index, chunk)
        image[part] = image[part] + wave[FWD % 2, pl.ds(inside + chunk * index, chunk)] * adj[1, part]

    theirs = (1 - core) * half
    mine = core * half
    swap = pltpu.make_async_remote_copy(
        src_ref=image.at[pl.ds(theirs, half)],
        dst_ref=from_core,
        send_sem=core_sem.at[0],
        recv_sem=core_sem.at[1],
        device_id=peer(partner),
        device_id_type=MESH,
    )
    swap.start()
    swap.wait()
    rows = size_y // chips
    for target in range(chips):
        cut = slice(target * rows, (target + 1) * rows)
        to_chip[target] = image[pl.ds(mine, half), cut] + from_core[:, cut]

    def chip_copy(target, landing):
        return pltpu.make_async_remote_copy(
            src_ref=to_chip.at[target],
            dst_ref=from_chip.at[landing],
            send_sem=chip_send.at[target],
            recv_sem=chip_recv.at[landing],
            device_id=peer(target * 2 + core),
            device_id_type=MESH,
        )

    def chip_start(turn, carry):
        chip_copy(lax.rem(chip + turn, chips), chip).start()
        return carry

    lax.fori_loop(1, chips, chip_start, 0)
    last[...] = to_chip[chip]

    def chip_add(turn, carry):
        other = lax.rem(chip + turn, chips)
        chip_copy(other, other).wait_recv()
        last[...] = last[...] + from_chip[other]
        return carry

    lax.fori_loop(1, chips, chip_add, 0)
    trade = pltpu.make_async_remote_copy(
        src_ref=last,
        dst_ref=last_in,
        send_sem=last_sem.at[0],
        recv_sem=last_sem.at[1],
        device_id=peer(partner),
        device_id_type=MESH,
    )
    trade.start()
    trade.wait()
    row_half = rows // 2
    first_core = core == 0
    for block, offset in ((last, mine), (last_in, theirs)):
        value = block[...]
        chosen = jnp.where(first_core, 1.0, 0.0)
        image_out[pl.ds(offset, half)] = (
            chosen * value[:, :row_half] + (1.0 - chosen) * value[:, row_half:]
        )

    def drain(turn, carry):
        other = lax.rem(me + turn, shots)
        for level in (1, 0):
            fetch_copy(level, other).wait_send()
        return carry

    lax.fori_loop(1, shots, drain, 0)

    def chip_drain(turn, carry):
        target = lax.rem(chip + turn, chips)
        chip_copy(target, chip).wait_send()
        return carry

    lax.fori_loop(1, chips, chip_drain, 0)
    result.wait()


def local(
    shots,
    spaces,
    courant,
    snapshot_store,
    slab_holder,
    snap_step,
    window_end,
    source_cell,
    wavelet,
    receiver_cells,
    residual_data,
    adjoint_prev,
    adjoint_now,
):
    planes, size_y, size_z = courant.shape
    slabs = snapshot_store.shape[0]
    cap = CAP
    chips = shots // 2
    rows = size_y // chips
    smem = pl.BlockSpec(memory_space=pltpu.SMEM)
    vmem = pl.BlockSpec(memory_space=pltpu.VMEM)
    anywhere = pl.BlockSpec(memory_space=pltpu.HBM)
    half = planes // 2
    padded = (2, planes + 2 * HALO, size_y, size_z)
    coded = (2, 2, HALO * size_y + SCALE_ROWS, size_z)
    dma = pltpu.SemaphoreType.DMA
    image, adjoint = pl.pallas_call(
        functools.partial(kernel, shots, spaces, cap),
        out_shape=(
            jax.ShapeDtypeStruct((planes, rows // 2, size_z), F32),
            jax.ShapeDtypeStruct((planes, size_y, size_z), F32),
        ),
        in_specs=[smem] * 5 + [vmem] * 2 + [anywhere] * 4,
        out_specs=(vmem, anywhere),
        scratch_shapes=[
            pltpu.VMEM((planes, size_y, size_z), F32),
            pltpu.VMEM((slabs, 2, size_y, size_z), BF16),
            pltpu.VMEM((ADJ + 2, planes, size_y, size_z), F32),
            pltpu.VMEM(padded, F32),
            pltpu.VMEM(padded, F32),
            pltpu.VMEM(coded, jnp.int16),
            pltpu.VMEM(coded, jnp.int16),
            pltpu.VMEM(coded, jnp.int16),
            pltpu.VMEM(coded, jnp.int16),
            pltpu.VMEM((2, shots * cap, size_y, size_z), BF16),
            pltpu.VMEM((2, shots * cap, size_y, size_z), BF16),
            pltpu.VMEM((size_z, size_z), BF16),
            pltpu.VMEM((HALO * size_y, HALO * size_y), BF16),
            pltpu.VMEM((size_y, size_z), F32),
            pltpu.VMEM((size_z, receiver_cells.shape[1]), BF16),
            pltpu.VMEM((planes, size_y, size_z), F32),
            pltpu.VMEM((half, size_y, size_z), F32),
            pltpu.VMEM((chips, half, rows, size_z), F32),
            pltpu.VMEM((chips, half, rows, size_z), F32),
            pltpu.VMEM((half, rows, size_z), F32),
            pltpu.VMEM((half, rows, size_z), F32),
            dma((4,)),
            dma((2, shots)),
            dma((2, shots)),
            dma((2, 2)),
            dma((2, 2)),
            dma((2, 2)),
            dma((2, 2)),
            dma((2,)),
            dma((chips,)),
            dma((chips,)),
            dma((2,)),
            dma((1,)),
        ],
        compiler_params=pltpu.CompilerParams(
            collective_id=0, has_side_effects=True, vmem_limit_bytes=48 * 2**20
        ),
    )(
        slab_holder,
        snap_step,
        window_end,
        source_cell,
        wavelet,
        receiver_cells,
        residual_data[0],
        courant,
        snapshot_store.reshape(slabs, 2, size_y, size_z),
        adjoint_prev[0],
        adjoint_now[0],
    )
    return (image * (1.0 / ADJ)).reshape(planes, rows // 2 * size_z), adjoint[None]


def solution(mesh):
    in_specs = (
        P("space", None, None),
        P("shot", None, "space", None, None),
        P(),
        P("shot"),
        P("shot"),
        P("shot"),
        P(),
        P("shot", None),
        P("shot", None, None),
        P("shot", "space", None, None),
        P("shot", "space", None, None),
    )
    out_specs = (P("space", "shot"), P("shot", "space", None, None))
    return jax.shard_map(
        functools.partial(local, mesh.shape["shot"], mesh.shape["space"]),
        mesh=mesh,
        in_specs=in_specs,
        out_specs=out_specs,
        check_vma=False,
    )
```

```python
import functools

import jax
import jax.numpy as jnp
from jax import lax
from jax.experimental import pallas as pl
from jax.experimental.pallas import tpu as pltpu
from jax.sharding import PartitionSpec as P

FWD = 8
ADJ = 3
HALO = 4
CAP = 2
SCALE = 5040.0
TAPS = (8064.0, -1008.0, 128.0, -9.0)
CENTRE_Z = -43008.0
CENTRE_Y = -42.0
CODE_BITS = 13.0
SCALE_ROWS = 16
MESH = pl.DeviceIdType.MESH
F32 = jnp.float32
BF16 = jnp.bfloat16


def band(size, block, centre):
    row = lax.broadcasted_iota(jnp.int32, (size, size), 0)
    col = lax.broadcasted_iota(jnp.int32, (size, size), 1)
    gap = jnp.abs(row - col)
    result = jnp.where(gap == 0, centre, 0.0)
    for offset, tap in enumerate(TAPS, 1):
        result = jnp.where(gap == offset, tap, result)
    if block < size:
        result = jnp.where(row // block == col // block, result, 0.0)
    return result.astype(BF16)


def split(value):
    high = value.astype(BF16)
    return high, (value - high.astype(F32)).astype(BF16)


def encode(value):
    rows = value.shape[0] * value.shape[1]
    flat = value.reshape(rows, value.shape[2])
    top = jnp.max(jnp.abs(flat), axis=0, keepdims=True)
    power = jnp.floor(jnp.log2(jnp.maximum(top, 1e-30)))
    code = jnp.round(flat * jnp.exp2(CODE_BITS - power)).astype(jnp.int32).astype(jnp.int16)
    scale = jnp.broadcast_to(power.astype(jnp.int32), (SCALE_ROWS, value.shape[2])).astype(jnp.int16)
    return code, scale


def decode(code, scale, shape):
    power = scale.astype(jnp.int32).astype(F32)[:1]
    return (code.astype(jnp.int32).astype(F32) * jnp.exp2(power - CODE_BITS)).reshape(shape)


def kernel(
    shots,
    spaces,
    cap,
    holder,
    snap_step,
    window_end,
    source_cell,
    wavelet,
    cells,
    residual,
    courant_in,
    store_in,
    prev_in,
    now_in,
    image_out,
    adjoint_out,
    courant,
    store,
    adj,
    field,
    wave,
    adj_code,
    adj_land,
    wave_code,
    wave_land,
    packed,
    landed_old,
    landed_new,
    band_z,
    band_y,
    spot,
    col_hot,
    image,
    split_image,
    from_core,
    to_chip,
    from_chip,
    sent_slots,
    own_slots,
    local_sem,
    fetch_send,
    fetch_recv,
    courant_send,
    courant_recv,
    adj_send,
    adj_recv,
    wave_send,
    wave_recv,
    core_send,
    core_recv,
    chip_send,
    chip_recv,
    out_sem,
):
    me = lax.axis_index("shot")
    place = lax.axis_index("space")
    slabs, _, size_y, size_z = store.shape
    planes = courant.shape[0] - 2 * HALO
    has_low = place > 0
    has_high = place < spaces - 1
    has_side = (has_low, has_high)
    core = lax.rem(me, 2)
    chip = lax.div(me, 2)
    chips = shots // 2
    partner = chip * 2 + 1 - core
    chunk = HALO
    chunks = planes // chunk
    deep = 2 * HALO
    edges = (0, chunks - 1)
    inner = tuple(range(1, chunks - 1))

    landed = (landed_old, landed_new)

    def peer(shot):
        return (shot, place)

    own_planes = pl.ds(HALO, planes)
    loads = [
        pltpu.make_async_copy(now_in, adj.at[1], local_sem.at[0]),
        pltpu.make_async_copy(courant_in, courant.at[own_planes], local_sem.at[1]),
        pltpu.make_async_copy(store_in, store, local_sem.at[2]),
        pltpu.make_async_copy(prev_in, adj.at[0], local_sem.at[3]),
    ]
    for load in loads:
        load.start()

    barrier = pltpu.get_barrier_semaphore()

    def greet(turn, carry):
        other = lax.rem(me + turn, shots)
        pl.semaphore_signal(barrier, inc=1, device_id=peer(other), device_id_type=MESH)
        return carry

    for side in range(2):

        @pl.when(has_side[side])
        def _():
            pl.semaphore_signal(
                barrier, inc=1, device_id=(me, place + 2 * side - 1), device_id_type=MESH
            )

    lax.fori_loop(1, shots, greet, 0)

    def find_sent(other, carry):
        found = jnp.int32(0)
        spots = [jnp.int32(0)] * cap
        for slab in range(slabs):
            slot = holder[other, slab]
            mine = lax.div(slot, slabs) == me
            where = lax.rem(slot, slabs)
            for rank in range(cap):
                spots[rank] = jnp.where(jnp.logical_and(mine, found == rank), where, spots[rank])
            found = found + jnp.where(mine, 1, 0)
        for rank in range(cap):
            sent_slots[other * cap + rank] = spots[rank]
        return carry

    lax.fori_loop(0, shots, find_sent, 0)

    def find_own(slab, carry):
        storer = lax.div(holder[me, slab], slabs)
        rank = jnp.int32(0)
        for before in range(slabs):
            same = jnp.logical_and(lax.div(holder[me, before], slabs) == storer, before < slab)
            rank = rank + jnp.where(same, 1, 0)
        own_slots[slab] = storer * cap + rank
        return carry

    band_z[...] = band(size_z, size_z, CENTRE_Z)
    band_y[...] = band(chunk * size_y, size_y, CENTRE_Y)
    for side in range(2):

        @pl.when(jnp.logical_not(has_side[side]))
        def _():
            nothing = jnp.zeros((HALO, size_y, size_z), F32)
            courant[pl.ds((planes + HALO) * side, HALO)] = nothing
            for slot in range(2):
                field[slot, pl.ds((planes + HALO) * side, HALO)] = nothing
                for piece in range(2):
                    wave[slot, pl.ds((planes + deep) * side + HALO * piece, HALO)] = nothing

    halo_rows = HALO * size_y
    edge_shape = (HALO, size_y, size_z)

    def adj_copy(slot, side):
        return pltpu.make_async_remote_copy(
            src_ref=adj_code.at[slot, side],
            dst_ref=adj_land.at[slot, side],
            send_sem=adj_send.at[slot, side],
            recv_sem=adj_recv.at[slot, side],
            device_id=(me, place + 2 * side - 1),
            device_id_type=MESH,
        )

    def adj_start(value, slot, side):
        @pl.when(has_side[side])
        def _():
            numbers, scale = encode(value)
            adj_code[slot, side, :halo_rows] = numbers
            adj_code[slot, side, halo_rows:] = scale
            adj_copy(slot, side).start()

    def adj_wait(slot, side):
        @pl.when(has_side[side])
        def _():
            adj_copy(slot, side).wait_send()
            adj_copy(slot, 1 - side).wait_recv()
            field[slot, pl.ds((HALO + planes) * side, HALO)] = decode(
                adj_land[slot, 1 - side, :halo_rows], adj_land[slot, 1 - side, halo_rows:], edge_shape
            )

    def wave_copy(slot, side, piece):
        return pltpu.make_async_remote_copy(
            src_ref=wave_code.at[slot, side, piece],
            dst_ref=wave_land.at[slot, side, piece],
            send_sem=wave_send.at[slot, side, piece],
            recv_sem=wave_recv.at[slot, side, piece],
            device_id=(me, place + 2 * side - 1),
            device_id_type=MESH,
        )

    def wave_start(level, slot, side, piece):
        index = piece if side == 0 else chunks - 1 - piece

        @pl.when(has_side[side])
        def _():
            numbers, scale = encode(wave[level, pl.ds(deep + chunk * index, chunk)])
            wave_code[slot, side, piece, :halo_rows] = numbers
            wave_code[slot, side, piece, halo_rows:] = scale
            wave_copy(slot, side, piece).start()

    def wave_wait(level, slot, side, piece):
        index = -1 - piece if side == 0 else chunks + piece

        @pl.when(has_side[side])
        def _():
            wave_copy(slot, side, piece).wait_send()
            wave_copy(slot, 1 - side, piece).wait_recv()
            wave[level, pl.ds(deep + chunk * index, chunk)] = decode(
                wave_land[slot, 1 - side, piece, :halo_rows],
                wave_land[slot, 1 - side, piece, halo_rows:],
                edge_shape,
            )

    def courant_copy(side):
        return pltpu.make_async_remote_copy(
            src_ref=courant_in.at[pl.ds((planes - HALO) * side, HALO)],
            dst_ref=courant.at[pl.ds((planes + HALO) * (1 - side), HALO)],
            send_sem=courant_send.at[side],
            recv_sem=courant_recv.at[side],
            device_id=(me, place + 2 * side - 1),
            device_id_type=MESH,
        )

    def stencil(ref, slot, first):
        middle = ref[slot, pl.ds(first, chunk)]
        high, low = split(middle.reshape(chunk * size_y, size_z))
        right = band_z[...]
        left = band_y[...]
        total = jnp.dot(high, right, preferred_element_type=F32)
        total += jnp.dot(low, right, preferred_element_type=F32)
        total += jnp.dot(left, high, preferred_element_type=F32)
        total += jnp.dot(left, low, preferred_element_type=F32)
        total = total.reshape(chunk, size_y, size_z)
        for offset, tap in enumerate(TAPS, 1):
            total += tap * (
                ref[slot, pl.ds(first + offset, chunk)] + ref[slot, pl.ds(first - offset, chunk)]
            )
        return total

    def first_field(index):
        part = pl.ds(HALO + chunk * index, chunk)
        scaled = courant[part] * (1.0 / SCALE)
        courant[part] = scaled
        value = scaled * adj[1, pl.ds(chunk * index, chunk)]
        field[0, part] = value
        return value

    loads[0].wait()
    loads[1].wait()
    low_count = jnp.where(has_low, 1, 0)
    high_count = jnp.where(has_high, 1, 0)
    pl.semaphore_wait(barrier, shots - 1 + low_count + high_count)
    for side, index in enumerate(edges):
        adj_start(first_field(index), 0, side)

    def fetch_copy(level, other):
        return pltpu.make_async_remote_copy(
            src_ref=packed.at[level, pl.ds(other * cap, cap)],
            dst_ref=landed[level].at[pl.ds(me * cap, cap)],
            send_sem=fetch_send.at[level, other],
            recv_sem=fetch_recv.at[level, me],
            device_id=peer(other),
            device_id_type=MESH,
        )

    def fetch_arrival(level, other):
        return pltpu.make_async_remote_copy(
            src_ref=packed.at[level, pl.ds(other * cap, cap)],
            dst_ref=landed[level].at[pl.ds(other * cap, cap)],
            send_sem=fetch_send.at[level, other],
            recv_sem=fetch_recv.at[level, other],
            device_id=peer(other),
            device_id_type=MESH,
        )

    loads[2].wait()
    for level in (1, 0):

        def pack(turn, carry):
            other = lax.rem(me + turn, shots)
            for rank in range(cap):
                packed[level, other * cap + rank] = store[sent_slots[other * cap + rank], level]
            fetch_copy(level, other).start()
            return carry

        lax.fori_loop(1, shots, pack, 0)

    for rank in range(cap):
        for level in (1, 0):
            landed[level][me * cap + rank] = store[sent_slots[me * cap + rank], level]

    for side in range(2):

        @pl.when(has_side[side])
        def _():
            courant_copy(side).start()

    for index in inner:
        first_field(index)
    lax.fori_loop(0, slabs, find_own, 0)

    plane_cells = size_y * size_z
    source = source_cell[0]
    source_plane = lax.div(source, plane_cells) - place * planes
    in_plane = lax.rem(source, plane_cells)
    flat = lax.broadcasted_iota(jnp.int32, (size_y, size_z), 0) * size_z + lax.broadcasted_iota(
        jnp.int32, (size_y, size_z), 1
    )
    spot[...] = jnp.where(flat == in_plane, 1.0, 0.0)

    recv_cells = cells[...]
    recv_row = recv_cells // size_z - place * (planes * size_y)
    recv_col = recv_cells % size_z
    count = recv_cells.shape[1]
    col_hot[...] = jnp.where(
        lax.broadcasted_iota(jnp.int32, (size_z, count), 0) == recv_col, 1.0, 0.0
    ).astype(BF16)

    loads[3].wait()

    def adjoint_step(turn, carry):
        slot = lax.rem(turn, 2)
        data = residual[0, pl.ds(turn, 1)]
        data_high, data_low = split(data)
        data_high = data_high.astype(F32)
        data_low = data_low.astype(F32)
        hot = col_hot[...]

        def advance(index):
            part = pl.ds(chunk * index, chunk)
            padded = pl.ds(HALO + chunk * index, chunk)
            row = lax.broadcasted_iota(jnp.int32, (chunk * size_y, count), 0) + (
                chunk * size_y * index
            )
            hit = row == recv_row
            total = lax.dot_general(
                jnp.where(hit, data_high, 0.0).astype(BF16),
                hot,
                (((1,), (1,)), ((), ())),
                preferred_element_type=F32,
            )
            total += lax.dot_general(
                jnp.where(hit, data_low, 0.0).astype(BF16),
                hot,
                (((1,), (1,)), ((), ())),
                preferred_element_type=F32,
            )
            total = total.reshape(chunk, size_y, size_z) + stencil(
                field, slot, HALO + chunk * index
            )
            current = adj[turn + 1, part]
            following = (current + current) - adj[turn, part] + total
            adj[turn + 2, part] = following
            field[1 - slot, padded] = courant[padded] * following

        for side, index in enumerate(edges):
            adj_wait(slot, side)
            advance(index)

            @pl.when(turn < ADJ - 1)
            def _():
                adj_start(field[1 - slot, pl.ds(HALO + chunk * index, chunk)], 1 - slot, side)

        for index in inner:
            advance(index)
        return carry

    lax.fori_loop(0, ADJ - 1, adjoint_step, 0)

    def arrive(level):
        def one(turn, carry):
            fetch_arrival(level, lax.rem(me + turn, shots)).wait_recv()
            return carry

        lax.fori_loop(1, shots, one, 0)

    arrive(1)

    def unpack(slab, carry):
        wave[0, deep + slab] = landed_new[own_slots[slab]].astype(F32)
        return carry

    lax.fori_loop(0, slabs, unpack, 0)
    for side in range(2):
        wave_start(0, 0, side, 0)

    steps = window_end[0] - snap_step[0]
    start = snap_step[0]

    def image_term(level, turn, index):
        behind = steps - turn
        weight = jnp.where(jnp.logical_and(behind >= 0, behind < ADJ), 1.0, 0.0)
        state = adj[1 + jnp.clip(behind, 0, ADJ - 1), pl.ds(chunk * index, chunk)]
        return (weight * state) * wave[level, pl.ds(deep + chunk * index, chunk)]

    def image_add(level, turn):
        for index in range(chunks):
            part = pl.ds(chunk * index, chunk)
            image[part] = image[part] + image_term(level, turn, index)

    def advance(level, turn, index, older=True):
        first = deep + chunk * index
        here = pl.ds(first, chunk)
        middle = wave[level, here]
        total = courant[pl.ds(first - HALO, chunk)] * stencil(wave, level, first)
        total = total + (middle + middle)
        if older:
            total = total - wave[1 - level, here]
        amplitude = wavelet[start + turn]
        pattern = spot[...]
        for plane in range(chunk):
            push = jnp.where(source_plane == chunk * index + plane, amplitude, 0.0)
            wave[1 - level, first + plane] = total[plane] + push * pattern

    for index in inner:
        advance(0, 0, index, older=False)
    for index in range(chunks):
        image[pl.ds(chunk * index, chunk)] = image_term(0, 0, index)
    adjoint_step(ADJ - 1, 0)
    result = pltpu.make_async_copy(adj.at[ADJ + 1], adjoint_out, out_sem.at[0])
    result.start()
    for side, index in enumerate(edges):
        wave_wait(0, 0, side, 0)
        advance(0, 0, index, older=False)
    arrive(0)

    def less(slab, carry):
        here = deep + slab
        wave[1, here] = wave[1, here] - landed_old[own_slots[slab]].astype(F32)
        return carry

    half = planes // 2
    for side in range(2):
        lax.fori_loop(half * side, half * (side + 1), less, 0)
        for piece in range(2):
            wave_start(1, 1, side, piece)

    for side in range(2):

        @pl.when(has_side[side])
        def _():
            courant_copy(side).wait_send()
            courant_copy(1 - side).wait_recv()
            part = pl.ds((planes + HALO) * side, HALO)
            courant[part] = courant[part] * (1.0 / SCALE)

    blocks = (FWD - 2) // 2

    def block(number, carry):
        turn = 1 + 2 * number
        slot = lax.rem(number + 1, 2)
        for index in inner:
            advance(1, turn, index)
        image_add(1, turn)
        for side in range(2):
            order = (0, 1) if side == 0 else (chunks - 1, chunks - 2)
            outside = -1 if side == 0 else chunks
            wave_wait(1, slot, side, 0)
            advance(1, turn, order[0])
            wave_wait(1, slot, side, 1)
            advance(1, turn, outside)
            advance(0, turn + 1, order[0])
            wave_start(1, 1 - slot, side, 0)
            advance(0, turn + 1, order[1])

            @pl.when(number < blocks - 1)
            def _():
                wave_start(1, 1 - slot, side, 1)

        image_add(0, turn + 1)
        return carry

    lax.fori_loop(0, blocks, block, 0)

    rows = size_y // chips
    row_half = rows // 2

    def cut_image(piece, place_in, index):
        value = image[pl.ds(chunk * index, chunk)] + image_term(0, FWD, index)
        for target in range(chips):
            for side in range(2):
                low = target * rows + side * row_half
                split_image[side, piece, target, pl.ds(chunk * place_in, chunk)] = value[
                    :, low : low + row_half
                ]

    def core_copy(piece):
        return pltpu.make_async_remote_copy(
            src_ref=split_image.at[1 - core, piece],
            dst_ref=from_core.at[piece],
            send_sem=core_send.at[piece],
            recv_sem=core_recv.at[piece],
            device_id=peer(partner),
            device_id_type=MESH,
        )

    def chip_copy(piece, target, landing):
        return pltpu.make_async_remote_copy(
            src_ref=to_chip.at[piece, target],
            dst_ref=from_chip.at[piece, landing],
            send_sem=chip_send.at[piece, target],
            recv_sem=chip_recv.at[piece, landing],
            device_id=peer(target * 2 + core),
            device_id_type=MESH,
        )

    def to_chips(piece):
        core_copy(piece).wait()

        def one(turn, carry):
            target = lax.rem(chip + turn, chips)
            to_chip[piece, target] = split_image[core, piece, target] + from_core[piece, target]
            chip_copy(piece, target, chip).start()
            return carry

        lax.fori_loop(1, chips, one, 0)
        to_chip[piece, chip] = split_image[core, piece, chip] + from_core[piece, chip]

    for index in inner:
        advance(1, FWD - 1, index)
    for order, index in enumerate(inner):
        image[pl.ds(chunk * index, chunk)] = image[pl.ds(chunk * index, chunk)] + image_term(
            1, FWD - 1, index
        )
        cut_image(0, order, index)
    core_copy(0).start()
    for index in edges:
        image[pl.ds(chunk * index, chunk)] = image[pl.ds(chunk * index, chunk)] + image_term(
            1, FWD - 1, index
        )
    to_chips(0)
    last_slot = (blocks + 1) % 2
    for side, index in enumerate(edges):
        wave_wait(1, last_slot, side, 0)
        advance(1, FWD - 1, index)
        cut_image(1, side, index)
    core_copy(1).start()
    to_chips(1)

    for piece in range(2):

        def add(turn, carry):
            other = lax.rem(chip + turn, chips)
            chip_copy(piece, other, other).wait_recv()
            chip_copy(piece, other, chip).wait_send()
            to_chip[piece, chip] = to_chip[piece, chip] + from_chip[piece, other]
            return carry

        lax.fori_loop(1, chips, add, 0)
        total = to_chip[piece, chip]
        for order, index in enumerate((inner, edges)[piece]):
            image_out[pl.ds(chunk * index, chunk)] = total[chunk * order : chunk * (order + 1)]

    def drain(turn, carry):
        other = lax.rem(me + turn, shots)
        for level in (1, 0):
            fetch_copy(level, other).wait_send()
        return carry

    lax.fori_loop(1, shots, drain, 0)
    result.wait()


def local(
    shots,
    spaces,
    courant,
    snapshot_store,
    slab_holder,
    snap_step,
    window_end,
    source_cell,
    wavelet,
    receiver_cells,
    residual_data,
    adjoint_prev,
    adjoint_now,
):
    planes, size_y, size_z = courant.shape
    slabs = snapshot_store.shape[0]
    cap = CAP
    chips = shots // 2
    rows = size_y // chips
    smem = pl.BlockSpec(memory_space=pltpu.SMEM)
    vmem = pl.BlockSpec(memory_space=pltpu.VMEM)
    hbm = pl.BlockSpec(memory_space=pltpu.HBM)
    half = planes // 2
    coded = (HALO * size_y + SCALE_ROWS, size_z)
    dma = pltpu.SemaphoreType.DMA
    image, adjoint = pl.pallas_call(
        functools.partial(kernel, shots, spaces, cap),
        out_shape=(
            jax.ShapeDtypeStruct((planes, rows // 2, size_z), F32),
            jax.ShapeDtypeStruct((planes, size_y, size_z), F32),
        ),
        in_specs=[smem] * 5 + [vmem] * 2 + [hbm] * 4,
        out_specs=(vmem, hbm),
        scratch_shapes=[
            pltpu.VMEM((planes + 2 * HALO, size_y, size_z), F32),
            pltpu.VMEM((slabs, 2, size_y, size_z), BF16),
            pltpu.VMEM((ADJ + 2, planes, size_y, size_z), F32),
            pltpu.VMEM((2, planes + 2 * HALO, size_y, size_z), F32),
            pltpu.VMEM((2, planes + 4 * HALO, size_y, size_z), F32),
            pltpu.VMEM((2, 2) + coded, jnp.int16),
            pltpu.VMEM((2, 2) + coded, jnp.int16),
            pltpu.VMEM((2, 2, 2) + coded, jnp.int16),
            pltpu.VMEM((2, 2, 2) + coded, jnp.int16),
            pltpu.VMEM((2, shots * cap, size_y, size_z), BF16),
            pltpu.VMEM((shots * cap, size_y, size_z), BF16),
            pltpu.VMEM((shots * cap, size_y, size_z), BF16),
            pltpu.VMEM((size_z, size_z), BF16),
            pltpu.VMEM((HALO * size_y, HALO * size_y), BF16),
            pltpu.VMEM((size_y, size_z), F32),
            pltpu.VMEM((size_z, receiver_cells.shape[1]), BF16),
            pltpu.VMEM((planes, size_y, size_z), F32),
            pltpu.VMEM((2, 2, chips, half, rows // 2, size_z), F32),
            pltpu.VMEM((2, chips, half, rows // 2, size_z), F32),
            pltpu.VMEM((2, chips, half, rows // 2, size_z), F32),
            pltpu.VMEM((2, chips, half, rows // 2, size_z), F32),
            pltpu.SMEM((shots * cap,), jnp.int32),
            pltpu.SMEM((slabs,), jnp.int32),
            dma((4,)),
            dma((2, shots)),
            dma((2, shots)),
            dma((2,)),
            dma((2,)),
            dma((2, 2)),
            dma((2, 2)),
            dma((2, 2, 2)),
            dma((2, 2, 2)),
            dma((2,)),
            dma((2,)),
            dma((2, chips)),
            dma((2, chips)),
            dma((1,)),
        ],
        compiler_params=pltpu.CompilerParams(
            collective_id=0, has_side_effects=True, vmem_limit_bytes=63 * 2**20
        ),
    )(
        slab_holder,
        snap_step,
        window_end,
        source_cell,
        wavelet,
        receiver_cells,
        residual_data,
        courant,
        snapshot_store.reshape(slabs, 2, size_y, size_z),
        adjoint_prev[0],
        adjoint_now[0],
    )
    return (image * (1.0 / ADJ)).reshape(planes, rows // 2 * size_z), adjoint[None]


def solution(mesh):
    in_specs = (
        P("space", None, None),
        P("shot", None, "space", None, None),
        P(),
        P("shot"),
        P("shot"),
        P("shot"),
        P(),
        P("shot", None),
        P("shot", None, None),
        P("shot", "space", None, None),
        P("shot", "space", None, None),
    )
    out_specs = (P("space", "shot"), P("shot", "space", None, None))
    return jax.shard_map(
        functools.partial(local, mesh.shape["shot"], mesh.shape["space"]),
        mesh=mesh,
        in_specs=in_specs,
        out_specs=out_specs,
        check_vma=False,
    )
```

```python
import functools

import jax
import jax.numpy as jnp
from jax import lax
from jax.experimental import pallas as pl
from jax.experimental.pallas import tpu as pltpu
from jax.sharding import PartitionSpec as P

FWD = 8
ADJ = 3
HALO = 4
CAP = 2
SCALE = 5040.0
TAPS = (8064.0, -1008.0, 128.0, -9.0)
CENTRE_Z = -43008.0
CENTRE_Y = -42.0
CODE_BITS = 13.0
RIM = 3 * HALO
SCALE_ROWS = 16
MESH = pl.DeviceIdType.MESH
F32 = jnp.float32
BF16 = jnp.bfloat16


def band(size, block, centre):
    row = lax.broadcasted_iota(jnp.int32, (size, size), 0)
    col = lax.broadcasted_iota(jnp.int32, (size, size), 1)
    gap = jnp.abs(row - col)
    result = jnp.where(gap == 0, centre, 0.0)
    for offset, tap in enumerate(TAPS, 1):
        result = jnp.where(gap == offset, tap, result)
    if block < size:
        result = jnp.where(row // block == col // block, result, 0.0)
    return result.astype(BF16)


def split(value):
    high = value.astype(BF16)
    return high, (value - high.astype(F32)).astype(BF16)


def encode(value):
    rows = value.shape[0] * value.shape[1]
    flat = value.reshape(rows, value.shape[2])
    top = jnp.max(jnp.abs(flat), axis=0, keepdims=True)
    power = jnp.floor(jnp.log2(jnp.maximum(top, 1e-30)))
    code = jnp.round(flat * jnp.exp2(CODE_BITS - power)).astype(jnp.int32).astype(jnp.int16)
    scale = jnp.broadcast_to(power.astype(jnp.int32), (SCALE_ROWS, value.shape[2])).astype(jnp.int16)
    return code, scale


def decode(code, scale, shape):
    power = scale.astype(jnp.int32).astype(F32)[:1]
    return (code.astype(jnp.int32).astype(F32) * jnp.exp2(power - CODE_BITS)).reshape(shape)


def kernel(
    shots,
    spaces,
    cap,
    holder,
    snap_step,
    window_end,
    source_cell,
    wavelet,
    cells,
    residual,
    courant_in,
    store_in,
    prev_in,
    now_in,
    image_out,
    adjoint_out,
    courant,
    store,
    adj,
    field,
    wave,
    adj_code,
    adj_land,
    wave_code,
    past_code,
    wave_land,
    packed,
    landed_old,
    landed_new,
    band_z,
    band_y,
    spot,
    col_hot,
    image,
    split_image,
    from_core,
    to_chip,
    from_chip,
    sent_slots,
    own_slots,
    local_sem,
    fetch_send,
    fetch_recv,
    courant_send,
    courant_recv,
    adj_send,
    adj_recv,
    wave_send,
    wave_recv,
    courant_swap_send,
    courant_swap_recv,
    core_send,
    core_recv,
    chip_send,
    chip_recv,
    out_sem,
):
    me = lax.axis_index("shot")
    place = lax.axis_index("space")
    slabs, _, size_y, size_z = store.shape
    planes = courant.shape[0] - 2 * RIM
    has_low = place > 0
    has_high = place < spaces - 1
    has_side = (has_low, has_high)
    core = lax.rem(me, 2)
    chip = lax.div(me, 2)
    chips = shots // 2
    partner = chip * 2 + 1 - core
    chunk = HALO
    chunks = planes // chunk
    deep = 4 * HALO
    edges = (0, chunks - 1)
    inner = tuple(range(1, chunks - 1))

    landed = (landed_old, landed_new)

    def peer(shot):
        return (shot, place)

    own_planes = pl.ds(RIM, planes)
    loads = [
        pltpu.make_async_copy(now_in, adj.at[1], local_sem.at[0]),
        pltpu.make_async_copy(courant_in, courant.at[own_planes], local_sem.at[1]),
        pltpu.make_async_copy(store_in, store, local_sem.at[2]),
        pltpu.make_async_copy(prev_in, adj.at[0], local_sem.at[3]),
    ]
    for load in loads:
        load.start()

    barrier = pltpu.get_barrier_semaphore()

    def greet(turn, carry):
        other = lax.rem(me + turn, shots)
        pl.semaphore_signal(barrier, inc=1, device_id=peer(other), device_id_type=MESH)
        return carry

    for side in range(2):

        @pl.when(has_side[side])
        def _():
            pl.semaphore_signal(
                barrier, inc=1, device_id=(me, place + 2 * side - 1), device_id_type=MESH
            )

    lax.fori_loop(1, shots, greet, 0)

    def find_sent(other):
        found = jnp.int32(0)
        spots = [jnp.int32(0)] * cap
        for slab in range(slabs):
            slot = holder[other, slab]
            mine = lax.div(slot, slabs) == me
            where = lax.rem(slot, slabs)
            for rank in range(cap):
                spots[rank] = jnp.where(jnp.logical_and(mine, found == rank), where, spots[rank])
            found = found + jnp.where(mine, 1, 0)
        for rank in range(cap):
            sent_slots[other * cap + rank] = spots[rank]

    def find_own(slab, carry):
        storer = lax.div(holder[me, slab], slabs)
        rank = jnp.int32(0)
        for before in range(slabs):
            same = jnp.logical_and(lax.div(holder[me, before], slabs) == storer, before < slab)
            rank = rank + jnp.where(same, 1, 0)
        own_slots[slab] = storer * cap + rank
        return carry

    halo_rows = HALO * size_y
    edge_shape = (HALO, size_y, size_z)

    def adj_copy(slot, side):
        return pltpu.make_async_remote_copy(
            src_ref=adj_code.at[slot, side],
            dst_ref=adj_land.at[slot, side],
            send_sem=adj_send.at[slot, side],
            recv_sem=adj_recv.at[slot, side],
            device_id=(me, place + 2 * side - 1),
            device_id_type=MESH,
        )

    def adj_start(value, slot, side):
        @pl.when(has_side[side])
        def _():
            numbers, scale = encode(value)
            adj_code[slot, side, :halo_rows] = numbers
            adj_code[slot, side, halo_rows:] = scale
            adj_copy(slot, side).start()

    def adj_wait(slot, side):
        @pl.when(has_side[side])
        def _():
            adj_copy(slot, side).wait_send()
            adj_copy(slot, 1 - side).wait_recv()
            field[slot, pl.ds((HALO + planes) * side, HALO)] = decode(
                adj_land[slot, 1 - side, :halo_rows], adj_land[slot, 1 - side, halo_rows:], edge_shape
            )

    def wave_copy(slot, side, piece):
        index = piece if side == 0 else chunks - 1 - piece
        if slot == 2 and piece == 3:
            source = past_code.at[side]
        else:
            source = wave_code.at[slot, index]
        return pltpu.make_async_remote_copy(
            src_ref=source,
            dst_ref=wave_land.at[slot, side, piece],
            send_sem=wave_send.at[slot, side, piece],
            recv_sem=wave_recv.at[slot, side, piece],
            device_id=(me, place + 2 * side - 1),
            device_id_type=MESH,
        )

    def wave_start(level, slot, index, pieces):
        numbers, scale = encode(wave[level, pl.ds(deep + chunk * index, chunk)])
        wave_code[slot, index, :halo_rows] = numbers
        wave_code[slot, index, halo_rows:] = scale
        for side in range(2):
            piece = index if side == 0 else chunks - 1 - index
            if piece < pieces:

                @pl.when(has_side[side])
                def _():
                    wave_copy(slot, side, piece).start()

    def past_start(level, side):
        index = 1 if side == 0 else chunks - 2

        @pl.when(has_side[side])
        def _():
            numbers, scale = encode(wave[level, pl.ds(deep + chunk * index, chunk)])
            past_code[side, :halo_rows] = numbers
            past_code[side, halo_rows:] = scale
            wave_copy(2, side, 3).start()

    def wave_wait(level, slot, side, piece, outside=None):
        if outside is None:
            outside = piece
        index = -1 - outside if side == 0 else chunks + outside

        @pl.when(has_side[side])
        def _():
            wave_copy(slot, side, piece).wait_send()
            wave_copy(slot, 1 - side, piece).wait_recv()
            wave[level, pl.ds(deep + chunk * index, chunk)] = decode(
                wave_land[slot, 1 - side, piece, :halo_rows],
                wave_land[slot, 1 - side, piece, halo_rows:],
                edge_shape,
            )

    rim_half = RIM // 2

    def courant_copy(side):
        return pltpu.make_async_remote_copy(
            src_ref=courant_in.at[pl.ds((planes - RIM) * side + rim_half * core, rim_half)],
            dst_ref=courant.at[pl.ds((planes + RIM) * (1 - side) + rim_half * core, rim_half)],
            send_sem=courant_send.at[side],
            recv_sem=courant_recv.at[side],
            device_id=(me, place + 2 * side - 1),
            device_id_type=MESH,
        )

    def courant_swap(side, half):
        part = pl.ds((planes + RIM) * side + rim_half * half, rim_half)
        return pltpu.make_async_remote_copy(
            src_ref=courant.at[part],
            dst_ref=courant.at[part],
            send_sem=courant_swap_send.at[side],
            recv_sem=courant_swap_recv.at[side],
            device_id=peer(partner),
            device_id_type=MESH,
        )

    def stencil(ref, slot, first):
        middle = ref[slot, pl.ds(first, chunk)]
        high, low = split(middle.reshape(chunk * size_y, size_z))
        right = band_z[...]
        left = band_y[...]
        total = jnp.dot(high, right, preferred_element_type=F32)
        total += jnp.dot(low, right, preferred_element_type=F32)
        total += jnp.dot(left, high, preferred_element_type=F32)
        total += jnp.dot(left, low, preferred_element_type=F32)
        total = total.reshape(chunk, size_y, size_z)
        for offset, tap in enumerate(TAPS, 1):
            total += tap * (
                ref[slot, pl.ds(first + offset, chunk)] + ref[slot, pl.ds(first - offset, chunk)]
            )
        return total

    def first_field(index):
        part = pl.ds(HALO + chunk * index, chunk)
        rim_part = pl.ds(RIM + chunk * index, chunk)
        scaled = courant[rim_part] * (1.0 / SCALE)
        courant[rim_part] = scaled
        value = scaled * adj[1, pl.ds(chunk * index, chunk)]
        field[0, part] = value
        return value

    loads[0].wait()
    loads[1].wait()
    low_count = jnp.where(has_low, 1, 0)
    high_count = jnp.where(has_high, 1, 0)
    pl.semaphore_wait(barrier, shots - 1 + low_count + high_count)
    for side, index in enumerate(edges):
        adj_start(first_field(index), 0, side)

    def fetch_copy(level, other):
        return pltpu.make_async_remote_copy(
            src_ref=packed.at[level, pl.ds(other * cap, cap)],
            dst_ref=landed[level].at[pl.ds(me * cap, cap)],
            send_sem=fetch_send.at[level, other],
            recv_sem=fetch_recv.at[level, me],
            device_id=peer(other),
            device_id_type=MESH,
        )

    def fetch_arrival(level, other):
        return pltpu.make_async_remote_copy(
            src_ref=packed.at[level, pl.ds(other * cap, cap)],
            dst_ref=landed[level].at[pl.ds(other * cap, cap)],
            send_sem=fetch_send.at[level, other],
            recv_sem=fetch_recv.at[level, other],
            device_id=peer(other),
            device_id_type=MESH,
        )

    loads[2].wait()
    for level in (1, 0):

        def pack(turn, carry):
            other = lax.rem(me + turn, shots)
            if level == 1:
                find_sent(other)
            for rank in range(cap):
                packed[level, other * cap + rank] = store[sent_slots[other * cap + rank], level]
            fetch_copy(level, other).start()
            return carry

        lax.fori_loop(1, shots, pack, 0)

    find_sent(me)
    for rank in range(cap):
        for level in (1, 0):
            landed[level][me * cap + rank] = store[sent_slots[me * cap + rank], level]

    for side in range(2):

        @pl.when(has_side[side])
        def _():
            courant_copy(side).start()

    band_z[...] = band(size_z, size_z, CENTRE_Z)
    band_y[...] = band(chunk * size_y, size_y, CENTRE_Y)
    for side in range(2):

        @pl.when(jnp.logical_not(has_side[side]))
        def _():
            nothing = jnp.zeros((HALO, size_y, size_z), F32)
            for piece in range(3):
                courant[pl.ds((planes + RIM) * side + HALO * piece, HALO)] = nothing
            for slot in range(2):
                field[slot, pl.ds((planes + HALO) * side, HALO)] = nothing
                for piece in range(4):
                    wave[slot, pl.ds((planes + deep) * side + HALO * piece, HALO)] = nothing

    for index in inner:
        first_field(index)
    lax.fori_loop(0, slabs, find_own, 0)

    plane_cells = size_y * size_z
    source = source_cell[0]
    source_plane = lax.div(source, plane_cells) - place * planes
    in_plane = lax.rem(source, plane_cells)
    flat = lax.broadcasted_iota(jnp.int32, (size_y, size_z), 0) * size_z + lax.broadcasted_iota(
        jnp.int32, (size_y, size_z), 1
    )
    spot[...] = jnp.where(flat == in_plane, 1.0, 0.0)

    recv_cells = cells[...]
    recv_row = recv_cells // size_z - place * (planes * size_y)
    recv_col = recv_cells % size_z
    count = recv_cells.shape[1]
    col_hot[...] = jnp.where(
        lax.broadcasted_iota(jnp.int32, (size_z, count), 0) == recv_col, 1.0, 0.0
    ).astype(BF16)

    loads[3].wait()

    def adjoint_step(turn, carry):
        slot = lax.rem(turn, 2)
        data = residual[turn]
        data_high, data_low = split(data)
        data_high = data_high.astype(F32)
        data_low = data_low.astype(F32)
        hot = col_hot[...]

        def advance(index):
            part = pl.ds(chunk * index, chunk)
            padded = pl.ds(HALO + chunk * index, chunk)
            row = lax.broadcasted_iota(jnp.int32, (chunk * size_y, count), 0) + (
                chunk * size_y * index
            )
            hit = row == recv_row
            total = lax.dot_general(
                jnp.where(hit, data_high, 0.0).astype(BF16),
                hot,
                (((1,), (1,)), ((), ())),
                preferred_element_type=F32,
            )
            total += lax.dot_general(
                jnp.where(hit, data_low, 0.0).astype(BF16),
                hot,
                (((1,), (1,)), ((), ())),
                preferred_element_type=F32,
            )
            total = total.reshape(chunk, size_y, size_z) + stencil(
                field, slot, HALO + chunk * index
            )
            current = adj[turn + 1, part]
            following = (current + current) - adj[turn, part] + total
            adj[turn + 2, part] = following
            field[1 - slot, padded] = courant[pl.ds(RIM + chunk * index, chunk)] * following

        for side, index in enumerate(edges):
            adj_wait(slot, side)
            advance(index)

            @pl.when(turn < ADJ - 1)
            def _():
                adj_start(field[1 - slot, pl.ds(HALO + chunk * index, chunk)], 1 - slot, side)

        for index in inner:
            advance(index)
        return carry

    adjoint_step(0, 0)

    for side in range(2):

        @pl.when(has_side[side])
        def _():
            courant_copy(side).wait_send()
            courant_copy(1 - side).wait_recv()
            courant_swap(side, core).start()

    def arrive(level):
        def one(turn, carry):
            fetch_arrival(level, lax.rem(me + turn, shots)).wait_recv()
            return carry

        lax.fori_loop(1, shots, one, 0)

    arrive(1)

    def unpack(slab, carry):
        wave[0, deep + slab] = landed_new[own_slots[slab]].astype(F32)
        return carry

    outer_first = edges + inner
    for index in outer_first:
        lax.fori_loop(chunk * index, chunk * (index + 1), unpack, 0)
        wave_start(0, 0, index, 3)
    adjoint_step(1, 0)

    steps = window_end[0] - snap_step[0]
    start = snap_step[0]

    def image_term(level, turn, index):
        behind = steps - turn
        weight = jnp.where(jnp.logical_and(behind >= 0, behind < ADJ), 1.0, 0.0)
        state = adj[1 + jnp.clip(behind, 0, ADJ - 1), pl.ds(chunk * index, chunk)]
        return (weight * state) * wave[level, pl.ds(deep + chunk * index, chunk)]

    def image_add(level, turn, index):
        part = pl.ds(chunk * index, chunk)
        image[part] = image[part] + image_term(level, turn, index)

    def advance(level, turn, index, older=True):
        first = deep + chunk * index
        here = pl.ds(first, chunk)
        middle = wave[level, here]
        total = courant[pl.ds(RIM + chunk * index, chunk)] * stencil(wave, level, first)
        total = total + (middle + middle)
        if older:
            total = total - wave[1 - level, here]
        amplitude = wavelet[start + turn]
        pattern = spot[...]
        for plane in range(chunk):
            push = jnp.where(source_plane == chunk * index + plane, amplitude, 0.0)
            wave[1 - level, first + plane] = total[plane] + push * pattern

    for index in inner:
        advance(0, 0, index, older=False)
    for index in range(chunks):
        image[pl.ds(chunk * index, chunk)] = image_term(0, 0, index)
    for side, index in enumerate(edges):
        wave_wait(0, 0, side, 0)
        advance(0, 0, index, older=False)
    arrive(0)

    def less(slab, carry):
        here = deep + slab
        wave[1, here] = wave[1, here] - landed_old[own_slots[slab]].astype(F32)
        return carry

    for index in outer_first:
        lax.fori_loop(chunk * index, chunk * (index + 1), less, 0)
        wave_start(1, 1, index, 4)
    adjoint_step(ADJ - 1, 0)
    result = pltpu.make_async_copy(adj.at[ADJ + 1], adjoint_out, out_sem.at[0])
    result.start()
    for index in range(chunks):
        image_add(1, 1, index)
    for piece in range(1, 3):
        for side in range(2):
            wave_wait(0, 0, side, piece)
    for side in range(2):

        @pl.when(has_side[side])
        def _():
            courant_swap(side, core).wait_send()
            courant_swap(side, 1 - core).wait_recv()
            for piece in range(3):
                part = pl.ds((planes + RIM) * side + HALO * piece, HALO)
                courant[part] = courant[part] * (1.0 / SCALE)

    def block(turn, length, slot, arrivals, finish):
        there = set(range(chunks))
        past = set(range(-3, chunks + 3)) if slot == 1 else set(range(-1, chunks + 1))
        done = set()

        def ready(step, index):
            if (step, index) in done:
                return False
            needs = (index - 1, index, index + 1)
            if step == 1:
                return index in past and all(need in there for need in needs)
            return all((step - 1, need) in done for need in needs)

        def run():
            for step in range(1, length + 1):
                reach = length - step
                for index in sorted(
                    range(-reach, chunks + reach), key=lambda at: (at not in edges, at)
                ):
                    if ready(step, index):
                        level = (turn + step - 1) % 2
                        advance(level, turn + step - 1, index)
                        done.add((step, index))
                        finish(step, index)

        run()
        for piece in arrivals:
            for side in range(2):
                sign = -1 if side == 0 else 1
                base = 0 if side == 0 else chunks - 1
                if slot == 2 and piece == 3:
                    wave_wait((turn + 1) % 2, slot, side, piece, outside=1)
                    past.add(base + sign * 2)
                else:
                    wave_wait(turn % 2, slot, side, piece)
                    there.add(base + sign * (1 + piece))
                run()

    def finish_long(step, index):
        own = 0 <= index < chunks
        if own:
            image_add((1 + step) % 2, 1 + step, index)
        if step == 3 and index in inner:
            past_start(0, 0 if index == 1 else 1)
        if step == 4:
            wave_start(1, 2, index, 3)

    block(1, 4, 1, (0, 1, 2, 3), finish_long)

    rows = size_y // chips
    row_half = rows // 2

    def cut_image(piece, place_in, index):
        value = image[pl.ds(chunk * index, chunk)] + image_term(0, FWD, index)
        for target in range(chips):
            for side in range(2):
                low = target * rows + side * row_half
                split_image[side, piece, target, pl.ds(chunk * place_in, chunk)] = value[
                    :, low : low + row_half
                ]

    def core_copy(piece):
        return pltpu.make_async_remote_copy(
            src_ref=split_image.at[1 - core, piece],
            dst_ref=from_core.at[piece],
            send_sem=core_send.at[piece],
            recv_sem=core_recv.at[piece],
            device_id=peer(partner),
            device_id_type=MESH,
        )

    def chip_copy(piece, target, landing):
        return pltpu.make_async_remote_copy(
            src_ref=to_chip.at[piece, target],
            dst_ref=from_chip.at[piece, landing],
            send_sem=chip_send.at[piece, target],
            recv_sem=chip_recv.at[piece, landing],
            device_id=peer(target * 2 + core),
            device_id_type=MESH,
        )

    def to_chips(piece):
        core_copy(piece).wait()

        def one(turn, carry):
            target = lax.rem(chip + turn, chips)
            to_chip[piece, target] = split_image[core, piece, target] + from_core[piece, target]
            chip_copy(piece, target, chip).start()
            return carry

        lax.fori_loop(1, chips, one, 0)
        to_chip[piece, chip] = split_image[core, piece, chip] + from_core[piece, chip]

    finished = set()

    def finish_last(step, index):
        if step < 3:
            if 0 <= index < chunks:
                image_add((5 + step) % 2, 5 + step, index)
            return
        piece = 0 if index in inner else 1
        cut_image(piece, (inner, edges)[piece].index(index), index)
        finished.add(index)
        if piece == 0 and all(other in finished for other in inner):
            core_copy(0).start()
        if piece == 1 and len(finished) == chunks - 1:
            to_chips(0)

    block(5, 3, 2, (0, 3, 1, 2), finish_last)
    core_copy(1).start()
    to_chips(1)

    for piece in range(2):

        def add(turn, carry):
            other = lax.rem(chip + turn, chips)
            chip_copy(piece, other, other).wait_recv()
            chip_copy(piece, other, chip).wait_send()
            to_chip[piece, chip] = to_chip[piece, chip] + from_chip[piece, other]
            return carry

        lax.fori_loop(1, chips, add, 0)
        total = to_chip[piece, chip]
        for order, index in enumerate((inner, edges)[piece]):
            image_out[pl.ds(chunk * index, chunk)] = total[chunk * order : chunk * (order + 1)]

    def drain(turn, carry):
        other = lax.rem(me + turn, shots)
        for level in (1, 0):
            fetch_copy(level, other).wait_send()
        return carry

    lax.fori_loop(1, shots, drain, 0)
    result.wait()


def finish(image, adjoint, image_out, adjoint_out, sem):
    copy = pltpu.make_async_copy(adjoint, adjoint_out.at[0], sem.at[0])
    copy.start()
    size_z = image.shape[2]
    for row in range(image.shape[1]):
        image_out[:, row * size_z : (row + 1) * size_z] = image[:, row] * (1.0 / ADJ)
    copy.wait()


def local(
    shots,
    spaces,
    courant,
    snapshot_store,
    slab_holder,
    snap_step,
    window_end,
    source_cell,
    wavelet,
    receiver_cells,
    residual_data,
    adjoint_prev,
    adjoint_now,
):
    planes, size_y, size_z = courant.shape
    slabs = snapshot_store.shape[0]
    cap = CAP
    chips = shots // 2
    rows = size_y // chips
    smem = pl.BlockSpec(memory_space=pltpu.SMEM)
    vmem = pl.BlockSpec(memory_space=pltpu.VMEM)
    hbm = pl.BlockSpec(memory_space=pltpu.HBM)
    half = planes // 2
    coded = (HALO * size_y + SCALE_ROWS, size_z)
    dma = pltpu.SemaphoreType.DMA
    image, adjoint = pl.pallas_call(
        functools.partial(kernel, shots, spaces, cap),
        out_shape=(
            jax.ShapeDtypeStruct((planes, rows // 2, size_z), F32),
            jax.ShapeDtypeStruct((planes, size_y, size_z), F32),
        ),
        in_specs=[smem] * 5 + [vmem] * 2 + [hbm] * 4,
        out_specs=(vmem, hbm),
        scratch_shapes=[
            pltpu.VMEM((planes + 2 * RIM, size_y, size_z), F32),
            pltpu.VMEM((slabs, 2, size_y, size_z), BF16),
            pltpu.VMEM((ADJ + 2, planes, size_y, size_z), F32),
            pltpu.VMEM((2, planes + 2 * HALO, size_y, size_z), F32),
            pltpu.VMEM((2, planes + 8 * HALO, size_y, size_z), F32),
            pltpu.VMEM((2, 2) + coded, jnp.int16),
            pltpu.VMEM((2, 2) + coded, jnp.int16),
            pltpu.VMEM((3, planes // HALO) + coded, jnp.int16),
            pltpu.VMEM((2,) + coded, jnp.int16),
            pltpu.VMEM((3, 2, 4) + coded, jnp.int16),
            pltpu.VMEM((2, shots * cap, size_y, size_z), BF16),
            pltpu.VMEM((shots * cap, size_y, size_z), BF16),
            pltpu.VMEM((shots * cap, size_y, size_z), BF16),
            pltpu.VMEM((size_z, size_z), BF16),
            pltpu.VMEM((HALO * size_y, HALO * size_y), BF16),
            pltpu.VMEM((size_y, size_z), F32),
            pltpu.VMEM((size_z, receiver_cells.shape[1]), BF16),
            pltpu.VMEM((planes, size_y, size_z), F32),
            pltpu.VMEM((2, 2, chips, half, rows // 2, size_z), F32),
            pltpu.VMEM((2, chips, half, rows // 2, size_z), F32),
            pltpu.VMEM((2, chips, half, rows // 2, size_z), F32),
            pltpu.VMEM((2, chips, half, rows // 2, size_z), F32),
            pltpu.SMEM((shots * cap,), jnp.int32),
            pltpu.SMEM((slabs,), jnp.int32),
            dma((4,)),
            dma((2, shots)),
            dma((2, shots)),
            dma((2,)),
            dma((2,)),
            dma((2, 2)),
            dma((2, 2)),
            dma((3, 2, 4)),
            dma((3, 2, 4)),
            dma((2,)),
            dma((2,)),
            dma((2,)),
            dma((2,)),
            dma((2, chips)),
            dma((2, chips)),
            dma((1,)),
        ],
        compiler_params=pltpu.CompilerParams(
            collective_id=0, has_side_effects=True, vmem_limit_bytes=63 * 2**20
        ),
    )(
        slab_holder,
        snap_step,
        window_end,
        source_cell,
        wavelet,
        receiver_cells,
        residual_data.transpose(1, 0, 2),
        courant,
        snapshot_store.reshape(slabs, 2, size_y, size_z),
        adjoint_prev[0],
        adjoint_now[0],
    )
    return pl.pallas_call(
        finish,
        out_shape=(
            jax.ShapeDtypeStruct((planes, rows // 2 * size_z), F32),
            jax.ShapeDtypeStruct((1, planes, size_y, size_z), F32),
        ),
        in_specs=[vmem, hbm],
        out_specs=(vmem, hbm),
        scratch_shapes=[dma((1,))],
        compiler_params=pltpu.CompilerParams(vmem_limit_bytes=63 * 2**20),
    )(image, adjoint)


def solution(mesh):
    in_specs = (
        P("space", None, None),
        P("shot", None, "space", None, None),
        P(),
        P("shot"),
        P("shot"),
        P("shot"),
        P(),
        P("shot", None),
        P("shot", None, None),
        P("shot", "space", None, None),
        P("shot", "space", None, None),
    )
    out_specs = (P("space", "shot"), P("shot", "space", None, None))
    return jax.shard_map(
        functools.partial(local, mesh.shape["shot"], mesh.shape["space"]),
        mesh=mesh,
        in_specs=in_specs,
        out_specs=out_specs,
        check_vma=False,
    )
```

```python
import functools

import jax
import jax.numpy as jnp
from jax import lax
from jax.experimental import pallas as pl
from jax.experimental.pallas import tpu as pltpu
from jax.sharding import PartitionSpec as P

FWD = 8
ADJ = 3
HALO = 4
CAP = 2
SCALE = 5040.0
TAPS = (8064.0, -1008.0, 128.0, -9.0)
CENTRE_Z = -43008.0
CENTRE_Y = -42.0
CODE_BITS = 13.0
SCALE_ROWS = 16
MESH = pl.DeviceIdType.MESH
F32 = jnp.float32
BF16 = jnp.bfloat16


def band(size, block, centre):
    row = lax.broadcasted_iota(jnp.int32, (size, size), 0)
    col = lax.broadcasted_iota(jnp.int32, (size, size), 1)
    gap = jnp.abs(row - col)
    result = jnp.where(gap == 0, centre, 0.0)
    for offset, tap in enumerate(TAPS, 1):
        result = jnp.where(gap == offset, tap, result)
    if block < size:
        result = jnp.where(row // block == col // block, result, 0.0)
    return result.astype(BF16)


def split(value):
    high = value.astype(BF16)
    return high, (value - high.astype(F32)).astype(BF16)


def encode(value):
    rows = value.shape[0] * value.shape[1]
    flat = value.reshape(rows, value.shape[2])
    top = jnp.max(jnp.abs(flat), axis=0, keepdims=True)
    power = jnp.floor(jnp.log2(jnp.maximum(top, 1e-30)))
    code = jnp.round(flat * jnp.exp2(CODE_BITS - power)).astype(jnp.int32).astype(jnp.int16)
    scale = jnp.broadcast_to(power.astype(jnp.int32), (SCALE_ROWS, value.shape[2])).astype(jnp.int16)
    return code, scale


def decode(code, scale, shape):
    power = scale.astype(jnp.int32).astype(F32)[:1]
    return (code.astype(jnp.int32).astype(F32) * jnp.exp2(power - CODE_BITS)).reshape(shape)


def kernel(
    shots,
    spaces,
    cap,
    holder,
    snap_step,
    window_end,
    source_cell,
    wavelet,
    cells,
    residual,
    courant_in,
    store_in,
    prev_in,
    now_in,
    image_out,
    adjoint_out,
    courant,
    store,
    adj,
    field,
    wave,
    adj_code,
    adj_land,
    wave_code,
    wave_land,
    packed,
    landed_old,
    landed_new,
    band_z,
    band_y,
    spot,
    col_hot,
    sums,
    image,
    split_image,
    from_core,
    to_chip,
    from_chip,
    sent_slots,
    own_slots,
    local_sem,
    fetch_send,
    fetch_recv,
    courant_send,
    courant_recv,
    adj_send,
    adj_recv,
    wave_send,
    wave_recv,
    core_send,
    core_recv,
    chip_send,
    chip_recv,
    out_sem,
):
    me = lax.axis_index("shot")
    place = lax.axis_index("space")
    slabs, _, size_y, size_z = store.shape
    planes = courant.shape[0] - 2 * HALO
    has_low = place > 0
    has_high = place < spaces - 1
    has_side = (has_low, has_high)
    core = lax.rem(me, 2)
    chip = lax.div(me, 2)
    chips = shots // 2
    partner = chip * 2 + 1 - core
    chunk = HALO
    chunks = planes // chunk
    deep = 2 * HALO
    edges = (0, chunks - 1)
    inner = tuple(range(1, chunks - 1))

    landed = (landed_old, landed_new)

    def peer(shot):
        return (shot, place)

    own_planes = pl.ds(HALO, planes)
    loads = [
        pltpu.make_async_copy(now_in, adj.at[1], local_sem.at[0]),
        pltpu.make_async_copy(courant_in, courant.at[own_planes], local_sem.at[1]),
        pltpu.make_async_copy(store_in, store, local_sem.at[2]),
        pltpu.make_async_copy(prev_in, adj.at[0], local_sem.at[3]),
    ]
    for load in loads:
        load.start()

    barrier = pltpu.get_barrier_semaphore()

    def greet(turn, carry):
        other = lax.rem(me + turn, shots)
        pl.semaphore_signal(barrier, inc=1, device_id=peer(other), device_id_type=MESH)
        return carry

    for side in range(2):

        @pl.when(has_side[side])
        def _():
            pl.semaphore_signal(
                barrier, inc=1, device_id=(me, place + 2 * side - 1), device_id_type=MESH
            )

    lax.fori_loop(1, shots, greet, 0)

    def find_sent(other):
        found = jnp.int32(0)
        spots = [jnp.int32(0)] * cap
        for slab in range(slabs):
            slot = holder[other, slab]
            mine = lax.div(slot, slabs) == me
            where = lax.rem(slot, slabs)
            for rank in range(cap):
                spots[rank] = jnp.where(jnp.logical_and(mine, found == rank), where, spots[rank])
            found = found + jnp.where(mine, 1, 0)
        for rank in range(cap):
            sent_slots[other * cap + rank] = spots[rank]

    def find_own(slab, carry):
        storer = lax.div(holder[me, slab], slabs)
        rank = jnp.int32(0)
        for before in range(slabs):
            same = jnp.logical_and(lax.div(holder[me, before], slabs) == storer, before < slab)
            rank = rank + jnp.where(same, 1, 0)
        own_slots[slab] = storer * cap + rank
        return carry

    halo_rows = HALO * size_y
    edge_shape = (HALO, size_y, size_z)

    def pick(turn, values):
        result = jnp.int32(values[0])
        for at, value in enumerate(values[1:], 1):
            result = jnp.where(turn == at, value, result)
        return result

    def neighbour(side):
        other = place + 2 * side - 1
        return other, jnp.logical_and(other >= 0, other < spaces)

    def remote(source, target, send, recv, side):
        return pltpu.make_async_remote_copy(
            src_ref=source,
            dst_ref=target,
            send_sem=send,
            recv_sem=recv,
            device_id=(me, place + 2 * side - 1),
            device_id_type=MESH,
        )

    def adj_copy(slot, side):
        return remote(
            adj_code.at[slot, side],
            adj_land.at[slot, side],
            adj_send.at[slot, side],
            adj_recv.at[slot, side],
            side,
        )

    def adj_start(index, slot, side):
        @pl.when(neighbour(side)[1])
        def _():
            numbers, scale = encode(field[slot, pl.ds(HALO + chunk * index, chunk)])
            adj_code[slot, side, :halo_rows] = numbers
            adj_code[slot, side, halo_rows:] = scale
            adj_copy(slot, side).start()

    def adj_wait(slot, side):
        @pl.when(neighbour(side)[1])
        def _():
            adj_copy(slot, side).wait_send()
            adj_copy(slot, 1 - side).wait_recv()
            field[slot, pl.ds((HALO + planes) * side, HALO)] = decode(
                adj_land[slot, 1 - side, :halo_rows], adj_land[slot, 1 - side, halo_rows:], edge_shape
            )

    def wave_copy(slot, side, piece):
        return remote(
            wave_code.at[slot, side, piece],
            wave_land.at[slot, side, piece],
            wave_send.at[slot, side, piece],
            wave_recv.at[slot, side, piece],
            side,
        )

    def wave_start(level, slot, side, piece):
        index = piece + side * (chunks - 1 - 2 * piece)

        @pl.when(neighbour(side)[1])
        def _():
            numbers, scale = encode(wave[level, pl.ds(deep + chunk * index, chunk)])
            wave_code[slot, side, piece, :halo_rows] = numbers
            wave_code[slot, side, piece, halo_rows:] = scale
            wave_copy(slot, side, piece).start()

    def wave_wait(level, slot, side, piece):
        index = -1 - piece + side * (chunks + 1 + 2 * piece)

        @pl.when(neighbour(side)[1])
        def _():
            wave_copy(slot, side, piece).wait_send()
            wave_copy(slot, 1 - side, piece).wait_recv()
            wave[level, pl.ds(deep + chunk * index, chunk)] = decode(
                wave_land[slot, 1 - side, piece, :halo_rows],
                wave_land[slot, 1 - side, piece, halo_rows:],
                edge_shape,
            )

    def courant_copy(side):
        return remote(
            courant_in.at[pl.ds((planes - HALO) * side, HALO)],
            courant.at[pl.ds((planes + HALO) * (1 - side), HALO)],
            courant_send.at[side],
            courant_recv.at[side],
            side,
        )

    def flat_part(ref, slot, first):
        middle = ref[slot, pl.ds(first, chunk)]
        high, low = split(middle.reshape(chunk * size_y, size_z))
        right = band_z[...]
        left = band_y[...]
        total = jnp.dot(high, right, preferred_element_type=F32)
        total += jnp.dot(low, right, preferred_element_type=F32)
        total += jnp.dot(left, high, preferred_element_type=F32)
        total += jnp.dot(left, low, preferred_element_type=F32)
        return total

    def deep_part(ref, slot, at, width):
        total = None
        for offset, tap in enumerate(TAPS, 1):
            term = tap * (ref[slot, pl.ds(at + offset, width)] + ref[slot, pl.ds(at - offset, width)])
            total = term if total is None else total + term
        return total

    order = (0, chunks - 1) + inner

    def first_field(turn, carry):
        index = pick(turn, order)
        part = pl.ds(HALO + chunk * index, chunk)
        scaled = courant[part] * (1.0 / SCALE)
        courant[part] = scaled
        field[0, part] = scaled * adj[1, pl.ds(chunk * index, chunk)]

        @pl.when(turn < 2)
        def _():
            adj_start(index, 0, turn)

        return carry

    loads[0].wait()
    loads[1].wait()
    low_count = jnp.where(has_low, 1, 0)
    high_count = jnp.where(has_high, 1, 0)
    pl.semaphore_wait(barrier, shots - 1 + low_count + high_count)
    lax.fori_loop(0, chunks, first_field, 0)

    def fetch_copy(level, other):
        return pltpu.make_async_remote_copy(
            src_ref=packed.at[level, pl.ds(other * cap, cap)],
            dst_ref=landed[level].at[pl.ds(me * cap, cap)],
            send_sem=fetch_send.at[level, other],
            recv_sem=fetch_recv.at[level, me],
            device_id=peer(other),
            device_id_type=MESH,
        )

    def fetch_arrival(level, other):
        return pltpu.make_async_remote_copy(
            src_ref=packed.at[level, pl.ds(other * cap, cap)],
            dst_ref=landed[level].at[pl.ds(other * cap, cap)],
            send_sem=fetch_send.at[level, other],
            recv_sem=fetch_recv.at[level, other],
            device_id=peer(other),
            device_id_type=MESH,
        )

    loads[2].wait()
    for level in (1, 0):

        def pack(turn, carry):
            other = lax.rem(me + turn, shots)
            if level == 1:
                find_sent(other)
            for rank in range(cap):
                packed[level, other * cap + rank] = store[sent_slots[other * cap + rank], level]

            @pl.when(turn < shots)
            def _():
                fetch_copy(level, other).start()

            return carry

        lax.fori_loop(1, shots + 1, pack, 0)

    def keep(rank, carry):
        for level in (1, 0):
            landed[level][me * cap + rank] = packed[level, me * cap + rank]
        return carry

    lax.fori_loop(0, cap, keep, 0)

    for side in range(2):

        @pl.when(has_side[side])
        def _():
            courant_copy(side).start()

    band_z[...] = band(size_z, size_z, CENTRE_Z)
    band_y[...] = band(chunk * size_y, size_y, CENTRE_Y)
    for side in range(2):

        @pl.when(jnp.logical_not(has_side[side]))
        def _():
            nothing = jnp.zeros((HALO, size_y, size_z), F32)
            courant[pl.ds((planes + HALO) * side, HALO)] = nothing
            for slot in range(2):
                field[slot, pl.ds((planes + HALO) * side, HALO)] = nothing
                for piece in range(2):
                    wave[slot, pl.ds((planes + deep) * side + HALO * piece, HALO)] = nothing

    lax.fori_loop(0, slabs, find_own, 0)

    plane_cells = size_y * size_z
    source = source_cell[0]
    source_plane = lax.div(source, plane_cells) - place * planes
    in_plane = lax.rem(source, plane_cells)
    flat = lax.broadcasted_iota(jnp.int32, (size_y, size_z), 0) * size_z + lax.broadcasted_iota(
        jnp.int32, (size_y, size_z), 1
    )
    spot[...] = jnp.where(flat == in_plane, 1.0, 0.0)

    recv_cells = cells[...]
    recv_row = recv_cells // size_z - place * (planes * size_y)
    recv_col = recv_cells % size_z
    count = recv_cells.shape[1]
    col_hot[...] = jnp.where(
        lax.broadcasted_iota(jnp.int32, (size_z, count), 0) == recv_col, 1.0, 0.0
    ).astype(BF16)

    loads[3].wait()

    pair = 2

    def adjoint_step(turn, carry):
        slot = lax.rem(turn, 2)
        data_high, data_low = split(residual[turn])
        data_high = data_high.astype(F32)
        data_low = data_low.astype(F32)

        def task(number, carry):
            index = pick(number, order)

            @pl.when(number < 2)
            def _():
                adj_wait(slot, number)

            hot = col_hot[...]
            row = lax.broadcasted_iota(jnp.int32, (chunk * size_y, count), 0) + (
                chunk * size_y * index
            )
            hit = row == recv_row
            total = flat_part(field, slot, HALO + chunk * index)
            for data in (data_high, data_low):
                total += lax.dot_general(
                    jnp.where(hit, data, 0.0).astype(BF16),
                    hot,
                    (((1,), (1,)), ((), ())),
                    preferred_element_type=F32,
                )
            sums[...] = total.reshape(chunk, size_y, size_z)

            def some(part, carry):
                plane = chunk * index + pair * part
                here = pl.ds(plane, pair)
                padded = pl.ds(HALO + plane, pair)
                total = sums[pl.ds(pair * part, pair)] + deep_part(
                    field, slot, HALO + plane, pair
                )
                current = adj[turn + 1, here]
                following = (current + current) - adj[turn, here] + total
                adj[turn + 2, here] = following
                field[1 - slot, padded] = courant[padded] * following
                return carry

            lax.fori_loop(0, chunk // pair, some, 0)

            @pl.when(jnp.logical_and(number < 2, turn < ADJ - 1))
            def _():
                adj_start(index, 1 - slot, number)

            return carry

        lax.fori_loop(0, chunks, task, 0)
        return carry

    lax.fori_loop(0, ADJ - 1, adjoint_step, 0)

    def arrive(level):
        def one(turn, carry):
            fetch_arrival(level, lax.rem(me + turn, shots)).wait_recv()
            return carry

        lax.fori_loop(1, shots, one, 0)

    arrive(1)

    def unpack(slab, carry):
        wave[0, deep + slab] = landed_new[own_slots[slab]].astype(F32)
        wave[1, deep + slab] = jnp.zeros((size_y, size_z), F32)
        image[slab] = jnp.zeros((size_y, size_z), F32)
        return carry

    lax.fori_loop(0, slabs, unpack, 0)

    def first_edges(side, carry):
        wave_start(0, 0, side, 0)
        return carry

    lax.fori_loop(0, 2, first_edges, 0)

    steps = window_end[0] - snap_step[0]
    start = snap_step[0]

    def image_term(level, turn, plane, width):
        behind = steps - turn
        weight = jnp.where(jnp.logical_and(behind >= 0, behind < ADJ), 1.0, 0.0)
        state = adj[1 + jnp.clip(behind, 0, ADJ - 1), pl.ds(plane, width)]
        return (weight * state) * wave[level, pl.ds(deep + plane, width)]

    def advance(level, turn, index):
        first = deep + chunk * index
        sums[...] = flat_part(wave, level, first).reshape(chunk, size_y, size_z)
        amplitude = wavelet[start + turn]

        def some(part, carry):
            at = first + pair * part
            here = pl.ds(at, pair)
            middle = wave[level, here]
            total = sums[pl.ds(pair * part, pair)] + deep_part(wave, level, at, pair)
            total = courant[pl.ds(at - HALO, pair)] * total
            total = total + (middle + middle) - wave[1 - level, here]
            pattern = spot[...]
            for plane in range(pair):
                push = jnp.where(source_plane == at - deep + plane, amplitude, 0.0)
                wave[1 - level, at + plane] = total[plane] + push * pattern
            return carry

        lax.fori_loop(0, chunk // pair, some, 0)

    rows = size_y // chips
    row_half = rows // 2

    def cut_image(piece, place_in, index):
        def some(part, carry):
            plane = chunk * index + pair * part
            value = image[pl.ds(plane, pair)] + image_term(0, FWD, plane, pair)
            into = pl.ds(chunk * place_in + pair * part, pair)
            for target in range(chips):
                for side in range(2):
                    low = target * rows + side * row_half
                    split_image[side, piece, target, into] = value[:, low : low + row_half]
            return carry

        lax.fori_loop(0, chunk // pair, some, 0)

    def core_copy(piece):
        return pltpu.make_async_remote_copy(
            src_ref=split_image.at[1 - core, piece],
            dst_ref=from_core.at[piece],
            send_sem=core_send.at[piece],
            recv_sem=core_recv.at[piece],
            device_id=peer(partner),
            device_id_type=MESH,
        )

    def chip_copy(piece, target, landing):
        return pltpu.make_async_remote_copy(
            src_ref=to_chip.at[piece, target],
            dst_ref=from_chip.at[piece, landing],
            send_sem=chip_send.at[piece, target],
            recv_sem=chip_recv.at[piece, landing],
            device_id=peer(target * 2 + core),
            device_id_type=MESH,
        )

    def to_chips(piece):
        core_copy(piece).wait()

        def one(turn, carry):
            target = lax.rem(chip + turn, chips)
            to_chip[piece, target] = split_image[core, piece, target] + from_core[piece, target]
            chip_copy(piece, target, chip).start()
            return carry

        lax.fori_loop(1, chips, one, 0)
        to_chip[piece, chip] = split_image[core, piece, chip] + from_core[piece, chip]

    stages = 2 + (FWD - 2) // 2

    def stage(number, carry):
        opening = number == 0
        closing = number == stages - 1
        level = jnp.where(opening, 0, 1)
        turn = jnp.where(opening, 0, 2 * number - 1)
        slot = lax.rem(number, 2)

        @pl.when(number > 0)
        def _():
            def add_terms(part, carry):
                plane = pair * part
                image[pl.ds(plane, pair)] = (
                    image[pl.ds(plane, pair)]
                    + image_term(1, turn, plane, pair)
                    + image_term(0, turn - 1, plane, pair)
                )
                return carry

            lax.fori_loop(0, planes // pair, add_terms, 0)

        def task(at, carry):
            index = pick(at, (1, 2, 0, 3, -1, 0, 1, 4, 3, 2))
            second = pick(at, (0, 0, 0, 0, 0, 1, 1, 0, 1, 1))
            side = pick(at, (0, 0, 0, 1, 0, 0, 0, 1, 1, 1))
            piece = pick(at, (0, 0, 0, 0, 1, 0, 1, 1, 0, 1))
            waits = pick(at, (0, 0, 1, 1, 1, 0, 0, 1, 0, 0))

            @pl.when(waits == 1)
            def _():
                wave_wait(level, slot, side, piece)

            source = jnp.where(second == 1, 1 - level, level)
            advance(source, turn + second, index)

            @pl.when(
                jnp.logical_and(second == 1, jnp.logical_or(piece == 0, number < stages - 2))
            )
            def _():
                wave_start(1, 1 - slot, side, piece)

            @pl.when(closing)
            def _():
                cut_image(jnp.where(at < 2, 0, 1), lax.rem(at, 2), index)

            @pl.when(jnp.logical_and(closing, at == 1))
            def _():
                core_copy(0).start()

            @pl.when(jnp.logical_and(closing, at == 2))
            def _():
                to_chips(0)

            return carry

        single = jnp.logical_or(opening, closing)
        lax.fori_loop(0, jnp.where(single, 4, 10), task, 0)

        @pl.when(opening)
        def _():
            arrive(0)

            def less(slab, carry):
                here = deep + slab
                wave[1, here] = wave[1, here] - landed_old[own_slots[slab]].astype(F32)
                return carry

            lax.fori_loop(0, slabs, less, 0)

            def edge(at, carry):
                wave_start(1, 1, lax.rem(at, 2), lax.div(at, 2))
                return carry

            lax.fori_loop(0, 4, edge, 0)
            adjoint_step(ADJ - 1, 0)
            pltpu.make_async_copy(adj.at[ADJ + 1], adjoint_out, out_sem.at[0]).start()
            for side in range(2):

                @pl.when(has_side[side])
                def _():
                    courant_copy(side).wait_send()
                    courant_copy(1 - side).wait_recv()
                    part = pl.ds((planes + HALO) * side, HALO)
                    courant[part] = courant[part] * (1.0 / SCALE)

        return carry

    lax.fori_loop(0, stages, stage, 0)
    core_copy(1).start()
    to_chips(1)

    for piece in range(2):

        def add(turn, carry):
            other = lax.rem(chip + turn, chips)
            chip_copy(piece, other, other).wait_recv()
            chip_copy(piece, other, chip).wait_send()
            to_chip[piece, chip] = to_chip[piece, chip] + from_chip[piece, other]
            return carry

        lax.fori_loop(1, chips, add, 0)
        total = to_chip[piece, chip]
        for at, index in enumerate((inner, edges)[piece]):
            image_out[pl.ds(chunk * index, chunk)] = total[chunk * at : chunk * (at + 1)]

    def drain(turn, carry):
        other = lax.rem(me + turn, shots)
        for level in (1, 0):
            fetch_copy(level, other).wait_send()
        return carry

    lax.fori_loop(1, shots, drain, 0)
    pltpu.make_async_copy(adj.at[ADJ + 1], adjoint_out, out_sem.at[0]).wait()


def finish(image, adjoint, image_out, adjoint_out, sem):
    copy = pltpu.make_async_copy(adjoint, adjoint_out.at[0], sem.at[0])
    copy.start()
    size_z = image.shape[2]
    for row in range(image.shape[1]):
        image_out[:, row * size_z : (row + 1) * size_z] = image[:, row] * (1.0 / ADJ)
    copy.wait()


def local(
    shots,
    spaces,
    courant,
    snapshot_store,
    slab_holder,
    snap_step,
    window_end,
    source_cell,
    wavelet,
    receiver_cells,
    residual_data,
    adjoint_prev,
    adjoint_now,
):
    planes, size_y, size_z = courant.shape
    slabs = snapshot_store.shape[0]
    cap = CAP
    chips = shots // 2
    rows = size_y // chips
    smem = pl.BlockSpec(memory_space=pltpu.SMEM)
    vmem = pl.BlockSpec(memory_space=pltpu.VMEM)
    hbm = pl.BlockSpec(memory_space=pltpu.HBM)
    half = planes // 2
    coded = (HALO * size_y + SCALE_ROWS, size_z)
    dma = pltpu.SemaphoreType.DMA
    image, adjoint = pl.pallas_call(
        functools.partial(kernel, shots, spaces, cap),
        out_shape=(
            jax.ShapeDtypeStruct((planes, rows // 2, size_z), F32),
            jax.ShapeDtypeStruct((planes, size_y, size_z), F32),
        ),
        in_specs=[smem] * 5 + [vmem] * 2 + [hbm] * 4,
        out_specs=(vmem, hbm),
        scratch_shapes=[
            pltpu.VMEM((planes + 2 * HALO, size_y, size_z), F32),
            pltpu.VMEM((slabs, 2, size_y, size_z), BF16),
            pltpu.VMEM((ADJ + 2, planes, size_y, size_z), F32),
            pltpu.VMEM((2, planes + 2 * HALO, size_y, size_z), F32),
            pltpu.VMEM((2, planes + 4 * HALO, size_y, size_z), F32),
            pltpu.VMEM((2, 2) + coded, jnp.int16),
            pltpu.VMEM((2, 2) + coded, jnp.int16),
            pltpu.VMEM((2, 2, 2) + coded, jnp.int16),
            pltpu.VMEM((2, 2, 2) + coded, jnp.int16),
            pltpu.VMEM((2, shots * cap, size_y, size_z), BF16),
            pltpu.VMEM((shots * cap, size_y, size_z), BF16),
            pltpu.VMEM((shots * cap, size_y, size_z), BF16),
            pltpu.VMEM((size_z, size_z), BF16),
            pltpu.VMEM((HALO * size_y, HALO * size_y), BF16),
            pltpu.VMEM((size_y, size_z), F32),
            pltpu.VMEM((size_z, receiver_cells.shape[1]), BF16),
            pltpu.VMEM((HALO, size_y, size_z), F32),
            pltpu.VMEM((planes, size_y, size_z), F32),
            pltpu.VMEM((2, 2, chips, half, rows // 2, size_z), F32),
            pltpu.VMEM((2, chips, half, rows // 2, size_z), F32),
            pltpu.VMEM((2, chips, half, rows // 2, size_z), F32),
            pltpu.VMEM((2, chips, half, rows // 2, size_z), F32),
            pltpu.SMEM((shots * cap,), jnp.int32),
            pltpu.SMEM((slabs,), jnp.int32),
            dma((4,)),
            dma((2, shots)),
            dma((2, shots)),
            dma((2,)),
            dma((2,)),
            dma((2, 2)),
            dma((2, 2)),
            dma((2, 2, 2)),
            dma((2, 2, 2)),
            dma((2,)),
            dma((2,)),
            dma((2, chips)),
            dma((2, chips)),
            dma((1,)),
        ],
        compiler_params=pltpu.CompilerParams(
            collective_id=0, has_side_effects=True, vmem_limit_bytes=63 * 2**20
        ),
    )(
        slab_holder,
        snap_step,
        window_end,
        source_cell,
        wavelet,
        receiver_cells,
        residual_data.transpose(1, 0, 2),
        courant,
        snapshot_store.reshape(slabs, 2, size_y, size_z),
        adjoint_prev[0],
        adjoint_now[0],
    )
    return pl.pallas_call(
        finish,
        out_shape=(
            jax.ShapeDtypeStruct((planes, rows // 2 * size_z), F32),
            jax.ShapeDtypeStruct((1, planes, size_y, size_z), F32),
        ),
        in_specs=[vmem, hbm],
        out_specs=(vmem, hbm),
        scratch_shapes=[dma((1,))],
        compiler_params=pltpu.CompilerParams(vmem_limit_bytes=63 * 2**20),
    )(image, adjoint)


def solution(mesh):
    in_specs = (
        P("space", None, None),
        P("shot", None, "space", None, None),
        P(),
        P("shot"),
        P("shot"),
        P("shot"),
        P(),
        P("shot", None),
        P("shot", None, None),
        P("shot", "space", None, None),
        P("shot", "space", None, None),
    )
    out_specs = (P("space", "shot"), P("shot", "space", None, None))
    return jax.shard_map(
        functools.partial(local, mesh.shape["shot"], mesh.shape["space"]),
        mesh=mesh,
        in_specs=in_specs,
        out_specs=out_specs,
        check_vma=False,
    )
```

```python
import functools

import jax
import jax.numpy as jnp
from jax import lax
from jax.experimental import pallas as pl
from jax.experimental.pallas import tpu as pltpu
from jax.sharding import PartitionSpec as P

FWD = 8
ADJ = 3
HALO = 4
CAP = 2
SCALE = 5040.0
TAPS = (8064.0, -1008.0, 128.0, -9.0)
CENTRE_Z = -43008.0
CENTRE_Y = -42.0
CODE_BITS = 13.0
SCALE_ROWS = 16
MESH = pl.DeviceIdType.MESH
F32 = jnp.float32
BF16 = jnp.bfloat16


def band(size, block, centre):
    row = lax.broadcasted_iota(jnp.int32, (size, size), 0)
    col = lax.broadcasted_iota(jnp.int32, (size, size), 1)
    gap = jnp.abs(row - col)
    result = jnp.where(gap == 0, centre, 0.0)
    for offset, tap in enumerate(TAPS, 1):
        result = jnp.where(gap == offset, tap, result)
    if block < size:
        result = jnp.where(row // block == col // block, result, 0.0)
    return result.astype(BF16)


def split(value):
    high = value.astype(BF16)
    return high, (value - high.astype(F32)).astype(BF16)


def encode(value):
    rows = value.shape[0] * value.shape[1]
    flat = value.reshape(rows, value.shape[2])
    top = jnp.max(jnp.abs(flat), axis=0, keepdims=True)
    power = jnp.floor(jnp.log2(jnp.maximum(top, 1e-30)))
    code = jnp.round(flat * jnp.exp2(CODE_BITS - power)).astype(jnp.int32).astype(jnp.int16)
    scale = jnp.broadcast_to(power.astype(jnp.int32), (SCALE_ROWS, value.shape[2])).astype(jnp.int16)
    return code, scale


def decode(code, scale, shape):
    power = scale.astype(jnp.int32).astype(F32)[:1]
    return (code.astype(jnp.int32).astype(F32) * jnp.exp2(power - CODE_BITS)).reshape(shape)


def kernel(
    shots,
    spaces,
    cap,
    holder,
    snap_step,
    window_end,
    source_cell,
    wavelet,
    cells,
    residual,
    courant_in,
    store_in,
    prev_in,
    now_in,
    image_out,
    adjoint_out,
    courant,
    store,
    adj,
    field,
    wave,
    adj_code,
    adj_land,
    wave_code,
    wave_land,
    packed,
    landed_old,
    landed_new,
    band_z,
    band_y,
    spot,
    col_hot,
    image,
    split_image,
    from_core,
    to_chip,
    from_chip,
    sent_slots,
    own_slots,
    local_sem,
    fetch_send,
    fetch_recv,
    courant_send,
    courant_recv,
    adj_send,
    adj_recv,
    wave_send,
    wave_recv,
    core_send,
    core_recv,
    chip_send,
    chip_recv,
    out_sem,
):
    me = lax.axis_index("shot")
    place = lax.axis_index("space")
    slabs, _, size_y, size_z = store.shape
    planes = courant.shape[0] - 2 * HALO
    has_low = place > 0
    has_high = place < spaces - 1
    has_side = (has_low, has_high)
    core = lax.rem(me, 2)
    chip = lax.div(me, 2)
    chips = shots // 2
    partner = chip * 2 + 1 - core
    chunk = HALO
    chunks = planes // chunk
    deep = 2 * HALO
    edges = (0, chunks - 1)
    inner = tuple(range(1, chunks - 1))

    landed = (landed_old, landed_new)

    def peer(shot):
        return (shot, place)

    own_planes = pl.ds(HALO, planes)
    loads = [
        pltpu.make_async_copy(now_in, adj.at[1], local_sem.at[0]),
        pltpu.make_async_copy(courant_in, courant.at[own_planes], local_sem.at[1]),
        pltpu.make_async_copy(store_in, store, local_sem.at[2]),
        pltpu.make_async_copy(prev_in, adj.at[0], local_sem.at[3]),
    ]
    for load in loads:
        load.start()

    barrier = pltpu.get_barrier_semaphore()

    def greet(turn, carry):
        other = lax.rem(me + turn, shots)
        pl.semaphore_signal(barrier, inc=1, device_id=peer(other), device_id_type=MESH)
        return carry

    for side in range(2):

        @pl.when(has_side[side])
        def _():
            pl.semaphore_signal(
                barrier, inc=1, device_id=(me, place + 2 * side - 1), device_id_type=MESH
            )

    lax.fori_loop(1, shots, greet, 0)

    def find_sent(other):
        found = jnp.int32(0)
        spots = [jnp.int32(0)] * cap
        for slab in range(slabs):
            slot = holder[other, slab]
            mine = lax.div(slot, slabs) == me
            where = lax.rem(slot, slabs)
            for rank in range(cap):
                spots[rank] = jnp.where(jnp.logical_and(mine, found == rank), where, spots[rank])
            found = found + jnp.where(mine, 1, 0)
        for rank in range(cap):
            sent_slots[other * cap + rank] = spots[rank]

    def find_own(slab, carry):
        storer = lax.div(holder[me, slab], slabs)
        rank = jnp.int32(0)
        for before in range(slabs):
            same = jnp.logical_and(lax.div(holder[me, before], slabs) == storer, before < slab)
            rank = rank + jnp.where(same, 1, 0)
        own_slots[slab] = storer * cap + rank
        return carry

    halo_rows = HALO * size_y
    edge_shape = (HALO, size_y, size_z)

    def pick(turn, values):
        result = jnp.int32(values[0])
        for at, value in enumerate(values[1:], 1):
            result = jnp.where(turn == at, value, result)
        return result

    def neighbour(side):
        other = place + 2 * side - 1
        return other, jnp.logical_and(other >= 0, other < spaces)

    def remote(source, target, send, recv, side):
        return pltpu.make_async_remote_copy(
            src_ref=source,
            dst_ref=target,
            send_sem=send,
            recv_sem=recv,
            device_id=(me, place + 2 * side - 1),
            device_id_type=MESH,
        )

    def adj_copy(slot, side):
        return remote(
            adj_code.at[slot, side],
            adj_land.at[slot, side],
            adj_send.at[slot, side],
            adj_recv.at[slot, side],
            side,
        )

    def adj_start(index, slot, side):
        @pl.when(neighbour(side)[1])
        def _():
            numbers, scale = encode(field[slot, pl.ds(HALO + chunk * index, chunk)])
            adj_code[slot, side, :halo_rows] = numbers
            adj_code[slot, side, halo_rows:] = scale
            adj_copy(slot, side).start()

    def adj_wait(slot, side):
        @pl.when(neighbour(side)[1])
        def _():
            adj_copy(slot, side).wait_send()
            adj_copy(slot, 1 - side).wait_recv()
            field[slot, pl.ds((HALO + planes) * side, HALO)] = decode(
                adj_land[slot, 1 - side, :halo_rows], adj_land[slot, 1 - side, halo_rows:], edge_shape
            )

    def wave_copy(slot, side, piece):
        return remote(
            wave_code.at[slot, side, piece],
            wave_land.at[slot, side, piece],
            wave_send.at[slot, side, piece],
            wave_recv.at[slot, side, piece],
            side,
        )

    def wave_start(level, slot, side, piece):
        index = piece + side * (chunks - 1 - 2 * piece)

        @pl.when(neighbour(side)[1])
        def _():
            numbers, scale = encode(wave[level, pl.ds(deep + chunk * index, chunk)])
            wave_code[slot, side, piece, :halo_rows] = numbers
            wave_code[slot, side, piece, halo_rows:] = scale
            wave_copy(slot, side, piece).start()

    def wave_wait(level, slot, side, piece):
        index = -1 - piece + side * (chunks + 1 + 2 * piece)

        @pl.when(neighbour(side)[1])
        def _():
            wave_copy(slot, side, piece).wait_send()
            wave_copy(slot, 1 - side, piece).wait_recv()
            wave[level, pl.ds(deep + chunk * index, chunk)] = decode(
                wave_land[slot, 1 - side, piece, :halo_rows],
                wave_land[slot, 1 - side, piece, halo_rows:],
                edge_shape,
            )

    def courant_copy(side):
        return remote(
            courant_in.at[pl.ds((planes - HALO) * side, HALO)],
            courant.at[pl.ds((planes + HALO) * (1 - side), HALO)],
            courant_send.at[side],
            courant_recv.at[side],
            side,
        )

    def stencil(ref, slot, first):
        middle = ref[slot, pl.ds(first, chunk)]
        high, low = split(middle.reshape(chunk * size_y, size_z))
        right = band_z[...]
        left = band_y[...]
        total = jnp.dot(high, right, preferred_element_type=F32)
        total += jnp.dot(low, right, preferred_element_type=F32)
        total += jnp.dot(left, high, preferred_element_type=F32)
        total += jnp.dot(left, low, preferred_element_type=F32)
        total = total.reshape(chunk, size_y, size_z)
        for offset, tap in enumerate(TAPS, 1):
            total += tap * (
                ref[slot, pl.ds(first + offset, chunk)] + ref[slot, pl.ds(first - offset, chunk)]
            )
        return total

    order = (0, chunks - 1) + inner

    def first_field(turn, carry):
        index = pick(turn, order)
        part = pl.ds(HALO + chunk * index, chunk)
        scaled = courant[part] * (1.0 / SCALE)
        courant[part] = scaled
        field[0, part] = scaled * adj[1, pl.ds(chunk * index, chunk)]

        @pl.when(turn < 2)
        def _():
            adj_start(index, 0, turn)

        return carry

    loads[0].wait()
    loads[1].wait()
    low_count = jnp.where(has_low, 1, 0)
    high_count = jnp.where(has_high, 1, 0)
    pl.semaphore_wait(barrier, shots - 1 + low_count + high_count)
    lax.fori_loop(0, chunks, first_field, 0)

    def fetch_copy(level, other):
        return pltpu.make_async_remote_copy(
            src_ref=packed.at[level, pl.ds(other * cap, cap)],
            dst_ref=landed[level].at[pl.ds(me * cap, cap)],
            send_sem=fetch_send.at[level, other],
            recv_sem=fetch_recv.at[level, me],
            device_id=peer(other),
            device_id_type=MESH,
        )

    def fetch_arrival(level, other):
        return pltpu.make_async_remote_copy(
            src_ref=packed.at[level, pl.ds(other * cap, cap)],
            dst_ref=landed[level].at[pl.ds(other * cap, cap)],
            send_sem=fetch_send.at[level, other],
            recv_sem=fetch_recv.at[level, other],
            device_id=peer(other),
            device_id_type=MESH,
        )

    loads[2].wait()
    for level in (1, 0):

        def pack(turn, carry):
            other = lax.rem(me + turn, shots)
            if level == 1:
                find_sent(other)
            for rank in range(cap):
                packed[level, other * cap + rank] = store[sent_slots[other * cap + rank], level]

            @pl.when(turn < shots)
            def _():
                fetch_copy(level, other).start()

            return carry

        lax.fori_loop(1, shots + 1, pack, 0)

    def keep(rank, carry):
        for level in (1, 0):
            landed[level][me * cap + rank] = packed[level, me * cap + rank]
        return carry

    lax.fori_loop(0, cap, keep, 0)

    for side in range(2):

        @pl.when(has_side[side])
        def _():
            courant_copy(side).start()

    band_z[...] = band(size_z, size_z, CENTRE_Z)
    band_y[...] = band(chunk * size_y, size_y, CENTRE_Y)
    for side in range(2):

        @pl.when(jnp.logical_not(has_side[side]))
        def _():
            nothing = jnp.zeros((HALO, size_y, size_z), F32)
            courant[pl.ds((planes + HALO) * side, HALO)] = nothing
            for slot in range(2):
                field[slot, pl.ds((planes + HALO) * side, HALO)] = nothing
                for piece in range(2):
                    wave[slot, pl.ds((planes + deep) * side + HALO * piece, HALO)] = nothing

    lax.fori_loop(0, slabs, find_own, 0)

    plane_cells = size_y * size_z
    source = source_cell[0]
    source_plane = lax.div(source, plane_cells) - place * planes
    in_plane = lax.rem(source, plane_cells)
    flat = lax.broadcasted_iota(jnp.int32, (size_y, size_z), 0) * size_z + lax.broadcasted_iota(
        jnp.int32, (size_y, size_z), 1
    )
    spot[...] = jnp.where(flat == in_plane, 1.0, 0.0)

    recv_cells = cells[...]
    recv_row = recv_cells // size_z - place * (planes * size_y)
    recv_col = recv_cells % size_z
    count = recv_cells.shape[1]
    col_hot[...] = jnp.where(
        lax.broadcasted_iota(jnp.int32, (size_z, count), 0) == recv_col, 1.0, 0.0
    ).astype(BF16)

    loads[3].wait()

    pair = 2

    def adjoint_step(turn, carry):
        slot = lax.rem(turn, 2)
        data_high, data_low = split(residual[turn])
        data_high = data_high.astype(F32)
        data_low = data_low.astype(F32)

        def work(index):
            hot = col_hot[...]
            row = lax.broadcasted_iota(jnp.int32, (chunk * size_y, count), 0) + (
                chunk * size_y * index
            )
            hit = row == recv_row
            total = jnp.zeros((chunk * size_y, size_z), F32)
            for data in (data_high, data_low):
                total += lax.dot_general(
                    jnp.where(hit, data, 0.0).astype(BF16),
                    hot,
                    (((1,), (1,)), ((), ())),
                    preferred_element_type=F32,
                )
            total = total.reshape(chunk, size_y, size_z)
            total = total + stencil(field, slot, HALO + chunk * index)
            here = pl.ds(chunk * index, chunk)
            padded = pl.ds(HALO + chunk * index, chunk)
            current = adj[turn + 1, here]
            following = (current + current) - adj[turn, here] + total
            adj[turn + 2, here] = following
            field[1 - slot, padded] = courant[padded] * following

        def task(side, carry):
            adj_wait(slot, side)
            index = (chunks - 1) * side
            work(index)

            @pl.when(turn < ADJ - 1)
            def _():
                adj_start(index, 1 - slot, side)

            return carry

        lax.fori_loop(0, 2, task, 0)
        for index in inner:
            work(index)
        return carry

    def arrive(level):
        def one(turn, carry):
            fetch_arrival(level, lax.rem(me + turn, shots)).wait_recv()
            return carry

        lax.fori_loop(1, shots, one, 0)

    def unpack(slab, carry):
        wave[0, deep + slab] = landed_new[own_slots[slab]].astype(F32)
        wave[1, deep + slab] = jnp.zeros((size_y, size_z), F32)
        image[slab] = jnp.zeros((size_y, size_z), F32)
        return carry

    def first_edges(side, carry):
        wave_start(0, 0, side, 0)
        return carry

    def early(turn, carry):
        adjoint_step(turn, 0)

        @pl.when(turn == 0)
        def _():
            arrive(1)
            lax.fori_loop(0, slabs, unpack, 0)
            lax.fori_loop(0, 2, first_edges, 0)

        return carry

    lax.fori_loop(0, ADJ - 1, early, 0)

    steps = window_end[0] - snap_step[0]
    start = snap_step[0]

    def image_term(level, turn, plane, width):
        behind = steps - turn
        weight = jnp.where(jnp.logical_and(behind >= 0, behind < ADJ), 1.0, 0.0)
        state = adj[1 + jnp.clip(behind, 0, ADJ - 1), pl.ds(plane, width)]
        return (weight * state) * wave[level, pl.ds(deep + plane, width)]

    def advance(level, turn, index):
        first = deep + chunk * index
        here = pl.ds(first, chunk)
        middle = wave[level, here]
        total = courant[pl.ds(first - HALO, chunk)] * stencil(wave, level, first)
        total = total + (middle + middle) - wave[1 - level, here]
        amplitude = wavelet[start + turn]
        pattern = spot[...]
        for plane in range(chunk):
            push = jnp.where(source_plane == chunk * index + plane, amplitude, 0.0)
            wave[1 - level, first + plane] = total[plane] + push * pattern

    rows = size_y // chips
    row_half = rows // 2

    def cut_image(piece, place_in, index):
        def some(part, carry):
            plane = chunk * index + pair * part
            value = image[pl.ds(plane, pair)] + image_term(0, FWD, plane, pair)
            into = pl.ds(chunk * place_in + pair * part, pair)
            for target in range(chips):
                for side in range(2):
                    low = target * rows + side * row_half
                    split_image[side, piece, target, into] = value[:, low : low + row_half]
            return carry

        lax.fori_loop(0, chunk // pair, some, 0)

    def core_copy(piece):
        return pltpu.make_async_remote_copy(
            src_ref=split_image.at[1 - core, piece],
            dst_ref=from_core.at[piece],
            send_sem=core_send.at[piece],
            recv_sem=core_recv.at[piece],
            device_id=peer(partner),
            device_id_type=MESH,
        )

    def chip_copy(piece, target, landing):
        return pltpu.make_async_remote_copy(
            src_ref=to_chip.at[piece, target],
            dst_ref=from_chip.at[piece, landing],
            send_sem=chip_send.at[piece, target],
            recv_sem=chip_recv.at[piece, landing],
            device_id=peer(target * 2 + core),
            device_id_type=MESH,
        )

    def to_chips(piece):
        core_copy(piece).wait()

        def one(turn, carry):
            target = lax.rem(chip + turn, chips)
            to_chip[piece, target] = split_image[core, piece, target] + from_core[piece, target]
            chip_copy(piece, target, chip).start()
            return carry

        lax.fori_loop(1, chips, one, 0)
        to_chip[piece, chip] = split_image[core, piece, chip] + from_core[piece, chip]

    stages = 2 + (FWD - 2) // 2

    def stage(number, carry):
        opening = number == 0
        closing = number == stages - 1
        level = jnp.where(opening, 0, 1)
        turn = jnp.where(opening, 0, 2 * number - 1)
        slot = lax.rem(number, 2)

        @pl.when(number > 0)
        def _():
            def add_terms(part, carry):
                plane = pair * part
                image[pl.ds(plane, pair)] = (
                    image[pl.ds(plane, pair)]
                    + image_term(1, turn, plane, pair)
                    + image_term(0, turn - 1, plane, pair)
                )
                return carry

            lax.fori_loop(0, planes // pair, add_terms, 0)

        for index in inner:
            advance(level, turn, index)

        @pl.when(closing)
        def _():
            def one(at, carry):
                cut_image(0, at, 1 + at)
                return carry

            lax.fori_loop(0, len(inner), one, 0)
            core_copy(0).start()

        def task(at, carry):
            index = pick(at, (0, 3, -1, 0, 1, 4, 3, 2))
            second = pick(at, (0, 0, 0, 1, 1, 0, 1, 1))
            side = pick(at, (0, 1, 0, 0, 0, 1, 1, 1))
            piece = pick(at, (0, 0, 1, 0, 1, 1, 0, 1))
            waits = pick(at, (1, 1, 1, 0, 0, 1, 0, 0))

            @pl.when(waits == 1)
            def _():
                wave_wait(level, slot, side, piece)

            source = jnp.where(second == 1, 1 - level, level)
            advance(source, turn + second, index)

            @pl.when(
                jnp.logical_and(second == 1, jnp.logical_or(piece == 0, number < stages - 2))
            )
            def _():
                wave_start(1, 1 - slot, side, piece)

            @pl.when(closing)
            def _():
                cut_image(1, at, index)

            @pl.when(jnp.logical_and(closing, at == 0))
            def _():
                to_chips(0)

            return carry

        single = jnp.logical_or(opening, closing)
        lax.fori_loop(0, jnp.where(single, 2, 8), task, 0)

        @pl.when(opening)
        def _():
            arrive(0)

            def less(slab, carry):
                here = deep + slab
                wave[1, here] = wave[1, here] - landed_old[own_slots[slab]].astype(F32)
                return carry

            lax.fori_loop(0, slabs, less, 0)

            def edge(at, carry):
                wave_start(1, 1, lax.rem(at, 2), lax.div(at, 2))
                return carry

            lax.fori_loop(0, 4, edge, 0)
            adjoint_step(ADJ - 1, 0)
            pltpu.make_async_copy(adj.at[ADJ + 1], adjoint_out, out_sem.at[0]).start()
            for side in range(2):

                @pl.when(has_side[side])
                def _():
                    courant_copy(side).wait_send()
                    courant_copy(1 - side).wait_recv()
                    part = pl.ds((planes + HALO) * side, HALO)
                    courant[part] = courant[part] * (1.0 / SCALE)

        return carry

    lax.fori_loop(0, stages, stage, 0)
    core_copy(1).start()
    to_chips(1)

    for piece in range(2):

        def add(turn, carry):
            other = lax.rem(chip + turn, chips)
            chip_copy(piece, other, other).wait_recv()
            chip_copy(piece, other, chip).wait_send()
            to_chip[piece, chip] = to_chip[piece, chip] + from_chip[piece, other]
            return carry

        lax.fori_loop(1, chips, add, 0)
        total = to_chip[piece, chip]
        for at, index in enumerate((inner, edges)[piece]):
            image_out[pl.ds(chunk * index, chunk)] = total[chunk * at : chunk * (at + 1)]

    def drain(turn, carry):
        other = lax.rem(me + turn, shots)
        for level in (1, 0):
            fetch_copy(level, other).wait_send()
        return carry

    lax.fori_loop(1, shots, drain, 0)
    pltpu.make_async_copy(adj.at[ADJ + 1], adjoint_out, out_sem.at[0]).wait()


def finish(image, adjoint, image_out, adjoint_out):
    size_z = image.shape[2]
    for row in range(image.shape[1]):
        image_out[:, row * size_z : (row + 1) * size_z] = image[:, row] * (1.0 / ADJ)

    def one(plane, carry):
        adjoint_out[0, plane] = adjoint[plane]
        return carry

    lax.fori_loop(0, adjoint.shape[0], one, 0)


def local(
    shots,
    spaces,
    courant,
    snapshot_store,
    slab_holder,
    snap_step,
    window_end,
    source_cell,
    wavelet,
    receiver_cells,
    residual_data,
    adjoint_prev,
    adjoint_now,
):
    planes, size_y, size_z = courant.shape
    slabs = snapshot_store.shape[0]
    cap = CAP
    chips = shots // 2
    rows = size_y // chips
    smem = pl.BlockSpec(memory_space=pltpu.SMEM)
    vmem = pl.BlockSpec(memory_space=pltpu.VMEM)
    hbm = pl.BlockSpec(memory_space=pltpu.HBM)
    half = planes // 2
    coded = (HALO * size_y + SCALE_ROWS, size_z)
    dma = pltpu.SemaphoreType.DMA
    image, adjoint = pl.pallas_call(
        functools.partial(kernel, shots, spaces, cap),
        out_shape=(
            jax.ShapeDtypeStruct((planes, rows // 2, size_z), F32),
            jax.ShapeDtypeStruct((planes, size_y, size_z), F32),
        ),
        in_specs=[smem] * 5 + [vmem] * 2 + [hbm] * 4,
        out_specs=(vmem, hbm),
        scratch_shapes=[
            pltpu.VMEM((planes + 2 * HALO, size_y, size_z), F32),
            pltpu.VMEM((slabs, 2, size_y, size_z), BF16),
            pltpu.VMEM((ADJ + 2, planes, size_y, size_z), F32),
            pltpu.VMEM((2, planes + 2 * HALO, size_y, size_z), F32),
            pltpu.VMEM((2, planes + 4 * HALO, size_y, size_z), F32),
            pltpu.VMEM((2, 2) + coded, jnp.int16),
            pltpu.VMEM((2, 2) + coded, jnp.int16),
            pltpu.VMEM((2, 2, 2) + coded, jnp.int16),
            pltpu.VMEM((2, 2, 2) + coded, jnp.int16),
            pltpu.VMEM((2, shots * cap, size_y, size_z), BF16),
            pltpu.VMEM((shots * cap, size_y, size_z), BF16),
            pltpu.VMEM((shots * cap, size_y, size_z), BF16),
            pltpu.VMEM((size_z, size_z), BF16),
            pltpu.VMEM((HALO * size_y, HALO * size_y), BF16),
            pltpu.VMEM((size_y, size_z), F32),
            pltpu.VMEM((size_z, receiver_cells.shape[1]), BF16),
            pltpu.VMEM((planes, size_y, size_z), F32),
            pltpu.VMEM((2, 2, chips, half, rows // 2, size_z), F32),
            pltpu.VMEM((2, chips, half, rows // 2, size_z), F32),
            pltpu.VMEM((2, chips, half, rows // 2, size_z), F32),
            pltpu.VMEM((2, chips, half, rows // 2, size_z), F32),
            pltpu.SMEM((shots * cap,), jnp.int32),
            pltpu.SMEM((slabs,), jnp.int32),
            dma((4,)),
            dma((2, shots)),
            dma((2, shots)),
            dma((2,)),
            dma((2,)),
            dma((2, 2)),
            dma((2, 2)),
            dma((2, 2, 2)),
            dma((2, 2, 2)),
            dma((2,)),
            dma((2,)),
            dma((2, chips)),
            dma((2, chips)),
            dma((1,)),
        ],
        compiler_params=pltpu.CompilerParams(
            collective_id=0, has_side_effects=True, vmem_limit_bytes=63 * 2**20
        ),
    )(
        slab_holder,
        snap_step,
        window_end,
        source_cell,
        wavelet,
        receiver_cells,
        residual_data.transpose(1, 0, 2),
        courant,
        snapshot_store.reshape(slabs, 2, size_y, size_z),
        adjoint_prev[0],
        adjoint_now[0],
    )
    return pl.pallas_call(
        finish,
        out_shape=(
            jax.ShapeDtypeStruct((planes, rows // 2 * size_z), F32),
            jax.ShapeDtypeStruct((1, planes, size_y, size_z), F32),
        ),
        in_specs=[vmem, vmem],
        out_specs=(vmem, vmem),
        compiler_params=pltpu.CompilerParams(vmem_limit_bytes=16 * 2**20),
    )(image, adjoint)


def solution(mesh):
    in_specs = (
        P("space", None, None),
        P("shot", None, "space", None, None),
        P(),
        P("shot"),
        P("shot"),
        P("shot"),
        P(),
        P("shot", None),
        P("shot", None, None),
        P("shot", "space", None, None),
        P("shot", "space", None, None),
    )
    out_specs = (P("space", "shot"), P("shot", "space", None, None))
    return jax.shard_map(
        functools.partial(local, mesh.shape["shot"], mesh.shape["space"]),
        mesh=mesh,
        in_specs=in_specs,
        out_specs=out_specs,
        check_vma=False,
    )
```

```python
import functools

import jax
import jax.numpy as jnp
from jax import lax
from jax.experimental import pallas as pl
from jax.experimental.pallas import tpu as pltpu
from jax.sharding import PartitionSpec as P

FWD = 8
ADJ = 3
HALO = 4
CAP = 2
SCALE = 5040.0
TAPS = (8064.0, -1008.0, 128.0, -9.0)
CENTRE_Z = -43008.0
CENTRE_Y = -42.0
CODE_BITS = 13.0
SCALE_ROWS = 16
MESH = pl.DeviceIdType.MESH
F32 = jnp.float32
BF16 = jnp.bfloat16


def band(size, block, centre):
    row = lax.broadcasted_iota(jnp.int32, (size, size), 0)
    col = lax.broadcasted_iota(jnp.int32, (size, size), 1)
    gap = jnp.abs(row - col)
    result = jnp.where(gap == 0, centre, 0.0)
    for offset, tap in enumerate(TAPS, 1):
        result = jnp.where(gap == offset, tap, result)
    if block < size:
        result = jnp.where(row // block == col // block, result, 0.0)
    return result.astype(BF16)


def split(value):
    high = value.astype(BF16)
    return high, (value - high.astype(F32)).astype(BF16)


def encode(value):
    rows = value.shape[0] * value.shape[1]
    flat = value.reshape(rows, value.shape[2])
    top = jnp.max(jnp.abs(flat), axis=0, keepdims=True)
    power = jnp.floor(jnp.log2(jnp.maximum(top, 1e-30)))
    code = jnp.round(flat * jnp.exp2(CODE_BITS - power)).astype(jnp.int32).astype(jnp.int16)
    scale = jnp.broadcast_to(power.astype(jnp.int32), (SCALE_ROWS, value.shape[2])).astype(jnp.int16)
    return code, scale


def decode(code, scale, shape):
    power = scale.astype(jnp.int32).astype(F32)[:1]
    return (code.astype(jnp.int32).astype(F32) * jnp.exp2(power - CODE_BITS)).reshape(shape)


def kernel(
    shots,
    spaces,
    cap,
    holder,
    snap_step,
    window_end,
    source_cell,
    wavelet,
    cells,
    residual,
    courant_in,
    store_in,
    prev_in,
    now_in,
    image_out,
    adjoint_out,
    courant,
    store,
    adj,
    field,
    wave,
    adj_code,
    adj_land,
    wave_code,
    wave_land,
    packed,
    landed_old,
    landed_new,
    band_z,
    band_y,
    spot,
    col_hot,
    image,
    split_image,
    from_core,
    to_chip,
    from_chip,
    sent_slots,
    own_slots,
    local_sem,
    fetch_send,
    fetch_recv,
    courant_send,
    courant_recv,
    adj_send,
    adj_recv,
    wave_send,
    wave_recv,
    core_send,
    core_recv,
    chip_send,
    chip_recv,
    out_sem,
):
    me = lax.axis_index("shot")
    place = lax.axis_index("space")
    slabs, _, size_y, size_z = store.shape
    planes = courant.shape[0] - 2 * HALO
    has_low = place > 0
    has_high = place < spaces - 1
    has_side = (has_low, has_high)
    core = lax.rem(me, 2)
    chip = lax.div(me, 2)
    chips = shots // 2
    partner = chip * 2 + 1 - core
    chunk = HALO
    chunks = planes // chunk
    deep = 2 * HALO
    edges = (0, chunks - 1)
    inner = tuple(range(1, chunks - 1))

    landed = (landed_old, landed_new)

    def peer(shot):
        return (shot, place)

    own_planes = pl.ds(HALO, planes)
    loads = [
        pltpu.make_async_copy(now_in, adj.at[1], local_sem.at[0]),
        pltpu.make_async_copy(courant_in, courant.at[own_planes], local_sem.at[1]),
        pltpu.make_async_copy(store_in, store, local_sem.at[2]),
        pltpu.make_async_copy(prev_in, adj.at[0], local_sem.at[3]),
    ]
    for load in loads:
        load.start()

    barrier = pltpu.get_barrier_semaphore()

    def greet(turn, carry):
        other = lax.rem(me + turn, shots)
        pl.semaphore_signal(barrier, inc=1, device_id=peer(other), device_id_type=MESH)
        return carry

    for side in range(2):

        @pl.when(has_side[side])
        def _():
            pl.semaphore_signal(
                barrier, inc=1, device_id=(me, place + 2 * side - 1), device_id_type=MESH
            )

    lax.fori_loop(1, shots, greet, 0)

    def find_sent(other):
        found = jnp.int32(0)
        spots = [jnp.int32(0)] * cap
        for slab in range(slabs):
            slot = holder[other, slab]
            mine = lax.div(slot, slabs) == me
            where = lax.rem(slot, slabs)
            for rank in range(cap):
                spots[rank] = jnp.where(jnp.logical_and(mine, found == rank), where, spots[rank])
            found = found + jnp.where(mine, 1, 0)
        for rank in range(cap):
            sent_slots[other * cap + rank] = spots[rank]

    def find_own(slab, carry):
        storer = lax.div(holder[me, slab], slabs)
        rank = jnp.int32(0)
        for before in range(slabs):
            same = jnp.logical_and(lax.div(holder[me, before], slabs) == storer, before < slab)
            rank = rank + jnp.where(same, 1, 0)
        own_slots[slab] = storer * cap + rank
        return carry

    halo_rows = HALO * size_y
    edge_shape = (HALO, size_y, size_z)

    def pick(turn, values):
        result = jnp.int32(values[0])
        for at, value in enumerate(values[1:], 1):
            result = jnp.where(turn == at, value, result)
        return result

    def neighbour(side):
        other = place + 2 * side - 1
        return other, jnp.logical_and(other >= 0, other < spaces)

    def remote(source, target, send, recv, side):
        return pltpu.make_async_remote_copy(
            src_ref=source,
            dst_ref=target,
            send_sem=send,
            recv_sem=recv,
            device_id=(me, place + 2 * side - 1),
            device_id_type=MESH,
        )

    def adj_copy(slot, side):
        return remote(
            adj_code.at[slot, side],
            adj_land.at[slot, side],
            adj_send.at[slot, side],
            adj_recv.at[slot, side],
            side,
        )

    def adj_start(index, slot, side):
        @pl.when(neighbour(side)[1])
        def _():
            numbers, scale = encode(field[slot, pl.ds(HALO + chunk * index, chunk)])
            adj_code[slot, side, :halo_rows] = numbers
            adj_code[slot, side, halo_rows:] = scale
            adj_copy(slot, side).start()

    def adj_wait(slot, side):
        @pl.when(neighbour(side)[1])
        def _():
            adj_copy(slot, side).wait_send()
            adj_copy(slot, 1 - side).wait_recv()
            field[slot, pl.ds((HALO + planes) * side, HALO)] = decode(
                adj_land[slot, 1 - side, :halo_rows], adj_land[slot, 1 - side, halo_rows:], edge_shape
            )

    def wave_copy(slot, side, piece):
        return remote(
            wave_code.at[slot, side, piece],
            wave_land.at[slot, side, piece],
            wave_send.at[slot, side, piece],
            wave_recv.at[slot, side, piece],
            side,
        )

    def wave_start(level, slot, side, piece):
        index = piece + side * (chunks - 1 - 2 * piece)

        @pl.when(neighbour(side)[1])
        def _():
            numbers, scale = encode(wave[level, pl.ds(deep + chunk * index, chunk)])
            wave_code[slot, side, piece, :halo_rows] = numbers
            wave_code[slot, side, piece, halo_rows:] = scale
            wave_copy(slot, side, piece).start()

    def wave_wait(level, slot, side, piece):
        index = -1 - piece + side * (chunks + 1 + 2 * piece)

        @pl.when(neighbour(side)[1])
        def _():
            wave_copy(slot, side, piece).wait_send()
            wave_copy(slot, 1 - side, piece).wait_recv()
            wave[level, pl.ds(deep + chunk * index, chunk)] = decode(
                wave_land[slot, 1 - side, piece, :halo_rows],
                wave_land[slot, 1 - side, piece, halo_rows:],
                edge_shape,
            )

    def courant_copy(side):
        return remote(
            courant_in.at[pl.ds((planes - HALO) * side, HALO)],
            courant.at[pl.ds((planes + HALO) * (1 - side), HALO)],
            courant_send.at[side],
            courant_recv.at[side],
            side,
        )

    def stencil(ref, slot, first):
        middle = ref[slot, pl.ds(first, chunk)]
        high, low = split(middle.reshape(chunk * size_y, size_z))
        right = band_z[...]
        left = band_y[...]
        total = jnp.dot(high, right, preferred_element_type=F32)
        total += jnp.dot(low, right, preferred_element_type=F32)
        total += jnp.dot(left, high, preferred_element_type=F32)
        total += jnp.dot(left, low, preferred_element_type=F32)
        total = total.reshape(chunk, size_y, size_z)
        for offset, tap in enumerate(TAPS, 1):
            total += tap * (
                ref[slot, pl.ds(first + offset, chunk)] + ref[slot, pl.ds(first - offset, chunk)]
            )
        return total

    order = (0, chunks - 1) + inner

    def first_field(turn, carry):
        index = pick(turn, order)
        part = pl.ds(HALO + chunk * index, chunk)
        scaled = courant[part] * (1.0 / SCALE)
        courant[part] = scaled
        field[0, part] = scaled * adj[1, pl.ds(chunk * index, chunk)]

        @pl.when(turn < 2)
        def _():
            adj_start(index, 0, turn)

        return carry

    loads[0].wait()
    loads[1].wait()
    low_count = jnp.where(has_low, 1, 0)
    high_count = jnp.where(has_high, 1, 0)
    pl.semaphore_wait(barrier, shots - 1 + low_count + high_count)
    lax.fori_loop(0, chunks, first_field, 0)

    def fetch_copy(level, other):
        return pltpu.make_async_remote_copy(
            src_ref=packed.at[level, pl.ds(other * cap, cap)],
            dst_ref=landed[level].at[pl.ds(me * cap, cap)],
            send_sem=fetch_send.at[level, other],
            recv_sem=fetch_recv.at[level, me],
            device_id=peer(other),
            device_id_type=MESH,
        )

    def fetch_arrival(level, other):
        return pltpu.make_async_remote_copy(
            src_ref=packed.at[level, pl.ds(other * cap, cap)],
            dst_ref=landed[level].at[pl.ds(other * cap, cap)],
            send_sem=fetch_send.at[level, other],
            recv_sem=fetch_recv.at[level, other],
            device_id=peer(other),
            device_id_type=MESH,
        )

    loads[2].wait()
    for level in (1, 0):

        def pack(turn, carry):
            other = lax.rem(me + turn, shots)
            if level == 1:
                find_sent(other)
            for rank in range(cap):
                packed[level, other * cap + rank] = store[sent_slots[other * cap + rank], level]

            @pl.when(turn < shots)
            def _():
                fetch_copy(level, other).start()

            return carry

        lax.fori_loop(1, shots + 1, pack, 0)

    def keep(rank, carry):
        for level in (1, 0):
            landed[level][me * cap + rank] = packed[level, me * cap + rank]
        return carry

    lax.fori_loop(0, cap, keep, 0)

    for side in range(2):

        @pl.when(has_side[side])
        def _():
            courant_copy(side).start()

    band_z[...] = band(size_z, size_z, CENTRE_Z)
    band_y[...] = band(chunk * size_y, size_y, CENTRE_Y)
    for side in range(2):

        @pl.when(jnp.logical_not(has_side[side]))
        def _():
            nothing = jnp.zeros((HALO, size_y, size_z), F32)
            courant[pl.ds((planes + HALO) * side, HALO)] = nothing
            for slot in range(2):
                field[slot, pl.ds((planes + HALO) * side, HALO)] = nothing
                for piece in range(2):
                    wave[slot, pl.ds((planes + deep) * side + HALO * piece, HALO)] = nothing

    lax.fori_loop(0, slabs, find_own, 0)

    plane_cells = size_y * size_z
    source = source_cell[0]
    source_plane = lax.div(source, plane_cells) - place * planes
    in_plane = lax.rem(source, plane_cells)
    flat = lax.broadcasted_iota(jnp.int32, (size_y, size_z), 0) * size_z + lax.broadcasted_iota(
        jnp.int32, (size_y, size_z), 1
    )
    spot[...] = jnp.where(flat == in_plane, 1.0, 0.0)

    recv_cells = cells[...]
    recv_row = recv_cells // size_z - place * (planes * size_y)
    recv_col = recv_cells % size_z
    count = recv_cells.shape[1]
    col_hot[...] = jnp.where(
        lax.broadcasted_iota(jnp.int32, (size_z, count), 0) == recv_col, 1.0, 0.0
    ).astype(BF16)

    loads[3].wait()

    pair = 4

    def adjoint_step(turn, carry):
        slot = lax.rem(turn, 2)
        data_high, data_low = split(residual[turn])
        data_high = data_high.astype(F32)
        data_low = data_low.astype(F32)

        def work(index):
            hot = col_hot[...]
            row = lax.broadcasted_iota(jnp.int32, (chunk * size_y, count), 0) + (
                chunk * size_y * index
            )
            hit = row == recv_row
            total = jnp.zeros((chunk * size_y, size_z), F32)
            for data in (data_high, data_low):
                total += lax.dot_general(
                    jnp.where(hit, data, 0.0).astype(BF16),
                    hot,
                    (((1,), (1,)), ((), ())),
                    preferred_element_type=F32,
                )
            total = total.reshape(chunk, size_y, size_z)
            total = total + stencil(field, slot, HALO + chunk * index)
            here = pl.ds(chunk * index, chunk)
            padded = pl.ds(HALO + chunk * index, chunk)
            current = adj[turn + 1, here]
            following = (current + current) - adj[turn, here] + total
            adj[turn + 2, here] = following
            field[1 - slot, padded] = courant[padded] * following

        def task(side, carry):
            adj_wait(slot, side)
            index = (chunks - 1) * side
            work(index)

            @pl.when(turn < ADJ - 1)
            def _():
                adj_start(index, 1 - slot, side)

            return carry

        lax.fori_loop(0, 2, task, 0)
        for index in inner:
            work(index)
        return carry

    def arrive(level):
        def one(turn, carry):
            fetch_arrival(level, lax.rem(me + turn, shots)).wait_recv()
            return carry

        lax.fori_loop(1, shots, one, 0)

    def unpack(slab, carry):
        wave[0, deep + slab] = landed_new[own_slots[slab]].astype(F32)
        wave[1, deep + slab] = jnp.zeros((size_y, size_z), F32)
        image[slab] = jnp.zeros((size_y, size_z), F32)
        return carry

    def first_edges(side, carry):
        wave_start(0, 0, side, 0)
        return carry

    lax.fori_loop(0, ADJ - 1, adjoint_step, 0)
    arrive(1)
    lax.fori_loop(0, slabs, unpack, 0)
    lax.fori_loop(0, 2, first_edges, 0)

    steps = window_end[0] - snap_step[0]
    start = snap_step[0]

    def image_term(level, turn, plane, width):
        behind = steps - turn
        weight = jnp.where(jnp.logical_and(behind >= 0, behind < ADJ), 1.0, 0.0)
        state = adj[1 + jnp.clip(behind, 0, ADJ - 1), pl.ds(plane, width)]
        return (weight * state) * wave[level, pl.ds(deep + plane, width)]

    def advance(level, turn, index):
        first = deep + chunk * index
        here = pl.ds(first, chunk)
        middle = wave[level, here]
        total = courant[pl.ds(first - HALO, chunk)] * stencil(wave, level, first)
        total = total + (middle + middle) - wave[1 - level, here]
        amplitude = wavelet[start + turn]
        pattern = spot[...]
        for plane in range(chunk):
            push = jnp.where(source_plane == chunk * index + plane, amplitude, 0.0)
            wave[1 - level, first + plane] = total[plane] + push * pattern

    rows = size_y // chips
    row_half = rows // 2

    def cut_image(piece, place_in, index):
        def some(part, carry):
            plane = chunk * index + pair * part
            value = image[pl.ds(plane, pair)] + image_term(0, FWD, plane, pair)
            into = pl.ds(chunk * place_in + pair * part, pair)
            for target in range(chips):
                for side in range(2):
                    low = target * rows + side * row_half
                    split_image[side, piece, target, into] = value[:, low : low + row_half]
            return carry

        lax.fori_loop(0, chunk // pair, some, 0)

    def core_copy(piece):
        return pltpu.make_async_remote_copy(
            src_ref=split_image.at[1 - core, piece],
            dst_ref=from_core.at[piece],
            send_sem=core_send.at[piece],
            recv_sem=core_recv.at[piece],
            device_id=peer(partner),
            device_id_type=MESH,
        )

    def chip_copy(piece, target, landing):
        return pltpu.make_async_remote_copy(
            src_ref=to_chip.at[piece, target],
            dst_ref=from_chip.at[piece, landing],
            send_sem=chip_send.at[piece, target],
            recv_sem=chip_recv.at[piece, landing],
            device_id=peer(target * 2 + core),
            device_id_type=MESH,
        )

    def to_chips(piece):
        core_copy(piece).wait()

        def one(turn, carry):
            target = lax.rem(chip + turn, chips)
            to_chip[piece, target] = split_image[core, piece, target] + from_core[piece, target]
            chip_copy(piece, target, chip).start()
            return carry

        lax.fori_loop(1, chips, one, 0)
        to_chip[piece, chip] = split_image[core, piece, chip] + from_core[piece, chip]

    stages = 2 + (FWD - 2) // 2

    def stage(number, carry):
        opening = number == 0
        closing = number == stages - 1
        level = jnp.where(opening, 0, 1)
        turn = jnp.where(opening, 0, 2 * number - 1)
        slot = lax.rem(number, 2)

        @pl.when(number > 0)
        def _():
            def add_terms(part, carry):
                plane = pair * part
                image[pl.ds(plane, pair)] = (
                    image[pl.ds(plane, pair)]
                    + image_term(1, turn, plane, pair)
                    + image_term(0, turn - 1, plane, pair)
                )
                return carry

            lax.fori_loop(0, planes // pair, add_terms, 0)

        for index in inner:
            advance(level, turn, index)

        @pl.when(closing)
        def _():
            def one(at, carry):
                cut_image(0, at, 1 + at)
                return carry

            lax.fori_loop(0, len(inner), one, 0)
            core_copy(0).start()

        def task(at, carry):
            index = pick(at, (0, 3, -1, 0, 1, 4, 3, 2))
            second = pick(at, (0, 0, 0, 1, 1, 0, 1, 1))
            side = pick(at, (0, 1, 0, 0, 0, 1, 1, 1))
            piece = pick(at, (0, 0, 1, 0, 1, 1, 0, 1))
            waits = pick(at, (1, 1, 1, 0, 0, 1, 0, 0))

            @pl.when(waits == 1)
            def _():
                wave_wait(level, slot, side, piece)

            source = jnp.where(second == 1, 1 - level, level)
            advance(source, turn + second, index)

            @pl.when(
                jnp.logical_and(second == 1, jnp.logical_or(piece == 0, number < stages - 2))
            )
            def _():
                wave_start(1, 1 - slot, side, piece)

            @pl.when(closing)
            def _():
                cut_image(1, at, index)

            @pl.when(jnp.logical_and(closing, at == 0))
            def _():
                to_chips(0)

            return carry

        single = jnp.logical_or(opening, closing)
        lax.fori_loop(0, jnp.where(single, 2, 8), task, 0)

        @pl.when(opening)
        def _():
            arrive(0)

            def less(slab, carry):
                here = deep + slab
                wave[1, here] = wave[1, here] - landed_old[own_slots[slab]].astype(F32)
                return carry

            lax.fori_loop(0, slabs, less, 0)

            def edge(at, carry):
                wave_start(1, 1, lax.rem(at, 2), lax.div(at, 2))
                return carry

            lax.fori_loop(0, 4, edge, 0)
            adjoint_step(ADJ - 1, 0)
            pltpu.make_async_copy(adj.at[ADJ + 1], adjoint_out, out_sem.at[0]).start()
            for side in range(2):

                @pl.when(has_side[side])
                def _():
                    courant_copy(side).wait_send()
                    courant_copy(1 - side).wait_recv()
                    part = pl.ds((planes + HALO) * side, HALO)
                    courant[part] = courant[part] * (1.0 / SCALE)

        return carry

    lax.fori_loop(0, stages, stage, 0)
    core_copy(1).start()
    to_chips(1)

    for piece in range(2):

        def add(turn, carry):
            other = lax.rem(chip + turn, chips)
            chip_copy(piece, other, other).wait_recv()
            chip_copy(piece, other, chip).wait_send()
            to_chip[piece, chip] = to_chip[piece, chip] + from_chip[piece, other]
            return carry

        lax.fori_loop(1, chips, add, 0)
        total = to_chip[piece, chip]
        for at, index in enumerate((inner, edges)[piece]):
            image_out[pl.ds(chunk * index, chunk)] = total[chunk * at : chunk * (at + 1)]

    def drain(turn, carry):
        other = lax.rem(me + turn, shots)
        for level in (1, 0):
            fetch_copy(level, other).wait_send()
        return carry

    lax.fori_loop(1, shots, drain, 0)
    pltpu.make_async_copy(adj.at[ADJ + 1], adjoint_out, out_sem.at[0]).wait()


def finish(image, adjoint, image_out, adjoint_out):
    size_z = image.shape[2]
    for row in range(image.shape[1]):
        image_out[:, row * size_z : (row + 1) * size_z] = image[:, row] * (1.0 / ADJ)

    def one(plane, carry):
        adjoint_out[0, plane] = adjoint[plane]
        return carry

    lax.fori_loop(0, adjoint.shape[0], one, 0)


def local(
    shots,
    spaces,
    courant,
    snapshot_store,
    slab_holder,
    snap_step,
    window_end,
    source_cell,
    wavelet,
    receiver_cells,
    residual_data,
    adjoint_prev,
    adjoint_now,
):
    planes, size_y, size_z = courant.shape
    slabs = snapshot_store.shape[0]
    cap = CAP
    chips = shots // 2
    rows = size_y // chips
    smem = pl.BlockSpec(memory_space=pltpu.SMEM)
    vmem = pl.BlockSpec(memory_space=pltpu.VMEM)
    hbm = pl.BlockSpec(memory_space=pltpu.HBM)
    half = planes // 2
    coded = (HALO * size_y + SCALE_ROWS, size_z)
    dma = pltpu.SemaphoreType.DMA
    image, adjoint = pl.pallas_call(
        functools.partial(kernel, shots, spaces, cap),
        out_shape=(
            jax.ShapeDtypeStruct((planes, rows // 2, size_z), F32),
            jax.ShapeDtypeStruct((planes, size_y, size_z), F32),
        ),
        in_specs=[smem] * 5 + [vmem] * 2 + [hbm] * 4,
        out_specs=(vmem, hbm),
        scratch_shapes=[
            pltpu.VMEM((planes + 2 * HALO, size_y, size_z), F32),
            pltpu.VMEM((slabs, 2, size_y, size_z), BF16),
            pltpu.VMEM((ADJ + 2, planes, size_y, size_z), F32),
            pltpu.VMEM((2, planes + 2 * HALO, size_y, size_z), F32),
            pltpu.VMEM((2, planes + 4 * HALO, size_y, size_z), F32),
            pltpu.VMEM((2, 2) + coded, jnp.int16),
            pltpu.VMEM((2, 2) + coded, jnp.int16),
            pltpu.VMEM((2, 2, 2) + coded, jnp.int16),
            pltpu.VMEM((2, 2, 2) + coded, jnp.int16),
            pltpu.VMEM((2, shots * cap, size_y, size_z), BF16),
            pltpu.VMEM((shots * cap, size_y, size_z), BF16),
            pltpu.VMEM((shots * cap, size_y, size_z), BF16),
            pltpu.VMEM((size_z, size_z), BF16),
            pltpu.VMEM((HALO * size_y, HALO * size_y), BF16),
            pltpu.VMEM((size_y, size_z), F32),
            pltpu.VMEM((size_z, receiver_cells.shape[1]), BF16),
            pltpu.VMEM((planes, size_y, size_z), F32),
            pltpu.VMEM((2, 2, chips, half, rows // 2, size_z), F32),
            pltpu.VMEM((2, chips, half, rows // 2, size_z), F32),
            pltpu.VMEM((2, chips, half, rows // 2, size_z), F32),
            pltpu.VMEM((2, chips, half, rows // 2, size_z), F32),
            pltpu.SMEM((shots * cap,), jnp.int32),
            pltpu.SMEM((slabs,), jnp.int32),
            dma((4,)),
            dma((2, shots)),
            dma((2, shots)),
            dma((2,)),
            dma((2,)),
            dma((2, 2)),
            dma((2, 2)),
            dma((2, 2, 2)),
            dma((2, 2, 2)),
            dma((2,)),
            dma((2,)),
            dma((2, chips)),
            dma((2, chips)),
            dma((1,)),
        ],
        compiler_params=pltpu.CompilerParams(
            collective_id=0, has_side_effects=True, vmem_limit_bytes=63 * 2**20
        ),
    )(
        slab_holder,
        snap_step,
        window_end,
        source_cell,
        wavelet,
        receiver_cells,
        residual_data.transpose(1, 0, 2),
        courant,
        snapshot_store.reshape(slabs, 2, size_y, size_z),
        adjoint_prev[0],
        adjoint_now[0],
    )
    return pl.pallas_call(
        finish,
        out_shape=(
            jax.ShapeDtypeStruct((planes, rows // 2 * size_z), F32),
            jax.ShapeDtypeStruct((1, planes, size_y, size_z), F32),
        ),
        in_specs=[vmem, vmem],
        out_specs=(vmem, vmem),
        compiler_params=pltpu.CompilerParams(vmem_limit_bytes=63 * 2**20),
    )(image, adjoint)


def solution(mesh):
    in_specs = (
        P("space", None, None),
        P("shot", None, "space", None, None),
        P(),
        P("shot"),
        P("shot"),
        P("shot"),
        P(),
        P("shot", None),
        P("shot", None, None),
        P("shot", "space", None, None),
        P("shot", "space", None, None),
    )
    out_specs = (P("space", "shot"), P("shot", "space", None, None))
    return jax.shard_map(
        functools.partial(local, mesh.shape["shot"], mesh.shape["space"]),
        mesh=mesh,
        in_specs=in_specs,
        out_specs=out_specs,
        check_vma=False,
    )
```

```python
import functools

import jax
import jax.numpy as jnp
from jax import lax
from jax.experimental import pallas as pl
from jax.experimental.pallas import tpu as pltpu
from jax.sharding import PartitionSpec as P

FWD = 8
ADJ = 3
HALO = 4
CAP = 2
SCALE = 5040.0
TAPS = (8064.0, -1008.0, 128.0, -9.0)
CENTRE_Z = -43008.0
CENTRE_Y = -42.0
CODE_BITS = 13.0
SCALE_ROWS = 16
MESH = pl.DeviceIdType.MESH
F32 = jnp.float32
BF16 = jnp.bfloat16


def band(size, block, centre):
    row = lax.broadcasted_iota(jnp.int32, (size, size), 0)
    col = lax.broadcasted_iota(jnp.int32, (size, size), 1)
    gap = jnp.abs(row - col)
    result = jnp.where(gap == 0, centre, 0.0)
    for offset, tap in enumerate(TAPS, 1):
        result = jnp.where(gap == offset, tap, result)
    if block < size:
        result = jnp.where(row // block == col // block, result, 0.0)
    return result.astype(BF16)


def split(value):
    high = value.astype(BF16)
    return high, (value - high.astype(F32)).astype(BF16)


def encode(value):
    rows = value.shape[0] * value.shape[1]
    flat = value.reshape(rows, value.shape[2])
    top = jnp.max(jnp.abs(flat), axis=0, keepdims=True)
    power = jnp.floor(jnp.log2(jnp.maximum(top, 1e-30)))
    code = jnp.round(flat * jnp.exp2(CODE_BITS - power)).astype(jnp.int32).astype(jnp.int16)
    scale = jnp.broadcast_to(power.astype(jnp.int32), (SCALE_ROWS, value.shape[2])).astype(jnp.int16)
    return code, scale


def decode(code, scale, shape):
    power = scale.astype(jnp.int32).astype(F32)[:1]
    return (code.astype(jnp.int32).astype(F32) * jnp.exp2(power - CODE_BITS)).reshape(shape)


def kernel(
    shots,
    spaces,
    cap,
    holder,
    snap_step,
    window_end,
    source_cell,
    wavelet,
    cells,
    residual,
    courant_in,
    store_in,
    prev_in,
    now_in,
    image_out,
    adjoint_out,
    courant,
    store,
    adj,
    field,
    wave,
    adj_code,
    adj_land,
    wave_code,
    wave_land,
    packed,
    landed_old,
    landed_new,
    band_z,
    band_y,
    spot,
    col_hot,
    image,
    split_image,
    from_core,
    to_chip,
    from_chip,
    sent_slots,
    own_slots,
    local_sem,
    fetch_send,
    fetch_recv,
    courant_send,
    courant_recv,
    adj_send,
    adj_recv,
    wave_send,
    wave_recv,
    core_send,
    core_recv,
    chip_send,
    chip_recv,
    out_sem,
):
    me = lax.axis_index("shot")
    place = lax.axis_index("space")
    slabs, _, size_y, size_z = store.shape
    planes = courant.shape[0] - 2 * HALO
    has_low = place > 0
    has_high = place < spaces - 1
    has_side = (has_low, has_high)
    core = lax.rem(me, 2)
    chip = lax.div(me, 2)
    chips = shots // 2
    partner = chip * 2 + 1 - core
    chunk = HALO
    chunks = planes // chunk
    deep = 2 * HALO
    edges = (0, chunks - 1)
    inner = tuple(range(1, chunks - 1))

    landed = (landed_old, landed_new)

    def peer(shot):
        return (shot, place)

    own_planes = pl.ds(HALO, planes)
    loads = [
        pltpu.make_async_copy(now_in, adj.at[1], local_sem.at[0]),
        pltpu.make_async_copy(courant_in, courant.at[own_planes], local_sem.at[1]),
        pltpu.make_async_copy(store_in, store, local_sem.at[2]),
        pltpu.make_async_copy(prev_in, adj.at[0], local_sem.at[3]),
    ]
    for load in loads:
        load.start()

    barrier = pltpu.get_barrier_semaphore()

    def greet(turn, carry):
        other = lax.rem(me + turn, shots)
        pl.semaphore_signal(barrier, inc=1, device_id=peer(other), device_id_type=MESH)
        return carry

    for side in range(2):

        @pl.when(has_side[side])
        def _():
            pl.semaphore_signal(
                barrier, inc=1, device_id=(me, place + 2 * side - 1), device_id_type=MESH
            )

    lax.fori_loop(1, shots, greet, 0)

    def find_sent(other):
        found = jnp.int32(0)
        spots = [jnp.int32(0)] * cap
        for slab in range(slabs):
            slot = holder[other, slab]
            mine = lax.div(slot, slabs) == me
            where = lax.rem(slot, slabs)
            for rank in range(cap):
                spots[rank] = jnp.where(jnp.logical_and(mine, found == rank), where, spots[rank])
            found = found + jnp.where(mine, 1, 0)
        for rank in range(cap):
            sent_slots[other * cap + rank] = spots[rank]

    def find_own(slab, carry):
        storer = lax.div(holder[me, slab], slabs)
        rank = jnp.int32(0)
        for before in range(slabs):
            same = jnp.logical_and(lax.div(holder[me, before], slabs) == storer, before < slab)
            rank = rank + jnp.where(same, 1, 0)
        own_slots[slab] = storer * cap + rank
        return carry

    halo_rows = HALO * size_y
    edge_shape = (HALO, size_y, size_z)

    def pick(turn, values):
        result = jnp.int32(values[0])
        for at, value in enumerate(values[1:], 1):
            result = jnp.where(turn == at, value, result)
        return result

    def neighbour(side):
        other = place + 2 * side - 1
        return other, jnp.logical_and(other >= 0, other < spaces)

    def remote(source, target, send, recv, side):
        return pltpu.make_async_remote_copy(
            src_ref=source,
            dst_ref=target,
            send_sem=send,
            recv_sem=recv,
            device_id=(me, place + 2 * side - 1),
            device_id_type=MESH,
        )

    def adj_copy(slot, side):
        return remote(
            adj_code.at[slot, side],
            adj_land.at[slot, side],
            adj_send.at[slot, side],
            adj_recv.at[slot, side],
            side,
        )

    def adj_start(index, slot, side):
        @pl.when(neighbour(side)[1])
        def _():
            numbers, scale = encode(field[slot, pl.ds(HALO + chunk * index, chunk)])
            adj_code[slot, side, :halo_rows] = numbers
            adj_code[slot, side, halo_rows:] = scale
            adj_copy(slot, side).start()

    def adj_wait(slot, side):
        @pl.when(neighbour(side)[1])
        def _():
            adj_copy(slot, side).wait_send()
            adj_copy(slot, 1 - side).wait_recv()
            field[slot, pl.ds((HALO + planes) * side, HALO)] = decode(
                adj_land[slot, 1 - side, :halo_rows], adj_land[slot, 1 - side, halo_rows:], edge_shape
            )

    def wave_copy(slot, side, piece):
        return remote(
            wave_code.at[slot, side, piece],
            wave_land.at[slot, side, piece],
            wave_send.at[slot, side, piece],
            wave_recv.at[slot, side, piece],
            side,
        )

    def wave_start(level, slot, side, piece):
        index = piece + side * (chunks - 1 - 2 * piece)

        @pl.when(neighbour(side)[1])
        def _():
            numbers, scale = encode(wave[level, pl.ds(deep + chunk * index, chunk)])
            wave_code[slot, side, piece, :halo_rows] = numbers
            wave_code[slot, side, piece, halo_rows:] = scale
            wave_copy(slot, side, piece).start()

    def wave_wait(level, slot, side, piece):
        index = -1 - piece + side * (chunks + 1 + 2 * piece)

        @pl.when(neighbour(side)[1])
        def _():
            wave_copy(slot, side, piece).wait_send()
            wave_copy(slot, 1 - side, piece).wait_recv()
            wave[level, pl.ds(deep + chunk * index, chunk)] = decode(
                wave_land[slot, 1 - side, piece, :halo_rows],
                wave_land[slot, 1 - side, piece, halo_rows:],
                edge_shape,
            )

    def courant_copy(side):
        return remote(
            courant_in.at[pl.ds((planes - HALO) * side, HALO)],
            courant.at[pl.ds((planes + HALO) * (1 - side), HALO)],
            courant_send.at[side],
            courant_recv.at[side],
            side,
        )

    def stencil(ref, slot, first):
        middle = ref[slot, pl.ds(first, chunk)]
        high, low = split(middle.reshape(chunk * size_y, size_z))
        right = band_z[...]
        left = band_y[...]
        total = jnp.dot(high, right, preferred_element_type=F32)
        total += jnp.dot(low, right, preferred_element_type=F32)
        total += jnp.dot(left, high, preferred_element_type=F32)
        total += jnp.dot(left, low, preferred_element_type=F32)
        total = total.reshape(chunk, size_y, size_z)
        for offset, tap in enumerate(TAPS, 1):
            total += tap * (
                ref[slot, pl.ds(first + offset, chunk)] + ref[slot, pl.ds(first - offset, chunk)]
            )
        return total

    order = (0, chunks - 1) + inner

    odd = lax.rem(place, 2)

    def mirror(side):
        return side + odd * (1 - 2 * side)


    def first_field(turn, carry):
        index = pick(turn, order)
        part = pl.ds(HALO + chunk * index, chunk)
        scaled = courant[part] * (1.0 / SCALE)
        courant[part] = scaled
        field[0, part] = scaled * adj[1, pl.ds(chunk * index, chunk)]

        @pl.when(turn < 2)
        def _():
            adj_start(index, 0, turn)

        return carry

    loads[0].wait()
    loads[1].wait()
    low_count = jnp.where(has_low, 1, 0)
    high_count = jnp.where(has_high, 1, 0)
    pl.semaphore_wait(barrier, shots - 1 + low_count + high_count)
    lax.fori_loop(0, chunks, first_field, 0)

    def fetch_copy(level, other):
        return pltpu.make_async_remote_copy(
            src_ref=packed.at[level, pl.ds(other * cap, cap)],
            dst_ref=landed[level].at[pl.ds(me * cap, cap)],
            send_sem=fetch_send.at[level, other],
            recv_sem=fetch_recv.at[level, me],
            device_id=peer(other),
            device_id_type=MESH,
        )

    def fetch_arrival(level, other):
        return pltpu.make_async_remote_copy(
            src_ref=packed.at[level, pl.ds(other * cap, cap)],
            dst_ref=landed[level].at[pl.ds(other * cap, cap)],
            send_sem=fetch_send.at[level, other],
            recv_sem=fetch_recv.at[level, other],
            device_id=peer(other),
            device_id_type=MESH,
        )

    loads[2].wait()
    for level in (1, 0):

        def pack(turn, carry):
            other = lax.rem(me + turn, shots)
            if level == 1:
                find_sent(other)
            for rank in range(cap):
                packed[level, other * cap + rank] = store[sent_slots[other * cap + rank], level]

            @pl.when(turn < shots)
            def _():
                fetch_copy(level, other).start()

            return carry

        lax.fori_loop(1, shots + 1, pack, 0)

    def keep(rank, carry):
        for level in (1, 0):
            landed[level][me * cap + rank] = packed[level, me * cap + rank]
        return carry

    lax.fori_loop(0, cap, keep, 0)

    for side in range(2):

        @pl.when(has_side[side])
        def _():
            courant_copy(side).start()

    band_z[...] = band(size_z, size_z, CENTRE_Z)
    band_y[...] = band(chunk * size_y, size_y, CENTRE_Y)
    for side in range(2):

        @pl.when(jnp.logical_not(has_side[side]))
        def _():
            nothing = jnp.zeros((HALO, size_y, size_z), F32)
            courant[pl.ds((planes + HALO) * side, HALO)] = nothing
            for slot in range(2):
                field[slot, pl.ds((planes + HALO) * side, HALO)] = nothing
                for piece in range(2):
                    wave[slot, pl.ds((planes + deep) * side + HALO * piece, HALO)] = nothing

    lax.fori_loop(0, slabs, find_own, 0)

    plane_cells = size_y * size_z
    source = source_cell[0]
    source_plane = lax.div(source, plane_cells) - place * planes
    in_plane = lax.rem(source, plane_cells)
    flat = lax.broadcasted_iota(jnp.int32, (size_y, size_z), 0) * size_z + lax.broadcasted_iota(
        jnp.int32, (size_y, size_z), 1
    )
    spot[...] = jnp.where(flat == in_plane, 1.0, 0.0)

    recv_cells = cells[...]
    recv_row = recv_cells // size_z - place * (planes * size_y)
    recv_col = recv_cells % size_z
    count = recv_cells.shape[1]
    col_hot[...] = jnp.where(
        lax.broadcasted_iota(jnp.int32, (size_z, count), 0) == recv_col, 1.0, 0.0
    ).astype(BF16)

    loads[3].wait()

    pair = 4

    def adjoint_step(turn, carry):
        slot = lax.rem(turn, 2)
        data_high, data_low = split(residual[turn])
        data_high = data_high.astype(F32)
        data_low = data_low.astype(F32)

        def work(index):
            hot = col_hot[...]
            row = lax.broadcasted_iota(jnp.int32, (chunk * size_y, count), 0) + (
                chunk * size_y * index
            )
            hit = row == recv_row
            total = jnp.zeros((chunk * size_y, size_z), F32)
            for data in (data_high, data_low):
                total += lax.dot_general(
                    jnp.where(hit, data, 0.0).astype(BF16),
                    hot,
                    (((1,), (1,)), ((), ())),
                    preferred_element_type=F32,
                )
            total = total.reshape(chunk, size_y, size_z)
            total = total + stencil(field, slot, HALO + chunk * index)
            here = pl.ds(chunk * index, chunk)
            padded = pl.ds(HALO + chunk * index, chunk)
            current = adj[turn + 1, here]
            following = (current + current) - adj[turn, here] + total
            adj[turn + 2, here] = following
            field[1 - slot, padded] = courant[padded] * following

        def task(at, carry):
            side = mirror(at)
            adj_wait(slot, side)
            index = (chunks - 1) * side
            work(index)

            @pl.when(turn < ADJ - 1)
            def _():
                adj_start(index, 1 - slot, side)

            return carry

        lax.fori_loop(0, 2, task, 0)
        for index in inner:
            work(index)
        return carry

    def arrive(level):
        def one(turn, carry):
            fetch_arrival(level, lax.rem(me + turn, shots)).wait_recv()
            return carry

        lax.fori_loop(1, shots, one, 0)

    def unpack(slab, carry):
        wave[0, deep + slab] = landed_new[own_slots[slab]].astype(F32)
        wave[1, deep + slab] = jnp.zeros((size_y, size_z), F32)
        image[slab] = jnp.zeros((size_y, size_z), F32)
        return carry

    def first_edges(at, carry):
        wave_start(0, 0, mirror(at), 0)
        return carry

    lax.fori_loop(0, ADJ - 1, adjoint_step, 0)
    arrive(1)
    lax.fori_loop(0, slabs, unpack, 0)
    lax.fori_loop(0, 2, first_edges, 0)

    steps = window_end[0] - snap_step[0]
    start = snap_step[0]

    def image_term(level, turn, plane, width):
        behind = steps - turn
        weight = jnp.where(jnp.logical_and(behind >= 0, behind < ADJ), 1.0, 0.0)
        state = adj[1 + jnp.clip(behind, 0, ADJ - 1), pl.ds(plane, width)]
        return (weight * state) * wave[level, pl.ds(deep + plane, width)]

    def advance(level, turn, index):
        first = deep + chunk * index
        here = pl.ds(first, chunk)
        middle = wave[level, here]
        total = courant[pl.ds(first - HALO, chunk)] * stencil(wave, level, first)
        total = total + (middle + middle) - wave[1 - level, here]
        amplitude = wavelet[start + turn]
        pattern = spot[...]
        for plane in range(chunk):
            push = jnp.where(source_plane == chunk * index + plane, amplitude, 0.0)
            wave[1 - level, first + plane] = total[plane] + push * pattern

    rows = size_y // chips
    row_half = rows // 2

    def cut_image(piece, place_in, index):
        def some(part, carry):
            plane = chunk * index + pair * part
            value = image[pl.ds(plane, pair)] + image_term(0, FWD, plane, pair)
            into = pl.ds(chunk * place_in + pair * part, pair)
            for target in range(chips):
                for side in range(2):
                    low = target * rows + side * row_half
                    split_image[side, piece, target, into] = value[:, low : low + row_half]
            return carry

        lax.fori_loop(0, chunk // pair, some, 0)

    def core_copy(piece):
        return pltpu.make_async_remote_copy(
            src_ref=split_image.at[1 - core, piece],
            dst_ref=from_core.at[piece],
            send_sem=core_send.at[piece],
            recv_sem=core_recv.at[piece],
            device_id=peer(partner),
            device_id_type=MESH,
        )

    def chip_copy(piece, target, landing):
        return pltpu.make_async_remote_copy(
            src_ref=to_chip.at[piece, target],
            dst_ref=from_chip.at[piece, landing],
            send_sem=chip_send.at[piece, target],
            recv_sem=chip_recv.at[piece, landing],
            device_id=peer(target * 2 + core),
            device_id_type=MESH,
        )

    def to_chips(piece):
        core_copy(piece).wait()

        def one(turn, carry):
            target = lax.rem(chip + turn, chips)
            to_chip[piece, target] = split_image[core, piece, target] + from_core[piece, target]
            chip_copy(piece, target, chip).start()
            return carry

        lax.fori_loop(1, chips, one, 0)
        to_chip[piece, chip] = split_image[core, piece, chip] + from_core[piece, chip]

    stages = 2 + (FWD - 2) // 2

    def stage(number, carry):
        opening = number == 0
        closing = number == stages - 1
        level = jnp.where(opening, 0, 1)
        turn = jnp.where(opening, 0, 2 * number - 1)
        slot = lax.rem(number, 2)

        @pl.when(number > 0)
        def _():
            def add_terms(part, carry):
                plane = pair * part
                image[pl.ds(plane, pair)] = (
                    image[pl.ds(plane, pair)]
                    + image_term(1, turn, plane, pair)
                    + image_term(0, turn - 1, plane, pair)
                )
                return carry

            lax.fori_loop(0, planes // pair, add_terms, 0)

        for index in inner:
            advance(level, turn, index)

        @pl.when(closing)
        def _():
            def one(at, carry):
                cut_image(0, at, 1 + at)
                return carry

            lax.fori_loop(0, len(inner), one, 0)
            core_copy(0).start()

        def task(at, carry):
            index = pick(at, (0, 3, -1, 0, 1, 4, 3, 2))
            index = index + odd * (chunks - 1 - 2 * index)
            second = pick(at, (0, 0, 0, 1, 1, 0, 1, 1))
            side = mirror(pick(at, (0, 1, 0, 0, 0, 1, 1, 1)))
            piece = pick(at, (0, 0, 1, 0, 1, 1, 0, 1))
            waits = pick(at, (1, 1, 1, 0, 0, 1, 0, 0))

            @pl.when(waits == 1)
            def _():
                wave_wait(level, slot, side, piece)

            source = jnp.where(second == 1, 1 - level, level)
            advance(source, turn + second, index)

            @pl.when(
                jnp.logical_and(second == 1, jnp.logical_or(piece == 0, number < stages - 2))
            )
            def _():
                wave_start(1, 1 - slot, side, piece)

            @pl.when(closing)
            def _():
                cut_image(1, mirror(at), index)

            @pl.when(jnp.logical_and(closing, at == 0))
            def _():
                to_chips(0)

            return carry

        single = jnp.logical_or(opening, closing)
        lax.fori_loop(0, jnp.where(single, 2, 8), task, 0)

        @pl.when(opening)
        def _():
            arrive(0)

            def less(slab, carry):
                here = deep + slab
                wave[1, here] = wave[1, here] - landed_old[own_slots[slab]].astype(F32)
                return carry

            lax.fori_loop(0, slabs, less, 0)

            def edge(at, carry):
                wave_start(1, 1, mirror(lax.rem(at, 2)), lax.div(at, 2))
                return carry

            lax.fori_loop(0, 4, edge, 0)
            adjoint_step(ADJ - 1, 0)
            pltpu.make_async_copy(adj.at[ADJ + 1], adjoint_out, out_sem.at[0]).start()
            for side in range(2):

                @pl.when(has_side[side])
                def _():
                    courant_copy(side).wait_send()
                    courant_copy(1 - side).wait_recv()
                    part = pl.ds((planes + HALO) * side, HALO)
                    courant[part] = courant[part] * (1.0 / SCALE)

        return carry

    lax.fori_loop(0, stages, stage, 0)
    core_copy(1).start()
    to_chips(1)

    for piece in range(2):

        def add(turn, carry):
            other = lax.rem(chip + turn, chips)
            chip_copy(piece, other, other).wait_recv()
            chip_copy(piece, other, chip).wait_send()
            to_chip[piece, chip] = to_chip[piece, chip] + from_chip[piece, other]
            return carry

        lax.fori_loop(1, chips, add, 0)
        total = to_chip[piece, chip]
        for at, index in enumerate((inner, edges)[piece]):
            image_out[pl.ds(chunk * index, chunk)] = total[chunk * at : chunk * (at + 1)]

    def drain(turn, carry):
        other = lax.rem(me + turn, shots)
        for level in (1, 0):
            fetch_copy(level, other).wait_send()
        return carry

    lax.fori_loop(1, shots, drain, 0)
    pltpu.make_async_copy(adj.at[ADJ + 1], adjoint_out, out_sem.at[0]).wait()


def finish(image, adjoint, image_out, adjoint_out):
    size_z = image.shape[2]
    for row in range(image.shape[1]):
        image_out[:, row * size_z : (row + 1) * size_z] = image[:, row] * (1.0 / ADJ)

    def one(plane, carry):
        adjoint_out[0, plane] = adjoint[plane]
        return carry

    lax.fori_loop(0, adjoint.shape[0], one, 0)


def local(
    shots,
    spaces,
    courant,
    snapshot_store,
    slab_holder,
    snap_step,
    window_end,
    source_cell,
    wavelet,
    receiver_cells,
    residual_data,
    adjoint_prev,
    adjoint_now,
):
    planes, size_y, size_z = courant.shape
    slabs = snapshot_store.shape[0]
    cap = CAP
    chips = shots // 2
    rows = size_y // chips
    smem = pl.BlockSpec(memory_space=pltpu.SMEM)
    vmem = pl.BlockSpec(memory_space=pltpu.VMEM)
    hbm = pl.BlockSpec(memory_space=pltpu.HBM)
    half = planes // 2
    coded = (HALO * size_y + SCALE_ROWS, size_z)
    dma = pltpu.SemaphoreType.DMA
    image, adjoint = pl.pallas_call(
        functools.partial(kernel, shots, spaces, cap),
        out_shape=(
            jax.ShapeDtypeStruct((planes, rows // 2, size_z), F32),
            jax.ShapeDtypeStruct((planes, size_y, size_z), F32),
        ),
        in_specs=[smem] * 5 + [vmem] * 2 + [hbm] * 4,
        out_specs=(vmem, hbm),
        scratch_shapes=[
            pltpu.VMEM((planes + 2 * HALO, size_y, size_z), F32),
            pltpu.VMEM((slabs, 2, size_y, size_z), BF16),
            pltpu.VMEM((ADJ + 2, planes, size_y, size_z), F32),
            pltpu.VMEM((2, planes + 2 * HALO, size_y, size_z), F32),
            pltpu.VMEM((2, planes + 4 * HALO, size_y, size_z), F32),
            pltpu.VMEM((2, 2) + coded, jnp.int16),
            pltpu.VMEM((2, 2) + coded, jnp.int16),
            pltpu.VMEM((2, 2, 2) + coded, jnp.int16),
            pltpu.VMEM((2, 2, 2) + coded, jnp.int16),
            pltpu.VMEM((2, shots * cap, size_y, size_z), BF16),
            pltpu.VMEM((shots * cap, size_y, size_z), BF16),
            pltpu.VMEM((shots * cap, size_y, size_z), BF16),
            pltpu.VMEM((size_z, size_z), BF16),
            pltpu.VMEM((HALO * size_y, HALO * size_y), BF16),
            pltpu.VMEM((size_y, size_z), F32),
            pltpu.VMEM((size_z, receiver_cells.shape[1]), BF16),
            pltpu.VMEM((planes, size_y, size_z), F32),
            pltpu.VMEM((2, 2, chips, half, rows // 2, size_z), F32),
            pltpu.VMEM((2, chips, half, rows // 2, size_z), F32),
            pltpu.VMEM((2, chips, half, rows // 2, size_z), F32),
            pltpu.VMEM((2, chips, half, rows // 2, size_z), F32),
            pltpu.SMEM((shots * cap,), jnp.int32),
            pltpu.SMEM((slabs,), jnp.int32),
            dma((4,)),
            dma((2, shots)),
            dma((2, shots)),
            dma((2,)),
            dma((2,)),
            dma((2, 2)),
            dma((2, 2)),
            dma((2, 2, 2)),
            dma((2, 2, 2)),
            dma((2,)),
            dma((2,)),
            dma((2, chips)),
            dma((2, chips)),
            dma((1,)),
        ],
        compiler_params=pltpu.CompilerParams(
            collective_id=0, has_side_effects=True, vmem_limit_bytes=63 * 2**20
        ),
    )(
        slab_holder,
        snap_step,
        window_end,
        source_cell,
        wavelet,
        receiver_cells,
        residual_data.transpose(1, 0, 2),
        courant,
        snapshot_store.reshape(slabs, 2, size_y, size_z),
        adjoint_prev[0],
        adjoint_now[0],
    )
    return pl.pallas_call(
        finish,
        out_shape=(
            jax.ShapeDtypeStruct((planes, rows // 2 * size_z), F32),
            jax.ShapeDtypeStruct((1, planes, size_y, size_z), F32),
        ),
        in_specs=[vmem, vmem],
        out_specs=(vmem, vmem),
        compiler_params=pltpu.CompilerParams(vmem_limit_bytes=63 * 2**20),
    )(image, adjoint)


def solution(mesh):
    in_specs = (
        P("space", None, None),
        P("shot", None, "space", None, None),
        P(),
        P("shot"),
        P("shot"),
        P("shot"),
        P(),
        P("shot", None),
        P("shot", None, None),
        P("shot", "space", None, None),
        P("shot", "space", None, None),
    )
    out_specs = (P("space", "shot"), P("shot", "space", None, None))
    return jax.shard_map(
        functools.partial(local, mesh.shape["shot"], mesh.shape["space"]),
        mesh=mesh,
        in_specs=in_specs,
        out_specs=out_specs,
        check_vma=False,
    )
```
